32 devices in a mesh: seq: 16 (over z, y, x), head: 2 (over core).
Axes of the slice: x: 2, y: 2, z: 4, core: 2. Of those that a mesh axis runs over, the one named last changes fastest.
Arguments:
- qk: bfloat16 [2, 8192, 128], P('head', 'seq'), may hold values from -32 to 32
- values: bfloat16 [2, 8192, 128], P('head', 'seq'), may hold values from -6 to 6
- grad_out: bfloat16 [2, 8192, 128], P('head', 'seq'), may hold values from -6 to 6
- members: int32 [2, 2, 48, 256], P('head'), may hold values from 0 to 8191, as said below
- counts: int32 [2, 2, 48], P('head'), may hold values from 1 to 256, as said below
Outputs:
- d_qk: bfloat16 [2, 8192, 128], P('head', 'seq')
- d_values: bfloat16 [2, 8192, 128], P('head', 'seq')
The draws below stay inside these ranges and needn't reach their ends.
Inputs may be any that keep to these rules, and one draw needn't show every extreme that they name: `members`: for each head and round, every token index is in exactly one valid slot; the valid slots of a group are its first counts ones and hold increasing tokens, other slots hold any token. The 3 groups c with c // 3 equal hold at most 64 valid slots whose tokens t have one value of t // 512. For each head and round the counts sum to 8192.
All inputs are finite; a program needn't handle non-finite values.
Results may differ from the reference program's by a relative error of at most 0.012.
Values may be sent and summed in bfloat16 or wider, within the bound.
No kernel may reach another device: no remote copies, remote signals or barrier semaphores. Data moves between devices by JAX's collectives and lax.ppermute only.
A program may use at most 64 MiB of HBM per device.

```python
import jax
import jax.numpy as jnp
from jax import lax

DH = 128
HEADS = 2
ROUNDS = 2
CAP = 256
TOK_DEV = 512
TOKENS = 8192
CH_DEV = 3
GROUPS = 48


def draw_qk(key, part):
    shape = (HEADS, TOKENS, DH)
    streams = jax.random.split(jax.random.fold_in(key, 3), 1)
    result = 1.5 * jax.random.truncated_normal(streams[0], -4.0, 4.0, shape, jnp.float32)
    return result.astype(jnp.bfloat16)


def route_one(key):
    device_total = TOKENS // TOK_DEV
    half_mean = TOK_DEV // device_total // 2
    streams = jax.random.split(key, 6)
    spread = jax.random.randint(streams[0], (device_total,), 0, half_mean + 1).at[0].set(half_mean).at[1].set(0)
    offset = spread - jnp.roll(spread, -1)
    tilt = jax.random.randint(streams[1], (device_total,), 0, half_mean + 1).at[0].set(half_mean).at[1].set(0)
    tilt_step = tilt - jnp.roll(tilt, -1)
    owners = jnp.arange(device_total, dtype=jnp.int32)
    pair_counts = 2 * half_mean + offset[(owners[:, None] - owners[None, :]) % device_total] + tilt_step[:, None]
    bounds = jnp.cumsum(pair_counts, axis=0)
    ranking = jax.vmap(lambda stream: jax.random.permutation(stream, TOK_DEV))(jax.random.split(streams[2], device_total))
    owner_of = jnp.sum((bounds.T[:, None, :] <= ranking[:, :, None]).astype(jnp.int32), axis=2).reshape(-1)
    order_key = owner_of * TOKENS + jax.random.permutation(streams[3], TOKENS).astype(jnp.int32)
    order = jnp.argsort(order_key).astype(jnp.int32)
    load = jnp.sum(pair_counts, axis=1)
    start = jnp.cumsum(load) - load
    quotient = load // CH_DEV
    remainder = load % CH_DEV
    group_ids = jnp.arange(CH_DEV, dtype=jnp.int32)
    base = quotient[:, None] + (group_ids[None, :] < remainder[:, None]).astype(jnp.int32)
    jitter_top = jnp.maximum(jnp.minimum(jnp.minimum(CAP - quotient - 1, quotient - 1), CAP // 4), 0)
    jitter = jax.random.randint(streams[4], (device_total, CH_DEV), 0, jitter_top[:, None] + 1)
    group_counts = base + jitter - jnp.roll(jitter, -1, axis=1)
    group_start = jnp.cumsum(group_counts, axis=1) - group_counts
    slots = jnp.arange(CAP, dtype=jnp.int32)
    places = start[:, None, None] + group_start[:, :, None] + slots[None, None, :]
    valid = slots[None, None, :] < group_counts[:, :, None]
    tokens_at = order[jnp.clip(places, 0, TOKENS - 1)]
    keyed = jnp.sort(jnp.where(valid, tokens_at, TOKENS + slots[None, None, :]), axis=2)
    filler = jax.random.randint(streams[5], keyed.shape, 0, TOKENS)
    listed = jnp.where(keyed < TOKENS, keyed, filler)
    return (listed.reshape(device_total * CH_DEV, CAP).astype(jnp.int32), group_counts.reshape(-1).astype(jnp.int32))


def routing(key):
    streams = jax.random.split(jax.random.fold_in(key, 7), HEADS * ROUNDS)
    listed, group_counts = lax.map(route_one, streams)
    return (listed.reshape(HEADS, ROUNDS, GROUPS, CAP), group_counts.reshape(HEADS, ROUNDS, GROUPS))


def draw_members(key, part):
    return routing(key)[0]


def draw_counts(key, part):
    return routing(key)[1]


def levels(stream_key, dims, cuts, smallest, high):
    factor_of = 1.0
    for position, parts in cuts:
        heights = jax.random.uniform(jax.random.fold_in(jax.random.fold_in(stream_key, 6), position), (parts,), jnp.float32, smallest / len(cuts), high / len(cuts))
        factor_of = factor_of * jnp.repeat(jnp.exp(heights), dims[position] // parts).reshape((-1,) + (1,) * (len(dims) - 1 - position))
    return factor_of


def scatter_about(rng, extent, scale, limit, shards=(), held_as=jnp.bfloat16):
    values = jax.random.normal(rng, extent, jnp.float32) * scale
    if len(shards) > 0:
        values = levels(rng, extent, shards, -0.22, 0.18) * values
    return jnp.clip(values, min=-limit, max=limit).astype(held_as)


def setup_inputs(seed: int = 0) -> dict:
    streams_of = jax.random.split(jax.random.key(seed), 6)
    return {
        "qk": draw_qk(jax.random.fold_in(streams_of[5], 71), 0),
        "values": scatter_about(streams_of[1], (HEADS, TOKENS, DH), 1.0, 6.0, ((0, 2), (1, 16))),
        "grad_out": scatter_about(streams_of[2], (HEADS, TOKENS, DH), 1.0, 6.0, ((0, 2), (1, 16))),
        "members": draw_members(jax.random.fold_in(streams_of[5], 71), 0),
        "counts": draw_counts(jax.random.fold_in(streams_of[5], 71), 0),
    }


masked_score = -1e+30
norm_eps = 1e-06

def group_forward(queries, key_rows, value_rows, allowed):
    key_float = key_rows.astype(jnp.float32)
    inverse = lax.rsqrt(lax.optimization_barrier(jnp.sum(key_float * key_float, axis=-1, keepdims=True)) + norm_eps)
    unit_keys = (key_float * inverse).astype(jnp.bfloat16)
    scores = jnp.dot(queries, unit_keys.T, preferred_element_type=jnp.float32)
    scores = jnp.where(allowed, scores, masked_score)
    highest = lax.optimization_barrier(jnp.max(scores, axis=-1, keepdims=True))
    log_total = highest + jnp.log(lax.optimization_barrier(jnp.sum(jnp.exp(scores - highest), axis=-1, keepdims=True)))
    probability = jnp.exp(scores - log_total)
    rounded = probability.astype(jnp.bfloat16)
    outputs = jnp.dot(rounded, value_rows, preferred_element_type=jnp.float32)
    return (unit_keys, inverse, probability, rounded, log_total[:, 0], outputs)

def group_backward(queries, key_rows, value_rows, unit_keys, inverse, probability, rounded, out_grad, log_grad):
    d_prob = jnp.dot(out_grad, value_rows.T, preferred_element_type=jnp.float32)
    center = lax.optimization_barrier(jnp.sum(probability * d_prob, axis=-1, keepdims=True))
    d_score = (probability * (d_prob - center + log_grad[:, None])).astype(jnp.bfloat16)
    d_query = jnp.dot(d_score, unit_keys, preferred_element_type=jnp.float32)
    d_unit = jnp.dot(d_score.T, queries, preferred_element_type=jnp.float32)
    key_float = key_rows.astype(jnp.float32)
    cubed = inverse * inverse * inverse
    d_key = inverse * d_unit - key_float * cubed * lax.optimization_barrier(jnp.sum(key_float * d_unit, axis=-1, keepdims=True))
    d_value = jnp.dot(rounded.T, out_grad, preferred_element_type=jnp.float32)
    return (d_query, d_key, d_value)

def head_reference(qk_rows, value_rows, cot_rows, members, counts):
    token_count, feature_size = qk_rows.shape
    rounds, groups, group_size = members.shape
    positions = jnp.arange(group_size, dtype=jnp.int32)
    filled = positions[None, None, :] < counts[:, :, None]
    indices = jnp.where(filled, members, token_count).astype(jnp.int32)

    def padded(rows):
        return jnp.concatenate([rows, jnp.zeros((1, feature_size), rows.dtype)], axis=0)[indices]
    q_slots = padded(qk_rows)
    v_slots = padded(value_rows)
    g_slots = padded(cot_rows)
    q_prev = jnp.roll(q_slots, 1, axis=1)
    v_prev = jnp.roll(v_slots, 1, axis=1)
    fill_prev = jnp.roll(filled, 1, axis=1)
    not_self = jnp.arange(2 * group_size, dtype=jnp.int32)[None, :] != positions[:, None] + group_size

    def flatten(array):
        return array.reshape((rounds * groups,) + array.shape[2:])
    items = (flatten(q_slots), flatten(q_prev), flatten(v_slots), flatten(v_prev), flatten(filled), flatten(fill_prev), flatten(g_slots))

    def prepare(entry):
        queries, prev_q, values_now, prev_v, fill_now, fill_before, cot_now = entry
        key_rows = jnp.concatenate([prev_q, queries], axis=0)
        value_keys = jnp.concatenate([prev_v, values_now], axis=0)
        allowed = jnp.concatenate([fill_before, fill_now], axis=0)[None, :] & not_self
        return (queries, key_rows, value_keys, allowed, cot_now)

    def forward_item(entry):
        queries, key_rows, value_keys, allowed, cot_now = prepare(entry)
        result = group_forward(queries, key_rows, value_keys, allowed)
        dots = lax.optimization_barrier(jnp.sum(cot_now.astype(jnp.float32) * result[5], axis=-1))
        return (result[4], dots)
    log_slots, dot_slots = lax.map(forward_item, items)
    log_slots = log_slots.reshape(rounds, groups, group_size)
    dot_slots = dot_slots.reshape(rounds, groups, group_size)
    round_grid = jnp.broadcast_to(jnp.arange(rounds, dtype=jnp.int32)[:, None, None], indices.shape)

    def to_tokens(slot_values):
        return jnp.zeros((rounds, token_count + 1), jnp.float32).at[round_grid, indices].set(slot_values)[:, :token_count]
    log_tok = to_tokens(log_slots)
    dot_tok = to_tokens(dot_slots)
    highest = lax.optimization_barrier(jnp.max(log_tok, axis=0))
    exponent = jnp.exp(log_tok - highest)
    weight = exponent / lax.optimization_barrier(jnp.sum(exponent, axis=0))
    mixture = lax.optimization_barrier(jnp.sum(weight * dot_tok, axis=0))
    log_grad = weight * (dot_tok - mixture)

    def to_slots(token_values):
        padded_values = jnp.concatenate([token_values, jnp.zeros((rounds, 1), jnp.float32)], axis=1)
        return padded_values[round_grid, indices]
    weight_slots = flatten(to_slots(weight))
    grad_slots = flatten(to_slots(log_grad))

    def backward_item(entry):
        base, weight_now, log_now = entry
        queries, key_rows, value_keys, allowed, cot_now = prepare(base)
        unit_keys, inverse, probability, rounded, log_total, outputs = group_forward(queries, key_rows, value_keys, allowed)
        out_grad = (weight_now[:, None] * cot_now.astype(jnp.float32)).astype(jnp.bfloat16)
        return group_backward(queries, key_rows, value_keys, unit_keys, inverse, probability, rounded, out_grad, log_now)
    d_query, d_key, d_value = lax.map(backward_item, (items, weight_slots, grad_slots))
    d_query = d_query.reshape(rounds, groups, group_size, feature_size)
    d_key = d_key.reshape(rounds, groups, 2 * group_size, feature_size)
    d_value = d_value.reshape(rounds, groups, 2 * group_size, feature_size)
    own_q = d_query + d_key[:, :, group_size:] + jnp.roll(d_key[:, :, :group_size], -1, axis=1)
    own_v = d_value[:, :, group_size:] + jnp.roll(d_value[:, :, :group_size], -1, axis=1)
    flat_index = indices.reshape(-1)
    grad_qk = jnp.zeros((token_count + 1, feature_size), jnp.float32).at[flat_index].add(own_q.reshape(-1, feature_size))
    grad_v = jnp.zeros((token_count + 1, feature_size), jnp.float32).at[flat_index].add(own_v.reshape(-1, feature_size))
    return (grad_qk[:token_count].astype(jnp.bfloat16), grad_v[:token_count].astype(jnp.bfloat16))

def head_item(entry):
    return head_reference(entry[0], entry[1], entry[2], entry[3], entry[4])

def reference(qk, values, grad_out, members, counts):
    d_qk, d_values = lax.map(head_item, (qk, values, grad_out, members, counts))
    return (d_qk, d_values)
```

```python
import functools

import jax
import jax.numpy as jnp
from jax import lax
from jax.experimental import pallas as pl
from jax.experimental.pallas import tpu as pltpu
from jax.sharding import PartitionSpec as P

masked_score = -1e30
norm_eps = 1e-06
lane = 128
f32 = jnp.float32
bf16 = jnp.bfloat16


def iota(shape, axis):
    return lax.broadcasted_iota(jnp.int32, shape, axis)


def float_iota(shape, axis):
    return iota(shape, axis).astype(f32)


def dot_nn(a, b):
    return lax.dot_general(a, b, (((1,), (0,)), ((), ())), preferred_element_type=f32)


def dot_nt(a, b):
    return lax.dot_general(a, b, (((1,), (1,)), ((), ())), preferred_element_type=f32)


def dot_tn(a, b):
    return lax.dot_general(a, b, (((0,), (0,)), ((), ())), preferred_element_type=f32)


def one_hot(condition):
    return jnp.where(condition, 1.0, 0.0).astype(bf16)


def earlier(size):
    return one_hot(iota((size, size), 0) < iota((size, size), 1))


def call(kernel, out_shapes, in_specs, scratch=()):
    return pl.pallas_call(
        kernel,
        out_shape=tuple(jax.ShapeDtypeStruct(shape, dtype) for shape, dtype in out_shapes),
        in_specs=in_specs,
        out_specs=tuple(pl.BlockSpec(memory_space=pltpu.VMEM) for _ in out_shapes),
        scratch_shapes=list(scratch),
        compiler_params=pltpu.CompilerParams(vmem_limit_bytes=50 * 1024 * 1024),
    )


def vmem(count):
    return [pl.BlockSpec(memory_space=pltpu.VMEM) for _ in range(count)]


def smem():
    return pl.BlockSpec(memory_space=pltpu.SMEM)


def pack_kernel(
    rounds, devices, bound, tokens_ref, q_ref, v_ref, g_ref, send_ref, pick_ref, key_ref, value_ref
):
    per_device, _, cap = tokens_ref.shape
    token_count = q_ref.shape[0]
    start = lax.axis_index("seq") * token_count
    before = earlier(cap)
    carry = jnp.zeros((rounds * devices, 1), f32)
    for group in range(per_device):
        local = tokens_ref[group] - start
        owned = (local >= 0) & (local < token_count)
        rank = dot_nn(one_hot(owned), before) + carry
        carry = carry + jnp.sum(jnp.where(owned, 1.0, 0.0), axis=1, keepdims=True)
        key_ref[group] = jnp.where(owned, rank, -1.0)
        value_ref[group] = jnp.where(owned, local + 1, 0).astype(f32)
    column = float_iota((bound, cap), 0)
    token = float_iota((bound, token_count), 1)

    def one_device(device, carried):
        for r in range(rounds):
            row = r * devices + device
            total = jnp.zeros((bound, cap), f32)
            for group in range(per_device):
                ranks = key_ref[group, pl.ds(row, 1), :]
                values = value_ref[group, pl.ds(row, 1), :]
                total = total + jnp.where(ranks == column, values, 0.0)
            index = jnp.sum(total, axis=1, keepdims=True) - 1.0
            at = pl.multiple_of((device * rounds + r) * bound, bound)
            pick_ref[pl.ds(at, bound), :] = one_hot(index == token)
        return carried

    lax.fori_loop(0, devices, one_device, 0, unroll=2)
    rows = jnp.concatenate([q_ref[...], v_ref[...], g_ref[...]], axis=1)
    total_rows = send_ref.shape[0]
    step = total_rows // 4
    for part in range(4):
        span = pl.ds(part * step, step)
        send_ref[span, :] = dot_nn(pick_ref[span, :], rows).astype(bf16)


def index_kernel(
    rounds,
    devices,
    bound,
    token_count,
    tokens_ref,
    spread_ref,
    spread_t_ref,
    partner_ref,
    low_ref,
    table_ref,
):
    per_device, _, cap = tokens_ref.shape
    me = lax.axis_index("seq")
    buffer_rows = devices * bound
    before = earlier(cap)
    source_start = iota((devices, cap), 0) * token_count
    source_place = float_iota((devices, cap), 0) * bound + 1.0
    place_column = float_iota((buffer_rows, cap), 0)
    place_lane = float_iota((cap, buffer_rows), 1)
    for r in range(rounds):
        carry = jnp.zeros((devices, 1), f32)
        for group in range(per_device):
            tokens = tokens_ref[group, pl.ds(r * devices + me, 1), :]
            owned = (tokens >= source_start) & (tokens < source_start + token_count)
            rank = dot_nn(one_hot(owned), before) + carry
            carry = carry + jnp.sum(jnp.where(owned, 1.0, 0.0), axis=1, keepdims=True)
            place = (
                jnp.sum(jnp.where(owned, rank + source_place, 0.0), axis=0, keepdims=True) - 1.0
            )
            span = pl.ds(group * cap, cap)
            spread_t_ref[r, :, span] = one_hot(place == place_column)
            upright = jnp.transpose(jnp.broadcast_to(place, (8, cap)))[:, :1]
            spread_ref[r, span, :] = one_hot(upright == place_lane)

    high_count = devices * token_count // lane
    high_start = iota((high_count, cap), 0) * lane
    low_index = iota((lane, cap), 0)
    slot = float_iota((high_count, cap), 1)

    def split(tokens):
        high = (tokens >= high_start) & (tokens < high_start + lane)
        low = jnp.bitwise_and(tokens, lane - 1) == low_index
        return high, low

    for r in range(rounds):

        def one_device(device, total):
            for group in range(per_device):
                tokens = tokens_ref[group, pl.ds(r * devices + device, 1), :]
                high, low = split(tokens)
                group_index = (device * per_device + group).astype(f32)
                sides = jnp.concatenate(
                    [
                        jnp.where(high, group_index, 0.0).astype(bf16),
                        jnp.where(high, slot, 0.0).astype(bf16),
                    ],
                    axis=0,
                )
                total = total + dot_nt(sides, one_hot(low))
            return total

        total = lax.fori_loop(
            0, devices, one_device, jnp.zeros((2 * high_count, lane), f32), unroll=2
        )
        table_ref[r] = total.astype(bf16)

    rows_per_device = 2 * rounds * per_device * cap // lane
    halves = cap // lane
    row_column = float_iota((devices * rows_per_device, cap), 0)
    for r in range(rounds):
        other = 1 - r
        for group in range(per_device):
            tokens = tokens_ref[group, pl.ds(r * devices + me, 1), :]
            high, low = split(tokens)
            high_hot = one_hot(high)
            found = []
            for part in range(2):
                table = table_ref[other, part * high_count : (part + 1) * high_count, :]
                picked = dot_tn(table, high_hot)
                found.append(jnp.sum(jnp.where(low, picked, 0.0), axis=0, keepdims=True))
            group_index, position = found
            device = jnp.floor((group_index + 0.5) * (1.0 / per_device))
            half = jnp.floor((position + 0.5) * (1.0 / lane))
            row = (
                device * rows_per_device
                + other * per_device * halves
                + (group_index - device * per_device) * halves
                + half
            )
            span = pl.ds(group * cap, cap)
            partner_ref[r, :, span] = one_hot(row == row_column)
            low_ref[pl.ds(r * per_device + group, 1), :] = position - half * lane


def last_kernel(rounds, devices, bound, got_ref, spread_ref, out_ref):
    features = out_ref.shape[2]
    for r in range(rounds):
        rows = got_ref[:, r * bound : (r + 1) * bound, :features].reshape(devices * bound, features)
        out_ref[r] = dot_nn(spread_ref[r], rows).astype(bf16)


def inverse_norm(rows):
    wide = rows.astype(f32)
    return lax.rsqrt(jnp.sum(wide * wide, axis=1, keepdims=True) + norm_eps)


def unit_rows(rows):
    return (rows.astype(f32) * inverse_norm(rows)).astype(bf16)


def forward(unit_before, unit_now, queries, value_before, value_now, cot, fill_before, fill_now):
    cap = queries.shape[0]
    key = iota((cap, cap), 0)
    score_before = jnp.where(key < fill_before, dot_nt(unit_before, queries), masked_score)
    allowed = (key < fill_now) & (key != iota((cap, cap), 1))
    score_now = jnp.where(allowed, dot_nt(unit_now, queries), masked_score)
    highest = jnp.maximum(
        jnp.max(score_before, axis=0, keepdims=True), jnp.max(score_now, axis=0, keepdims=True)
    )
    exp_before = jnp.exp(score_before - highest)
    exp_now = jnp.exp(score_now - highest)
    total = jnp.sum(exp_before, axis=0, keepdims=True) + jnp.sum(exp_now, axis=0, keepdims=True)
    inverse = 1.0 / total
    prob_before = exp_before * inverse
    prob_now = exp_now * inverse
    inner_before = dot_nt(value_before, cot)
    inner_now = dot_nt(value_now, cot)
    dots = jnp.sum(prob_before * inner_before, axis=0, keepdims=True) + jnp.sum(
        prob_now * inner_now, axis=0, keepdims=True
    )
    probs = (prob_before.astype(bf16), prob_now.astype(bf16))
    inners = (inner_before.astype(bf16), inner_now.astype(bf16))
    return highest + jnp.log(total), dots, probs, inners


def forward_inner_kernel(
    rounds, devices, bound, counts_ref, got_ref, spread_ref, rows_ref, prob_ref, inner_ref, sums_ref
):
    cap = prob_ref.shape[3]
    per_device = spread_ref.shape[1] // cap
    size = rows_ref.shape[3] // 3
    first = lax.axis_index("seq") * per_device
    for r in range(rounds):
        received = got_ref[:, r * bound : (r + 1) * bound, :].reshape(devices * bound, 3 * size)
        unpacked = dot_nn(spread_ref[r], received).astype(bf16)
        units = []
        for group in range(per_device):
            rows = unpacked[group * cap : (group + 1) * cap]
            rows_ref[r, group] = rows
            units.append(unit_rows(rows[:, :size]))
        for group in range(1, per_device):
            rows = unpacked[group * cap : (group + 1) * cap]
            behind = unpacked[(group - 1) * cap : group * cap]
            log_total, dots, probs, inners = forward(
                units[group - 1],
                units[group],
                rows[:, :size],
                behind[:, size : 2 * size],
                rows[:, size : 2 * size],
                rows[:, 2 * size :],
                counts_ref[r, first + group - 1],
                counts_ref[r, first + group],
            )
            for side in range(2):
                prob_ref[r, group - 1, side * cap : (side + 1) * cap, :] = probs[side]
                inner_ref[r, group - 1, side * cap : (side + 1) * cap, :] = inners[side]
            sums_ref[pl.ds(r * per_device + group, 1), :] = log_total
            sums_ref[pl.ds((rounds + r) * per_device + group, 1), :] = dots


def forward_first_kernel(
    rounds,
    devices,
    counts_ref,
    rows_ref,
    behind_ref,
    inner_sums_ref,
    prob_ref,
    inner_ref,
    sums_ref,
    send_ref,
):
    cap = prob_ref.shape[2]
    per_device = rows_ref.shape[1]
    size = rows_ref.shape[3] // 3
    groups = counts_ref.shape[1]
    first = lax.axis_index("seq") * per_device
    before = lax.rem(first + groups - 1, groups)
    sums_ref[...] = inner_sums_ref[...]
    for r in range(rounds):
        rows = rows_ref[r, 0]
        behind = behind_ref[r]
        log_total, dots, probs, inners = forward(
            unit_rows(behind[:, :size]),
            unit_rows(rows[:, :size]),
            rows[:, :size],
            behind[:, size:],
            rows[:, size : 2 * size],
            rows[:, 2 * size :],
            counts_ref[r, before],
            counts_ref[r, first],
        )
        for side in range(2):
            prob_ref[r, side * cap : (side + 1) * cap, :] = probs[side]
            inner_ref[r, side * cap : (side + 1) * cap, :] = inners[side]
        sums_ref[pl.ds(r * per_device, 1), :] = log_total
        sums_ref[pl.ds((rounds + r) * per_device, 1), :] = dots
    halves = cap // lane
    for row in range(2 * rounds * per_device):
        for half in range(halves):
            part = sums_ref[row : row + 1, half * lane : (half + 1) * lane]
            send_ref[:, row * halves + half : row * halves + half + 1, :] = jnp.broadcast_to(
                part[None], (devices, 1, lane)
            )


def backward(unit_before, unit_now, queries, cot, probs, inners, weight, mixture):
    cap = queries.shape[0]
    units = (unit_before, unit_now)
    query_grad = jnp.zeros((cap, queries.shape[1]), f32)
    unit_grads = []
    value_grads = []
    for side in range(2):
        weighted = probs[side].astype(f32) * weight
        score_grad = (weighted * (inners[side].astype(f32) - mixture)).astype(bf16)
        unit_grads.append(dot_nn(score_grad, queries))
        value_grads.append(dot_nn(weighted.astype(bf16), cot))
        query_grad = query_grad + dot_tn(score_grad, units[side])
    return query_grad, unit_grads, value_grads


def key_grad(rows, unit_grad):
    wide = rows.astype(f32)
    inverse = inverse_norm(rows)
    along = jnp.sum(wide * unit_grad, axis=1, keepdims=True)
    return inverse * unit_grad - wide * (inverse * inverse * inverse * along)


def three_parts(values):
    high = values.astype(bf16)
    rest = values - high.astype(f32)
    middle = rest.astype(bf16)
    return high, middle, (rest - middle.astype(f32)).astype(bf16)


def backward_first_kernel(
    rounds,
    counts_ref,
    everyone_ref,
    partner_ref,
    low_ref,
    sums_ref,
    rows_ref,
    behind_ref,
    prob_ref,
    inner_ref,
    edge_ref,
    query_ref,
    part_ref,
    scale_ref,
):
    cap = prob_ref.shape[2]
    per_device = rows_ref.shape[1]
    size = rows_ref.shape[3] // 3
    first = lax.axis_index("seq") * per_device
    table_rows = everyone_ref.shape[0]
    apart = rounds * per_device * cap // lane
    table = everyone_ref[...]
    both = jnp.concatenate([table, pltpu.roll(table, table_rows - apart, 0)], axis=1)
    upright = jnp.concatenate(three_parts(jnp.transpose(both)), axis=0)
    low_column = float_iota((lane, cap), 0)
    slot = iota((1, cap), 1)
    for r in range(rounds):
        picked = dot_nn(upright, partner_ref[r])
        picked = picked[: 2 * lane] + (picked[2 * lane : 4 * lane] + picked[4 * lane :])
        for group in range(per_device):
            at = r * per_device + group
            here = low_ref[at : at + 1, :] == low_column
            span = slice(group * cap, (group + 1) * cap)
            other_log = jnp.sum(jnp.where(here, picked[:lane, span], 0.0), axis=0, keepdims=True)
            other_dot = jnp.sum(jnp.where(here, picked[lane:, span], 0.0), axis=0, keepdims=True)
            own_log = sums_ref[at : at + 1, :]
            own_dot = sums_ref[rounds * per_device + at : rounds * per_device + at + 1, :]
            weight = 1.0 / (1.0 + jnp.exp(other_log - own_log))
            other_weight = 1.0 / (1.0 + jnp.exp(own_log - other_log))
            mixture = weight * own_dot + other_weight * other_dot
            valid = slot < counts_ref[r, first + group]
            scale_ref[at : at + 1, :] = jnp.where(valid, weight, 0.0)
            scale_ref[rounds * per_device + at : rounds * per_device + at + 1, :] = jnp.where(
                valid, mixture, 0.0
            )
    for r in range(rounds):
        rows = rows_ref[r, 0]
        at = r * per_device
        query_grad, unit_grads, value_grads = backward(
            unit_rows(behind_ref[r][:, :size]),
            unit_rows(rows[:, :size]),
            rows[:, :size],
            rows[:, 2 * size :],
            (prob_ref[r, :cap, :], prob_ref[r, cap:, :]),
            (inner_ref[r, :cap, :], inner_ref[r, cap:, :]),
            scale_ref[at : at + 1, :],
            scale_ref[rounds * per_device + at : rounds * per_device + at + 1, :],
        )
        edge_ref[r] = jnp.concatenate([unit_grads[0], value_grads[0]], axis=1).astype(bf16)
        query_ref[r] = query_grad
        part_ref[r] = jnp.concatenate([unit_grads[1], value_grads[1]], axis=1)


def backward_inner_kernel(
    rounds,
    rows_ref,
    prob_ref,
    inner_ref,
    scale_ref,
    query_ref,
    part_ref,
    done_ref,
    last_query_ref,
    last_part_ref,
):
    cap = prob_ref.shape[3]
    per_device = rows_ref.shape[1]
    size = rows_ref.shape[3] // 3
    for r in range(rounds):
        query_grad = query_ref[r]
        part = part_ref[r]
        for group in range(1, per_device):
            rows = rows_ref[r, group]
            behind = rows_ref[r, group - 1][:, :size]
            at = r * per_device + group
            next_query, unit_grads, value_grads = backward(
                unit_rows(behind),
                unit_rows(rows[:, :size]),
                rows[:, :size],
                rows[:, 2 * size :],
                (prob_ref[r, group - 1, :cap, :], prob_ref[r, group - 1, cap:, :]),
                (inner_ref[r, group - 1, :cap, :], inner_ref[r, group - 1, cap:, :]),
                scale_ref[at : at + 1, :],
                scale_ref[rounds * per_device + at : rounds * per_device + at + 1, :],
            )
            done = jnp.concatenate(
                [
                    query_grad + key_grad(behind, part[:, :size] + unit_grads[0]),
                    part[:, size:] + value_grads[0],
                ],
                axis=1,
            )
            done_ref[r, (group - 1) * cap : group * cap, :] = done.astype(bf16)
            query_grad = next_query
            part = jnp.concatenate([unit_grads[1], value_grads[1]], axis=1)
        last_query_ref[r] = query_grad
        last_part_ref[r] = part


def return_kernel(
    rounds,
    devices,
    bound,
    rows_ref,
    done_ref,
    query_ref,
    part_ref,
    edge_ref,
    spread_t_ref,
    send_ref,
):
    size = query_ref.shape[2]
    for r in range(rounds):
        total = part_ref[r] + edge_ref[r].astype(f32)
        last = jnp.concatenate(
            [query_ref[r] + key_grad(rows_ref[r, rows_ref.shape[1] - 1][:, :size], total[:, :size]), total[:, size:]],
            axis=1,
        ).astype(bf16)
        grads = jnp.concatenate([done_ref[r], last], axis=0)
        packed = dot_nn(spread_t_ref[r], grads).astype(bf16)
        send_ref[:, r * bound : (r + 1) * bound, :] = packed.reshape(devices, bound, 2 * size)


def home_kernel(pick_ref, got_ref, qk_ref, value_ref):
    size = qk_ref.shape[1]
    total = dot_tn(pick_ref[...], got_ref[...])
    qk_ref[...] = total[:, :size].astype(bf16)
    value_ref[...] = total[:, size:].astype(bf16)


def exchange(array):
    return lax.all_to_all(array, "seq", split_axis=0, concat_axis=0, tiled=True)


def shifted(array, by):
    devices = lax.axis_size("seq")
    return lax.ppermute(array, "seq", [(i, (i + by) % devices) for i in range(devices)])


def head_backward(qk, values, cot, members, counts):
    devices = lax.axis_size("seq")
    token_count, size = qk.shape
    rounds, groups, cap = members.shape
    per_device = groups // devices
    slots = per_device * cap
    bound = 2 * token_count // devices
    span = rounds * bound
    sum_rows = 2 * rounds * per_device
    table_rows = devices * sum_rows * cap // lane
    filled = jnp.arange(cap, dtype=jnp.int32) < counts[..., None]
    tokens = jnp.transpose(
        jnp.where(filled, members, -1).reshape(rounds * devices, per_device, cap), (1, 0, 2)
    )
    send, pick = call(
        functools.partial(pack_kernel, rounds, devices, bound),
        [((devices * span, 3 * size), bf16), ((devices * span, token_count), bf16)],
        vmem(4),
        [pltpu.VMEM((per_device, rounds * devices, cap), f32)] * 2,
    )(tokens, qk, values, cot)
    got = exchange(send).reshape(devices, span, 3 * size)
    spread, spread_t, partner, low = call(
        functools.partial(index_kernel, rounds, devices, bound, token_count),
        [
            ((rounds, slots, devices * bound), bf16),
            ((rounds, devices * bound, slots), bf16),
            ((rounds, table_rows, slots), bf16),
            ((rounds * per_device, cap), f32),
        ],
        vmem(1),
        [pltpu.VMEM((rounds, 2 * devices * token_count // lane, lane), bf16)],
    )(tokens)
    (last,) = call(
        functools.partial(last_kernel, rounds, devices, bound),
        [((rounds, cap, 2 * size), bf16)],
        vmem(2),
    )(got, spread[:, slots - cap :])
    behind = shifted(last, 1)
    rows, prob, inner, inner_sums = call(
        functools.partial(forward_inner_kernel, rounds, devices, bound),
        [
            ((rounds, per_device, cap, 3 * size), bf16),
            ((rounds, per_device - 1, 2 * cap, cap), bf16),
            ((rounds, per_device - 1, 2 * cap, cap), bf16),
            ((sum_rows, cap), f32),
        ],
        [smem()] + vmem(2),
    )(counts, got, spread)
    first_prob, first_inner, sums, sums_send = call(
        functools.partial(forward_first_kernel, rounds, devices),
        [
            ((rounds, 2 * cap, cap), bf16),
            ((rounds, 2 * cap, cap), bf16),
            ((sum_rows, cap), f32),
            ((devices, sum_rows * cap // lane, lane), f32),
        ],
        [smem()] + vmem(3),
    )(counts, rows, behind, inner_sums)
    everyone = exchange(sums_send.reshape(table_rows, lane))
    edge, query, part, scale = call(
        functools.partial(backward_first_kernel, rounds),
        [
            ((rounds, cap, 2 * size), bf16),
            ((rounds, cap, size), f32),
            ((rounds, cap, 2 * size), f32),
            ((sum_rows, cap), f32),
        ],
        [smem()] + vmem(8),
    )(counts, everyone, partner, low, sums, rows, behind, first_prob, first_inner)
    edge_in = shifted(edge, -1)
    done, last_query, last_part = call(
        functools.partial(backward_inner_kernel, rounds),
        [
            ((rounds, slots - cap, 2 * size), bf16),
            ((rounds, cap, size), f32),
            ((rounds, cap, 2 * size), f32),
        ],
        vmem(6),
    )(rows, prob, inner, scale, query, part)
    (grads_send,) = call(
        functools.partial(return_kernel, rounds, devices, bound),
        [((devices, span, 2 * size), bf16)],
        vmem(6),
    )(rows, done, last_query, last_part, edge_in, spread_t)
    home = exchange(grads_send.reshape(devices * span, 2 * size))
    return call(
        home_kernel, [((token_count, size), bf16), ((token_count, size), bf16)], vmem(2)
    )(pick, home)


def on_device(qk, values, grad_out, members, counts):
    grad_qk, grad_v = head_backward(qk[0], values[0], grad_out[0], members[0], counts[0])
    return (grad_qk[None], grad_v[None])


def solution(mesh):
    in_specs = (
        P("head", "seq", None),
        P("head", "seq", None),
        P("head", "seq", None),
        P("head", None, None, None),
        P("head", None, None),
    )
    out_specs = (P("head", "seq", None), P("head", "seq", None))
    return jax.shard_map(
        on_device, mesh=mesh, in_specs=in_specs, out_specs=out_specs, check_vma=False
    )
```

```python
import functools
import math

import jax
import jax.numpy as jnp
from jax import lax
from jax.experimental import pallas as pl
from jax.experimental.pallas import tpu as pltpu
from jax.sharding import PartitionSpec as P

masked_score = -1e30
norm_eps = 1e-06
lane = 128
f32 = jnp.float32
bf16 = jnp.bfloat16


def iota(shape, axis):
    return lax.broadcasted_iota(jnp.int32, shape, axis)


def float_iota(shape, axis):
    return iota(shape, axis).astype(f32)


def dot_nn(a, b):
    return lax.dot_general(a, b, (((1,), (0,)), ((), ())), preferred_element_type=f32)


def dot_nt(a, b):
    return lax.dot_general(a, b, (((1,), (1,)), ((), ())), preferred_element_type=f32)


def dot_tn(a, b):
    return lax.dot_general(a, b, (((0,), (0,)), ((), ())), preferred_element_type=f32)


def one_hot(condition):
    return jnp.where(condition, 1.0, 0.0).astype(bf16)


def block_of(device, devices):
    if devices % 4:
        return device
    depth = devices // 4
    level, column = device // 4, device % 4
    turn = column ^ (column >> 1)
    step = level + (turn % 2) * (depth - 1 - 2 * level)
    return turn * depth + step


def device_of(block, devices):
    if devices % 4:
        return block
    depth = devices // 4
    turn, step = block // depth, block % depth
    level = step + (turn % 2) * (depth - 1 - 2 * step)
    return level * 4 + (turn ^ (turn >> 1))


def earlier(size):
    return one_hot(iota((size, size), 0) < iota((size, size), 1))


def call(kernel, out_shapes, operands, scratch=(), scalars=0, remote=0, semaphores=0, far=(), direct=()):
    count = len(operands)
    held = sum(array.size * array.dtype.itemsize for array in operands[scalars : count - remote])
    for shape, dtype in list(out_shapes) + list(scratch):
        held += math.prod(shape) * jnp.dtype(dtype).itemsize
    spaces = (
        [pltpu.SMEM] * scalars + [pltpu.VMEM] * (count - scalars - remote) + [pltpu.HBM] * remote
    )
    operands = [
        pltpu.with_memory_space_constraint(array, space) if space is pltpu.HBM else array
        for array, space in zip(operands, spaces)
    ]
    return pl.pallas_call(
        kernel,
        out_shape=tuple(
            pltpu.HBM(shape, dtype) if at in far else jax.ShapeDtypeStruct(shape, dtype)
            for at, (shape, dtype) in enumerate(out_shapes)
        ),
        in_specs=[pl.BlockSpec(memory_space=space) for space in spaces],
        out_specs=tuple(
            pl.BlockSpec(memory_space=pltpu.HBM if at in direct else pltpu.VMEM)
            for at in range(len(out_shapes))
        ),
        scratch_shapes=[pltpu.VMEM(shape, dtype) for shape, dtype in scratch]
        + [pltpu.SemaphoreType.DMA((semaphores,))] * min(semaphores, 1),
        compiler_params=pltpu.CompilerParams(vmem_limit_bytes=held + 12 * 1024 * 1024),
    )(*operands)


def slot_tokens(members_ref, counts_ref, devices, group):
    rounds, groups = counts_ref.shape
    per_device = groups // devices
    rows = pl.ds(group, rounds * devices, stride=per_device)
    parts = [members_ref[half, rows, :] for half in range(members_ref.shape[0])]
    listed = jnp.concatenate(parts, axis=1)
    diagonal = iota((devices, groups), 1) == iota((devices, groups), 0) * per_device + group
    limits = [
        jnp.sum(
            jnp.where(diagonal, counts_ref[r : r + 1, :].astype(f32), 0.0), axis=1, keepdims=True
        )
        for r in range(rounds)
    ]
    limit = jnp.concatenate(limits, axis=0)
    return jnp.where(float_iota(listed.shape, 1) < limit, listed, -1)


def rank_slots(rounds, devices, token_count, tokens_ref, key_ref, value_ref):
    per_device, _, cap = key_ref.shape
    start = lax.axis_index("seq") * token_count
    before = earlier(cap)
    carry = jnp.zeros((rounds * devices, 1), f32)
    for group in range(per_device):
        local = tokens_ref[group] - start
        owned = (local >= 0) & (local < token_count)
        rank = dot_nn(one_hot(owned), before) + carry
        carry = carry + jnp.sum(jnp.where(owned, 1.0, 0.0), axis=1, keepdims=True)
        key_ref[group] = jnp.where(owned, rank, -1.0)
        value_ref[group] = jnp.where(owned, local + 1, 0).astype(f32)


def pick_rows(rounds, devices, bound, block, token_count, key_ref, value_ref):
    per_device, _, cap = key_ref.shape
    column = float_iota((bound, cap), 0)
    token = float_iota((bound, token_count), 1)
    picks = []
    for r in range(rounds):
        row = r * devices + block
        total = jnp.zeros((bound, cap), f32)
        for group in range(per_device):
            ranks = key_ref[group, pl.ds(row, 1), :]
            values = value_ref[group, pl.ds(row, 1), :]
            total = total + jnp.where(ranks == column, values, 0.0)
        index = jnp.sum(total, axis=1, keepdims=True) - 1.0
        picks.append(one_hot(index == token))
    return jnp.concatenate(picks, axis=0)


def pack_kernel(
    rounds,
    devices,
    bound,
    counts_hbm,
    members_hbm,
    q_hbm,
    v_hbm,
    g_hbm,
    send_hbm,
    tokens_ref,
    packed_ref,
    key_ref,
    value_ref,
    counts_ref,
    members_ref,
    rows_ref,
    sems,
):
    token_count, size = q_hbm.shape
    halves = members_ref.shape[0]
    copies = [pltpu.make_async_copy(counts_hbm, counts_ref, sems.at[halves + 3])]
    for half in range(halves):
        source = members_hbm.at[:, pl.ds(half * lane, lane)]
        copies.append(pltpu.make_async_copy(source, members_ref.at[half], sems.at[half]))
    for at, source in enumerate((q_hbm, v_hbm, g_hbm)):
        target = rows_ref.at[:, pl.ds(at * size, size)]
        copies.append(pltpu.make_async_copy(source, target, sems.at[halves + at]))
    for copy in copies:
        copy.start()
    for copy in copies[: halves + 1]:
        copy.wait()
    for group in range(tokens_ref.shape[0]):
        tokens_ref[group] = slot_tokens(members_ref, counts_ref, devices, group)
    rank_slots(rounds, devices, token_count, tokens_ref, key_ref, value_ref)
    parts = 4
    step = devices // parts
    sends = []
    for part in range(parts):
        picks = [
            pick_rows(
                rounds, devices, bound, block_of(device, devices), token_count, key_ref, value_ref
            )
            for device in range(part * step, (part + 1) * step)
        ]
        if part == 0:
            for copy in copies[halves + 1 :]:
                copy.wait()
        span = pl.ds(part * step * rounds * bound, step * rounds * bound)
        packed_ref[span, :] = dot_nn(jnp.concatenate(picks, axis=0), rows_ref[...]).astype(bf16)
        copy = pltpu.make_async_copy(
            packed_ref.at[span, :], send_hbm.at[span, :], sems.at[halves + 4 + part]
        )
        copy.start()
        sends.append(copy)
    for copy in sends:
        copy.wait()


def index_kernel(
    rounds,
    devices,
    bound,
    token_count,
    tokens_ref,
    place_ref,
    spread_t_ref,
    partner_ref,
    low_ref,
    home_ref,
    table_ref,
    pick_ref,
    key_ref,
    value_ref,
):
    per_device, _, cap = tokens_ref.shape
    me = block_of(lax.axis_index("seq"), devices)
    after = lax.rem(me + 1, devices)
    buffer_rows = devices * bound
    before = earlier(cap)
    source_start = iota((devices, cap), 0) * token_count
    source_place = float_iota((devices, cap), 0) * bound + 1.0
    place_column = float_iota((buffer_rows, cap), 0)
    for r in range(rounds):
        carry = jnp.zeros((devices, 1), f32)
        for group in range(per_device):
            tokens = tokens_ref[group, pl.ds(r * devices + me, 1), :]
            owned = (tokens >= source_start) & (tokens < source_start + token_count)
            rank = dot_nn(one_hot(owned), before) + carry
            carry = carry + jnp.sum(jnp.where(owned, 1.0, 0.0), axis=1, keepdims=True)
            place = (
                jnp.sum(jnp.where(owned, rank + source_place, 0.0), axis=0, keepdims=True) - 1.0
            )
            span = pl.ds(group * cap, cap)
            spread_t_ref[r, :, span] = one_hot(place == place_column)
            place_ref[pl.ds(r * per_device + group, 1), :] = place

    high_count = devices * token_count // lane
    high_start = iota((high_count, cap), 0) * lane
    low_index = iota((lane, cap), 0)
    slot = float_iota((high_count, cap), 1)

    def split(tokens):
        high = (tokens >= high_start) & (tokens < high_start + lane)
        low = jnp.bitwise_and(tokens, lane - 1) == low_index
        return high, low

    for r in range(rounds):

        def one_block(block, total):
            device = device_of(block, devices)
            for group in range(per_device):
                tokens = tokens_ref[group, pl.ds(r * devices + block, 1), :]
                high, low = split(tokens)
                group_index = (device * per_device + group).astype(f32)
                sides = jnp.concatenate(
                    [
                        jnp.where(high, group_index, 0.0).astype(bf16),
                        jnp.where(high, slot, 0.0).astype(bf16),
                    ],
                    axis=0,
                )
                total = total + dot_nt(sides, one_hot(low))
            return total

        total = lax.fori_loop(
            0, devices, one_block, jnp.zeros((2 * high_count, lane), f32), unroll=2
        )
        table_ref[r] = total.astype(bf16)

    halves = cap // lane
    kept = table_kept(per_device * halves)
    row_column = float_iota((devices * kept, cap), 0)
    for r in range(rounds):
        other = 1 - r
        for group in range(per_device + 1):
            if group < per_device:
                tokens = tokens_ref[group, pl.ds(r * devices + me, 1), :]
            else:
                tokens = tokens_ref[0, pl.ds(r * devices + after, 1), :]
            high, low = split(tokens)
            high_hot = one_hot(high)
            found = []
            for part in range(2):
                table = table_ref[other, part * high_count : (part + 1) * high_count, :]
                picked = dot_tn(table, high_hot)
                found.append(jnp.sum(jnp.where(low, picked, 0.0), axis=0, keepdims=True))
            group_index, position = found
            device = jnp.floor((group_index + 0.5) * (1.0 / per_device))
            half = jnp.floor((position + 0.5) * (1.0 / lane))
            row = device * kept + (group_index - device * per_device) * halves + half
            span = pl.ds(group * cap, cap)
            partner_ref[r, :, span] = one_hot(row == row_column)
            low_ref[pl.ds(r * (per_device + 1) + group, 1), :] = position - half * lane

    rank_slots(rounds, devices, token_count, tokens_ref, key_ref, value_ref)

    def pick_device(device, carried):
        at = pl.multiple_of(device * rounds * bound, rounds * bound)
        pick_ref[pl.ds(at, rounds * bound), :] = pick_rows(
            rounds, devices, bound, block_of(device, devices), token_count, key_ref, value_ref
        )
        return carried

    lax.fori_loop(0, devices, pick_device, 0, unroll=2)
    home_ref[...] = jnp.transpose(pick_ref[...])


def table_kept(count):
    return (count + 7) // 8 * 8


def unpack(got_ref, place_ref, r, group, rounds):
    devices, span, width = got_ref.shape
    bound = span // rounds
    cap = place_ref.shape[1]
    row = r * (place_ref.shape[0] // rounds) + group
    received = got_ref[:, r * bound : (r + 1) * bound, :].reshape(devices * bound, width)
    spread = one_hot(place_ref[row : row + 1, :] == float_iota((devices * bound, cap), 0))
    return dot_tn(spread, received).astype(bf16)


def ends_kernel(
    rounds, got_ref, place_ref, last_ref, first_ref, last_cot_ref, first_value_ref
):
    size = got_ref.shape[2] // 3
    per_device = place_ref.shape[0] // rounds
    for r in range(rounds):
        rows = unpack(got_ref, place_ref, r, per_device - 1, rounds)
        last_ref[r] = rows[:, : 2 * size]
        last_cot_ref[r] = rows[:, 2 * size :]
        rows = unpack(got_ref, place_ref, r, 0, rounds)
        first_ref[r, :, :size] = rows[:, :size]
        first_ref[r, :, size:] = rows[:, 2 * size :]
        first_value_ref[r] = rows[:, size : 2 * size]


def inverse_norm(rows):
    wide = rows.astype(f32)
    return lax.rsqrt(jnp.sum(wide * wide, axis=1, keepdims=True) + norm_eps)


def unit_rows(rows):
    return (rows.astype(f32) * inverse_norm(rows)).astype(bf16)


def scored(unit, queries, fill, own):
    cap = queries.shape[0]
    key = iota((cap, cap), 0)
    allowed = key < fill
    if own:
        allowed = allowed & (key != iota((cap, cap), 1))
    return jnp.where(allowed, dot_nt(unit, queries), masked_score)


def normalised(scores, inners):
    highest = jnp.maximum(
        jnp.max(scores[0], axis=0, keepdims=True), jnp.max(scores[1], axis=0, keepdims=True)
    )
    exps = [jnp.exp(score - highest) for score in scores]
    total = jnp.sum(exps[0], axis=0, keepdims=True) + jnp.sum(exps[1], axis=0, keepdims=True)
    inverse = 1.0 / total
    probs = [part * inverse for part in exps]
    dots = jnp.sum(probs[0] * inners[0], axis=0, keepdims=True) + jnp.sum(
        probs[1] * inners[1], axis=0, keepdims=True
    )
    return highest + jnp.log(total), dots, [prob.astype(bf16) for prob in probs]


def forward_inner_kernel(
    rounds,
    devices,
    counts_ref,
    got_ref,
    place_ref,
    last_ref,
    first_ref,
    last_cot_ref,
    first_value_ref,
    rows_ref,
    units_ref,
    prob_ref,
    inner_ref,
    first_score_ref,
    first_inner_ref,
    sums_ref,
):
    cap = prob_ref.shape[3]
    per_device = rows_ref.shape[1]
    size = rows_ref.shape[3] // 3
    base = block_of(lax.axis_index("seq"), devices) * per_device
    for r in range(rounds):
        rows_ref[r, 0, :, :size] = first_ref[r, :, :size]
        rows_ref[r, 0, :, size : 2 * size] = first_value_ref[r]
        rows_ref[r, 0, :, 2 * size :] = first_ref[r, :, size:]
        for group in range(1, per_device - 1):
            rows_ref[r, group] = unpack(got_ref, place_ref, r, group, rounds)
        rows_ref[r, per_device - 1, :, : 2 * size] = last_ref[r]
        rows_ref[r, per_device - 1, :, 2 * size :] = last_cot_ref[r]
        units = [unit_rows(rows_ref[r, group, :, :size]) for group in range(per_device)]
        for group in range(per_device):
            units_ref[r, group] = units[group]
        for group in range(per_device):
            queries = rows_ref[r, group, :, :size]
            cot = rows_ref[r, group, :, 2 * size :]
            values = rows_ref[r, group, :, size : 2 * size]
            score_now = scored(units[group], queries, counts_ref[r, base + group], True)
            inner_now = dot_nt(values, cot)
            if group == 0:
                first_score_ref[r] = score_now
                first_inner_ref[r] = inner_now
                continue
            values = rows_ref[r, group - 1, :, size : 2 * size]
            inner_before = dot_nt(values, cot)
            score_before = scored(
                units[group - 1], queries, counts_ref[r, base + group - 1], False
            )
            inners = [inner_before, inner_now]
            log_total, dots, probs = normalised([score_before, score_now], inners)
            for side in range(2):
                span = slice(side * cap, (side + 1) * cap)
                prob_ref[r, group - 1, span, :] = probs[side]
                inner_ref[r, group - 1, span, :] = inners[side].astype(bf16)
            row = r * per_device + group
            sums_ref[row : row + 1, :] = log_total
            row = (rounds + r) * per_device + group
            sums_ref[row : row + 1, :] = dots


def forward_first_kernel(
    rounds,
    devices,
    counts_ref,
    rows_ref,
    units_ref,
    behind_ref,
    ahead_ref,
    score_ref,
    inner_now_ref,
    inner_sums_ref,
    unit_ref,
    prob_ref,
    inner_ref,
    ahead_score_ref,
    ahead_inner_ref,
    sums_ref,
    send_ref,
):
    cap = prob_ref.shape[2]
    per_device = rows_ref.shape[1]
    size = rows_ref.shape[3] // 3
    groups = counts_ref.shape[1]
    base = block_of(lax.axis_index("seq"), devices) * per_device
    before = lax.rem(base + groups - 1, groups)
    sums_ref[...] = inner_sums_ref[...]
    last = per_device - 1
    for r in range(rounds):
        behind_unit = unit_rows(behind_ref[r, :, :size])
        unit_ref[r] = behind_unit
        queries = rows_ref[r, 0, :, :size]
        cot = rows_ref[r, 0, :, 2 * size :]
        score_before = scored(behind_unit, queries, counts_ref[r, before], False)
        inners = [dot_nt(behind_ref[r, :, size:], cot), inner_now_ref[r]]
        log_total, dots, probs = normalised([score_before, score_ref[r]], inners)
        for side in range(2):
            span = slice(side * cap, (side + 1) * cap)
            prob_ref[r, span, :] = probs[side]
            inner_ref[r, span, :] = inners[side].astype(bf16)
        row = r * per_device
        sums_ref[row : row + 1, :] = log_total
        row = (rounds + r) * per_device
        sums_ref[row : row + 1, :] = dots
        ahead_score_ref[r] = scored(
            units_ref[r, last], ahead_ref[r, :, :size], counts_ref[r, base + last], False
        )
        values = rows_ref[r, last, :, size : 2 * size]
        ahead_inner_ref[r] = dot_nt(values, ahead_ref[r, :, size:]).astype(bf16)
    halves = cap // lane
    count = per_device * halves
    for r in range(rounds):
        for kind in range(2):
            for group in range(per_device):
                row = (kind * rounds + r) * per_device + group
                for half in range(halves):
                    part = sums_ref[row : row + 1, half * lane : (half + 1) * lane]
                    at = (2 * r + kind) * count + group * halves + half
                    send_ref[:, at : at + 1, :] = jnp.broadcast_to(part[None], (devices, 1, lane))


def key_grad(rows, unit_grad):
    wide = rows.astype(f32)
    inverse = inverse_norm(rows)
    along = jnp.sum(wide * unit_grad, axis=1, keepdims=True)
    return inverse * unit_grad - wide * (inverse * inverse * inverse * along)


def three_parts(values):
    high = values.astype(bf16)
    rest = values - high.astype(f32)
    middle = rest.astype(bf16)
    return high, middle, (rest - middle.astype(f32)).astype(bf16)


def backward_kernel(
    rounds,
    devices,
    bound,
    counts_ref,
    everyone_ref,
    partner_ref,
    low_ref,
    sums_ref,
    rows_ref,
    ahead_ref,
    units_ref,
    behind_unit_ref,
    first_prob_ref,
    first_inner_ref,
    prob_ref,
    inner_ref,
    ahead_score_ref,
    ahead_inner_ref,
    spread_t_ref,
    send_ref,
    grads_ref,
):
    cap = rows_ref.shape[2]
    per_device = rows_ref.shape[1]
    size = rows_ref.shape[3] // 3
    groups = counts_ref.shape[1]
    me = block_of(lax.axis_index("seq"), devices)
    ahead_device = device_of(lax.rem(me + 1, devices), devices)
    halves = cap // lane
    count = per_device * halves
    kept = table_kept(count)
    low_column = float_iota((lane, cap), 0)
    slot = iota((1, cap), 1)

    def sums_of_all(r, kind):
        start = (2 * r + kind) * count
        held = min(start, everyone_ref.shape[1] - kept)
        rows = everyone_ref[:, held : held + kept, :]
        if start > held:
            rows = jnp.concatenate(
                [rows[:, start - held :], jnp.zeros((devices, start - held, lane), f32)], axis=1
            )
        return jnp.transpose(rows.reshape(devices * kept, lane))

    def ahead_sums(r, kind):
        start = (2 * r + kind) * count
        rows = [everyone_ref[ahead_device, start + h : start + h + 1, :] for h in range(halves)]
        return jnp.concatenate(rows, axis=1)

    for r in range(rounds):
        logs = three_parts(sums_of_all(1 - r, 0))
        dots = three_parts(sums_of_all(1 - r, 1))
        upright = jnp.concatenate(logs + dots[:2], axis=0)
        picked = dot_nn(upright, partner_ref[r])
        picked_log = picked[:lane] + (picked[lane : 2 * lane] + picked[2 * lane : 3 * lane])
        picked_dot = picked[3 * lane : 4 * lane] + picked[4 * lane :]
        scales = []
        for group in range(per_device + 1):
            at = r * (per_device + 1) + group
            here = low_ref[at : at + 1, :] == low_column
            span = slice(group * cap, (group + 1) * cap)
            other_log = jnp.sum(jnp.where(here, picked_log[:, span], 0.0), axis=0, keepdims=True)
            other_dot = jnp.sum(jnp.where(here, picked_dot[:, span], 0.0), axis=0, keepdims=True)
            if group < per_device:
                row = r * per_device + group
                own_log = sums_ref[row : row + 1, :]
                own_dot = sums_ref[rounds * per_device + row : rounds * per_device + row + 1, :]
            else:
                own_log = ahead_sums(r, 0)
                own_dot = ahead_sums(r, 1)
                ahead_log = own_log
            weight = 1.0 / (1.0 + jnp.exp(other_log - own_log))
            other_weight = 1.0 / (1.0 + jnp.exp(own_log - other_log))
            mixture = weight * own_dot + other_weight * other_dot
            valid = slot < counts_ref[r, lax.rem(me * per_device + group, groups)]
            scales.append((jnp.where(valid, weight, 0.0), jnp.where(valid, mixture, 0.0)))

        def score_grads(prob, inner, scale):
            weighted = prob.astype(f32) * scale[0]
            score_grad = (weighted * (inner.astype(f32) - scale[1])).astype(bf16)
            return weighted.astype(bf16), score_grad

        query_grad = None
        unit_grad = None
        value_grad = None
        for group in range(per_device + 1):
            if group < per_device:
                queries = rows_ref[r, group][:, :size]
                cot = rows_ref[r, group][:, 2 * size :]
            else:
                queries = ahead_ref[r][:, :size]
                cot = ahead_ref[r][:, size:]
            if group == 0:
                probs = [first_prob_ref[r, :cap, :], first_prob_ref[r, cap:, :]]
                inners = [first_inner_ref[r, :cap, :], first_inner_ref[r, cap:, :]]
            elif group < per_device:
                probs = [prob_ref[r, group - 1, :cap, :], prob_ref[r, group - 1, cap:, :]]
                inners = [inner_ref[r, group - 1, :cap, :], inner_ref[r, group - 1, cap:, :]]
            else:
                probs = [jnp.exp(ahead_score_ref[r] - ahead_log)]
                inners = [ahead_inner_ref[r]]
            weighted, score_grad = score_grads(probs[0], inners[0], scales[group])
            if group > 0:
                unit_grad = unit_grad + dot_nn(score_grad, queries)
                value_grad = value_grad + dot_nn(weighted, cot)
                key_part = key_grad(rows_ref[r, group - 1][:, :size], unit_grad)
                span = slice((group - 1) * cap, group * cap)
                grads_ref[span, :size] = (query_grad + key_part).astype(bf16)
                grads_ref[span, size:] = value_grad.astype(bf16)
            if group < per_device:
                unit_before = behind_unit_ref[r] if group == 0 else units_ref[r, group - 1]
                query_grad = dot_tn(score_grad, unit_before)
                weighted, score_grad = score_grads(probs[1], inners[1], scales[group])
                query_grad = query_grad + dot_tn(score_grad, units_ref[r, group])
                unit_grad = dot_nn(score_grad, queries)
                value_grad = dot_nn(weighted, cot)
        packed = dot_nn(spread_t_ref[r], grads_ref[...]).astype(bf16)
        send_ref[:, r * bound : (r + 1) * bound, :] = packed.reshape(devices, bound, 2 * size)


def home_kernel(home_ref, got_ref, qk_ref, value_ref):
    size = qk_ref.shape[1]
    total = dot_nn(home_ref[...], got_ref[...])
    qk_ref[...] = total[:, :size].astype(bf16)
    value_ref[...] = total[:, size:].astype(bf16)


def exchange(array):
    return lax.all_to_all(array, "seq", split_axis=0, concat_axis=0, tiled=True)


def shifted(array, by):
    devices = lax.axis_size("seq")
    order = [device_of(block, devices) for block in range(devices)]
    return lax.ppermute(array, "seq", [(order[i], order[(i + by) % devices]) for i in range(devices)])


def head_backward(qk, values, cot, members, counts):
    devices = lax.axis_size("seq")
    token_count, size = qk.shape
    rounds, groups, cap = members.shape
    per_device = groups // devices
    slots = per_device * cap
    bound = 2 * token_count // devices
    span = rounds * bound
    buffer_rows = devices * bound
    sum_rows = 2 * rounds * per_device
    listed = members.reshape(rounds * groups, cap)
    keys = [((per_device, rounds * devices, cap), f32)] * 2
    pick = ((devices * span, token_count), bf16)
    send, tokens = call(
        functools.partial(pack_kernel, rounds, devices, bound),
        [((devices * span, 3 * size), bf16), (keys[0][0], jnp.int32)],
        [counts, listed, qk, values, cot],
        [((devices * span, 3 * size), bf16)]
        + keys
        + [
            (counts.shape, jnp.int32),
            ((cap // lane, rounds * groups, lane), jnp.int32),
            ((token_count, 3 * size), bf16),
        ],
        remote=5,
        semaphores=cap // lane + 8,
        far=(0,),
        direct=(0,),
    )
    got = exchange(send).reshape(devices, span, 3 * size)
    place, spread_t, partner, low, home_pick = call(
        functools.partial(index_kernel, rounds, devices, bound, token_count),
        [
            ((rounds * per_device, cap), f32),
            ((rounds, buffer_rows, slots), bf16),
            ((rounds, devices * table_kept(slots // lane), slots + cap), bf16),
            ((rounds * (per_device + 1), cap), f32),
            ((token_count, devices * span), bf16),
        ],
        [tokens],
        [((rounds, 2 * devices * token_count // lane, lane), bf16), pick] + keys,
        far=(1, 2, 4),
    )
    last, first, last_cot, first_value = call(
        functools.partial(ends_kernel, rounds),
        [((rounds, cap, 2 * size), bf16)] * 2 + [((rounds, cap, size), bf16)] * 2,
        [got, place],
    )
    behind = shifted(last, 1)
    ahead = shifted(first, -1)
    square = (rounds, cap, cap)
    rows, units, prob, inner, first_score, first_inner_now, inner_sums = call(
        functools.partial(forward_inner_kernel, rounds, devices),
        [
            ((rounds, per_device, cap, 3 * size), bf16),
            ((rounds, per_device, cap, size), bf16),
            ((rounds, per_device - 1, 2 * cap, cap), bf16),
            ((rounds, per_device - 1, 2 * cap, cap), bf16),
            (square, f32),
            (square, f32),
            ((sum_rows, cap), f32),
        ],
        [counts, got, place, last, first, last_cot, first_value],
        scalars=1,
    )
    behind_unit, first_prob, first_inner, ahead_score, ahead_inner, sums, sums_send = call(
        functools.partial(forward_first_kernel, rounds, devices),
        [
            ((rounds, cap, size), bf16),
            ((rounds, 2 * cap, cap), bf16),
            ((rounds, 2 * cap, cap), bf16),
            (square, f32),
            (square, bf16),
            ((sum_rows, cap), f32),
            ((devices, sum_rows * cap // lane, lane), f32),
        ],
        [counts, rows, units, behind, ahead, first_score, first_inner_now, inner_sums],
        scalars=1,
    )
    everyone = exchange(sums_send)
    (grads_send,) = call(
        functools.partial(backward_kernel, rounds, devices, bound),
        [((devices, span, 2 * size), bf16)],
        [
            counts,
            everyone,
            partner,
            low,
            sums,
            rows,
            ahead,
            units,
            behind_unit,
            first_prob,
            first_inner,
            prob,
            inner,
            ahead_score,
            ahead_inner,
            spread_t,
        ],
        [((slots, 2 * size), bf16)],
        scalars=1,
    )
    home = exchange(grads_send.reshape(devices * span, 2 * size))
    return call(
        home_kernel,
        [((token_count, size), bf16), ((token_count, size), bf16)],
        [home_pick, home],
    )


def on_device(qk, values, grad_out, members, counts):
    grad_qk, grad_v = head_backward(qk[0], values[0], grad_out[0], members[0], counts[0])
    return (grad_qk[None], grad_v[None])


def solution(mesh):
    in_specs = (
        P("head", "seq", None),
        P("head", "seq", None),
        P("head", "seq", None),
        P("head", None, None, None),
        P("head", None, None),
    )
    out_specs = (P("head", "seq", None), P("head", "seq", None))
    return jax.shard_map(
        on_device, mesh=mesh, in_specs=in_specs, out_specs=out_specs, check_vma=False
    )
```

```python
import functools
import math

import jax
import jax.numpy as jnp
from jax import lax
from jax.experimental import pallas as pl
from jax.experimental.pallas import tpu as pltpu
from jax.sharding import PartitionSpec as P

masked_score = -1e30
norm_eps = 1e-06
lane = 128
f32 = jnp.float32
bf16 = jnp.bfloat16


def iota(shape, axis):
    return lax.broadcasted_iota(jnp.int32, shape, axis)


def float_iota(shape, axis):
    return iota(shape, axis).astype(f32)


def dot_nn(a, b):
    return lax.dot_general(a, b, (((1,), (0,)), ((), ())), preferred_element_type=f32)


def dot_nt(a, b):
    return lax.dot_general(a, b, (((1,), (1,)), ((), ())), preferred_element_type=f32)


def dot_tn(a, b):
    return lax.dot_general(a, b, (((0,), (0,)), ((), ())), preferred_element_type=f32)


def one_hot(condition):
    return jnp.where(condition, 1.0, 0.0).astype(bf16)


def short_hot(index, shape, axis):
    place = iota(shape, axis).astype(jnp.int16)
    short = jnp.broadcast_to(index.astype(jnp.int32), shape).astype(jnp.int16)
    return jnp.where(short == place, jnp.ones(shape, bf16), jnp.zeros(shape, bf16))


def block_of(device, devices):
    if devices % 4:
        return device
    depth = devices // 4
    level, column = device // 4, device % 4
    turn = column ^ (column >> 1)
    step = level + (turn % 2) * (depth - 1 - 2 * level)
    return turn * depth + step


def device_of(block, devices):
    if devices % 4:
        return block
    depth = devices // 4
    turn, step = block // depth, block % depth
    level = step + (turn % 2) * (depth - 1 - 2 * step)
    return level * 4 + (turn ^ (turn >> 1))


def earlier(size):
    return one_hot(iota((size, size), 0) < iota((size, size), 1))


def call(kernel, out_shapes, operands, scratch=(), scalars=0, remote=0, semaphores=0, far=(), direct=()):
    count = len(operands)
    held = sum(array.size * array.dtype.itemsize for array in operands[scalars : count - remote])
    for shape, dtype in list(out_shapes) + list(scratch):
        held += math.prod(shape) * jnp.dtype(dtype).itemsize
    spaces = (
        [pltpu.SMEM] * scalars + [pltpu.VMEM] * (count - scalars - remote) + [pltpu.HBM] * remote
    )
    operands = [
        pltpu.with_memory_space_constraint(array, space) if space is pltpu.HBM else array
        for array, space in zip(operands, spaces)
    ]
    return pl.pallas_call(
        kernel,
        out_shape=tuple(
            pltpu.HBM(shape, dtype) if at in far else jax.ShapeDtypeStruct(shape, dtype)
            for at, (shape, dtype) in enumerate(out_shapes)
        ),
        in_specs=[pl.BlockSpec(memory_space=space) for space in spaces],
        out_specs=tuple(
            pl.BlockSpec(memory_space=pltpu.HBM if at in direct else pltpu.VMEM)
            for at in range(len(out_shapes))
        ),
        scratch_shapes=[pltpu.VMEM(shape, dtype) for shape, dtype in scratch]
        + [pltpu.SemaphoreType.DMA((semaphores,))] * min(semaphores, 1),
        compiler_params=pltpu.CompilerParams(vmem_limit_bytes=held + 12 * 1024 * 1024),
    )(*operands)


def slot_tokens(members_ref, counts_ref, devices, group):
    rounds, groups = counts_ref.shape
    per_device = groups // devices
    rows = pl.ds(group, rounds * devices, stride=per_device)
    parts = [members_ref[half, rows, :] for half in range(members_ref.shape[0])]
    listed = jnp.concatenate(parts, axis=1)
    diagonal = iota((devices, groups), 1) == iota((devices, groups), 0) * per_device + group
    limits = [
        jnp.sum(
            jnp.where(diagonal, counts_ref[r : r + 1, :].astype(f32), 0.0), axis=1, keepdims=True
        )
        for r in range(rounds)
    ]
    limit = jnp.concatenate(limits, axis=0)
    return jnp.where(float_iota(listed.shape, 1) < limit, listed, -1)


def rank_slots(rounds, devices, token_count, tokens_ref, key_ref, value_ref):
    per_device, _, cap = key_ref.shape
    start = lax.axis_index("seq") * token_count
    before = earlier(cap)
    carry = jnp.zeros((rounds * devices, 1), f32)
    for group in range(per_device):
        local = tokens_ref[group] - start
        owned = (local >= 0) & (local < token_count)
        rank = dot_nn(one_hot(owned), before) + carry
        carry = carry + jnp.sum(jnp.where(owned, 1.0, 0.0), axis=1, keepdims=True)
        key_ref[group] = jnp.where(owned, rank, -1.0)
        value_ref[group] = jnp.where(owned, local + 1, 0).astype(f32)


def pick_rows(rounds, devices, bound, block, token_count, key_ref, value_ref):
    per_device, _, cap = key_ref.shape
    column = float_iota((bound, cap), 0)
    picks = []
    for r in range(rounds):
        row = r * devices + block
        total = jnp.zeros((bound, cap), f32)
        for group in range(per_device):
            ranks = key_ref[group, pl.ds(row, 1), :]
            values = value_ref[group, pl.ds(row, 1), :]
            total = total + jnp.where(ranks == column, values, 0.0)
        index = jnp.sum(total, axis=1, keepdims=True) - 1.0
        picks.append(short_hot(index, (bound, token_count), 1))
    return jnp.concatenate(picks, axis=0)


def pack_kernel(
    rounds,
    devices,
    bound,
    counts_hbm,
    members_hbm,
    q_hbm,
    v_hbm,
    g_hbm,
    send_hbm,
    tokens_ref,
    packed_ref,
    key_ref,
    value_ref,
    counts_ref,
    members_ref,
    rows_ref,
    sems,
):
    token_count, size = q_hbm.shape
    halves = members_ref.shape[0]
    copies = [pltpu.make_async_copy(counts_hbm, counts_ref, sems.at[halves + 3])]
    for half in range(halves):
        source = members_hbm.at[:, pl.ds(half * lane, lane)]
        copies.append(pltpu.make_async_copy(source, members_ref.at[half], sems.at[half]))
    for at, source in enumerate((q_hbm, v_hbm, g_hbm)):
        target = rows_ref.at[:, pl.ds(at * size, size)]
        copies.append(pltpu.make_async_copy(source, target, sems.at[halves + at]))
    for copy in copies:
        copy.start()
    for copy in copies[: halves + 1]:
        copy.wait()
    for group in range(tokens_ref.shape[0]):
        tokens_ref[group] = slot_tokens(members_ref, counts_ref, devices, group)
    rank_slots(rounds, devices, token_count, tokens_ref, key_ref, value_ref)
    parts = 4
    step = devices // parts
    sends = []
    for part in range(parts):
        picks = [
            pick_rows(
                rounds, devices, bound, block_of(device, devices), token_count, key_ref, value_ref
            )
            for device in range(part * step, (part + 1) * step)
        ]
        if part == 0:
            for copy in copies[halves + 1 :]:
                copy.wait()
        span = pl.ds(part * step * rounds * bound, step * rounds * bound)
        packed_ref[span, :] = dot_nn(jnp.concatenate(picks, axis=0), rows_ref[...]).astype(bf16)
        copy = pltpu.make_async_copy(
            packed_ref.at[span, :], send_hbm.at[span, :], sems.at[halves + 4 + part]
        )
        copy.start()
        sends.append(copy)
    for copy in sends:
        copy.wait()


def index_kernel(
    rounds,
    devices,
    bound,
    token_count,
    tokens_ref,
    place_ref,
    spread_t_ref,
    partner_ref,
    low_ref,
    home_ref,
    table_ref,
    pick_ref,
    key_ref,
    value_ref,
):
    per_device, _, cap = tokens_ref.shape
    me = block_of(lax.axis_index("seq"), devices)
    after = lax.rem(me + 1, devices)
    buffer_rows = devices * bound
    before = earlier(cap)
    source_start = iota((devices, cap), 0) * token_count
    source_place = float_iota((devices, cap), 0) * bound + 1.0
    place_column = float_iota((buffer_rows, cap), 0)
    for r in range(rounds):
        carry = jnp.zeros((devices, 1), f32)
        for group in range(per_device):
            tokens = tokens_ref[group, pl.ds(r * devices + me, 1), :]
            owned = (tokens >= source_start) & (tokens < source_start + token_count)
            rank = dot_nn(one_hot(owned), before) + carry
            carry = carry + jnp.sum(jnp.where(owned, 1.0, 0.0), axis=1, keepdims=True)
            place = (
                jnp.sum(jnp.where(owned, rank + source_place, 0.0), axis=0, keepdims=True) - 1.0
            )
            span = pl.ds(group * cap, cap)
            spread_t_ref[r, :, span] = one_hot(place == place_column)
            place_ref[pl.ds(r * per_device + group, 1), :] = place

    high_count = devices * token_count // lane
    high_start = iota((high_count, cap), 0) * lane
    low_index = iota((lane, cap), 0)
    slot = float_iota((high_count, cap), 1)

    def split(tokens):
        high = (tokens >= high_start) & (tokens < high_start + lane)
        low = jnp.bitwise_and(tokens, lane - 1) == low_index
        return high, low

    for r in range(rounds):

        def one_block(block, total):
            device = device_of(block, devices)
            for group in range(per_device):
                tokens = tokens_ref[group, pl.ds(r * devices + block, 1), :]
                high, low = split(tokens)
                group_index = (device * per_device + group).astype(f32)
                sides = jnp.concatenate(
                    [
                        jnp.where(high, group_index, 0.0).astype(bf16),
                        jnp.where(high, slot, 0.0).astype(bf16),
                    ],
                    axis=0,
                )
                total = total + dot_nt(sides, one_hot(low))
            return total

        total = lax.fori_loop(
            0, devices, one_block, jnp.zeros((2 * high_count, lane), f32), unroll=2
        )
        table_ref[r] = total.astype(bf16)

    halves = cap // lane
    kept = table_kept(per_device * halves)
    row_column = float_iota((devices * kept, cap), 0)
    for r in range(rounds):
        other = 1 - r
        for group in range(per_device + 1):
            if group < per_device:
                tokens = tokens_ref[group, pl.ds(r * devices + me, 1), :]
            else:
                tokens = tokens_ref[0, pl.ds(r * devices + after, 1), :]
            high, low = split(tokens)
            high_hot = one_hot(high)
            found = []
            for part in range(2):
                table = table_ref[other, part * high_count : (part + 1) * high_count, :]
                picked = dot_tn(table, high_hot)
                found.append(jnp.sum(jnp.where(low, picked, 0.0), axis=0, keepdims=True))
            group_index, position = found
            device = jnp.floor((group_index + 0.5) * (1.0 / per_device))
            half = jnp.floor((position + 0.5) * (1.0 / lane))
            row = device * kept + (group_index - device * per_device) * halves + half
            span = pl.ds(group * cap, cap)
            partner_ref[r, :, span] = one_hot(row == row_column)
            low_ref[pl.ds(r * (per_device + 1) + group, 1), :] = position - half * lane

    rank_slots(rounds, devices, token_count, tokens_ref, key_ref, value_ref)

    def pick_device(device, carried):
        at = pl.multiple_of(device * rounds * bound, rounds * bound)
        pick_ref[pl.ds(at, rounds * bound), :] = pick_rows(
            rounds, devices, bound, block_of(device, devices), token_count, key_ref, value_ref
        )
        return carried

    lax.fori_loop(0, devices, pick_device, 0, unroll=2)
    home_ref[...] = jnp.transpose(pick_ref[...])


def table_kept(count):
    return (count + 7) // 8 * 8


def spread_of(place_ref, r, group, rounds, buffer_rows):
    row = r * (place_ref.shape[0] // rounds) + group
    cap = place_ref.shape[1]
    return short_hot(place_ref[row : row + 1, :], (buffer_rows, cap), 0)


def received_rows(got_ref, r, rounds):
    devices, span, width = got_ref.shape
    bound = span // rounds
    return got_ref[:, r * bound : (r + 1) * bound, :].reshape(devices * bound, width)


def last_kernel(rounds, got_ref, place_ref, last_ref):
    size = got_ref.shape[2] // 3
    per_device = place_ref.shape[0] // rounds
    for r in range(rounds):
        received = received_rows(got_ref, r, rounds)
        spread = spread_of(place_ref, r, per_device - 1, rounds, received.shape[0])
        last_ref[r] = dot_tn(spread, received[:, : 2 * size]).astype(bf16)


def first_kernel(rounds, got_ref, place_ref, first_ref):
    size = got_ref.shape[2] // 3
    for r in range(rounds):
        received = received_rows(got_ref, r, rounds)
        spread = spread_of(place_ref, r, 0, rounds, received.shape[0])
        wanted = jnp.concatenate([received[:, :size], received[:, 2 * size :]], axis=1)
        first_ref[r] = dot_tn(spread, wanted).astype(bf16)


def inverse_norm(rows):
    wide = rows.astype(f32)
    return lax.rsqrt(jnp.sum(wide * wide, axis=1, keepdims=True) + norm_eps)


def unit_rows(rows):
    return (rows.astype(f32) * inverse_norm(rows)).astype(bf16)


def scored(unit, queries, fill, own):
    cap = queries.shape[0]
    key = iota((cap, cap), 0)
    allowed = key < fill
    if own:
        allowed = allowed & (key != iota((cap, cap), 1))
    return jnp.where(allowed, dot_nt(unit, queries), masked_score)


def normalised(scores, inners):
    highest = jnp.maximum(
        jnp.max(scores[0], axis=0, keepdims=True), jnp.max(scores[1], axis=0, keepdims=True)
    )
    exps = [jnp.exp(score - highest) for score in scores]
    total = jnp.sum(exps[0], axis=0, keepdims=True) + jnp.sum(exps[1], axis=0, keepdims=True)
    inverse = 1.0 / total
    probs = [part * inverse for part in exps]
    dots = jnp.sum(probs[0] * inners[0], axis=0, keepdims=True) + jnp.sum(
        probs[1] * inners[1], axis=0, keepdims=True
    )
    return highest + jnp.log(total), dots, [prob.astype(bf16) for prob in probs]


def forward_inner_kernel(
    rounds,
    devices,
    counts_ref,
    got_ref,
    place_ref,
    last_ref,
    first_ref,
    rows_ref,
    units_ref,
    prob_ref,
    inner_ref,
    first_score_ref,
    first_inner_ref,
    sums_ref,
):
    cap = prob_ref.shape[3]
    per_device = rows_ref.shape[1]
    size = rows_ref.shape[3] // 3
    base = block_of(lax.axis_index("seq"), devices) * per_device
    for r in range(rounds):
        received = received_rows(got_ref, r, rounds)
        for group in range(per_device):
            spread = spread_of(place_ref, r, group, rounds, received.shape[0])
            if group == 0:
                values = dot_tn(spread, received[:, size : 2 * size]).astype(bf16)
                rows_ref[r, group, :, :size] = first_ref[r, :, :size]
                rows_ref[r, group, :, size : 2 * size] = values
                rows_ref[r, group, :, 2 * size :] = first_ref[r, :, size:]
            elif group < per_device - 1:
                rows_ref[r, group] = dot_tn(spread, received).astype(bf16)
            else:
                rows_ref[r, group, :, : 2 * size] = last_ref[r]
                cots = dot_tn(spread, received[:, 2 * size :]).astype(bf16)
                rows_ref[r, group, :, 2 * size :] = cots
        units = [unit_rows(rows_ref[r, group, :, :size]) for group in range(per_device)]
        for group in range(per_device):
            units_ref[r, group] = units[group]
        for group in range(per_device):
            queries = rows_ref[r, group, :, :size]
            cot = rows_ref[r, group, :, 2 * size :]
            values = rows_ref[r, group, :, size : 2 * size]
            score_now = scored(units[group], queries, counts_ref[r, base + group], True)
            inner_now = dot_nt(values, cot)
            if group == 0:
                first_score_ref[r] = score_now
                first_inner_ref[r] = inner_now
                continue
            values = rows_ref[r, group - 1, :, size : 2 * size]
            inner_before = dot_nt(values, cot)
            score_before = scored(
                units[group - 1], queries, counts_ref[r, base + group - 1], False
            )
            inners = [inner_before, inner_now]
            log_total, dots, probs = normalised([score_before, score_now], inners)
            for side in range(2):
                span = slice(side * cap, (side + 1) * cap)
                prob_ref[r, group - 1, span, :] = probs[side]
                inner_ref[r, group - 1, span, :] = inners[side].astype(bf16)
            row = r * per_device + group
            sums_ref[row : row + 1, :] = log_total
            row = (rounds + r) * per_device + group
            sums_ref[row : row + 1, :] = dots


def forward_first_kernel(
    rounds,
    devices,
    counts_ref,
    rows_ref,
    behind_ref,
    score_ref,
    inner_now_ref,
    inner_sums_ref,
    unit_ref,
    prob_ref,
    inner_ref,
    sums_ref,
    send_ref,
    block_ref,
):
    cap = prob_ref.shape[2]
    per_device = rows_ref.shape[1]
    size = rows_ref.shape[3] // 3
    groups = counts_ref.shape[1]
    base = block_of(lax.axis_index("seq"), devices) * per_device
    before = lax.rem(base + groups - 1, groups)
    sums_ref[...] = inner_sums_ref[...]
    for r in range(rounds):
        behind_unit = unit_rows(behind_ref[r, :, :size])
        unit_ref[r] = behind_unit
        queries = rows_ref[r, 0, :, :size]
        cot = rows_ref[r, 0, :, 2 * size :]
        score_before = scored(behind_unit, queries, counts_ref[r, before], False)
        inners = [dot_nt(behind_ref[r, :, size:], cot), inner_now_ref[r]]
        log_total, dots, probs = normalised([score_before, score_ref[r]], inners)
        for side in range(2):
            span = slice(side * cap, (side + 1) * cap)
            prob_ref[r, span, :] = probs[side]
            inner_ref[r, span, :] = inners[side].astype(bf16)
        row = r * per_device
        sums_ref[row : row + 1, :] = log_total
        row = (rounds + r) * per_device
        sums_ref[row : row + 1, :] = dots
    halves = cap // lane
    count = per_device * halves
    for r in range(rounds):
        for kind in range(2):
            for group in range(per_device):
                row = (kind * rounds + r) * per_device + group
                for half in range(halves):
                    at = (2 * r + kind) * count + group * halves + half
                    block_ref[at : at + 1, :] = sums_ref[
                        row : row + 1, half * lane : (half + 1) * lane
                    ]
    block = block_ref[...]
    for device in range(devices):
        send_ref[device] = block


def key_grad(rows, unit_grad):
    wide = rows.astype(f32)
    inverse = inverse_norm(rows)
    along = jnp.sum(wide * unit_grad, axis=1, keepdims=True)
    return inverse * unit_grad - wide * (inverse * inverse * inverse * along)


def three_parts(values):
    high = values.astype(bf16)
    rest = values - high.astype(f32)
    middle = rest.astype(bf16)
    return high, middle, (rest - middle.astype(f32)).astype(bf16)


def backward_kernel(
    rounds,
    devices,
    bound,
    counts_ref,
    everyone_ref,
    partner_ref,
    low_ref,
    sums_ref,
    rows_ref,
    ahead_ref,
    units_ref,
    behind_unit_ref,
    first_prob_ref,
    first_inner_ref,
    prob_ref,
    inner_ref,
    spread_t_ref,
    send_ref,
    grads_ref,
):
    cap = rows_ref.shape[2]
    per_device = rows_ref.shape[1]
    size = rows_ref.shape[3] // 3
    groups = counts_ref.shape[1]
    me = block_of(lax.axis_index("seq"), devices)
    ahead_device = device_of(lax.rem(me + 1, devices), devices)
    halves = cap // lane
    count = per_device * halves
    kept = table_kept(count)
    low_column = float_iota((lane, cap), 0)
    slot = iota((1, cap), 1)

    def sums_of_all(r, kind):
        start = (2 * r + kind) * count
        held = min(start, everyone_ref.shape[1] - kept)
        rows = everyone_ref[:, held : held + kept, :]
        if start > held:
            rows = jnp.concatenate(
                [rows[:, start - held :], jnp.zeros((devices, start - held, lane), f32)], axis=1
            )
        return jnp.transpose(rows.reshape(devices * kept, lane))

    def ahead_sums(r, kind):
        start = (2 * r + kind) * count
        rows = [everyone_ref[ahead_device, start + h : start + h + 1, :] for h in range(halves)]
        return jnp.concatenate(rows, axis=1)

    for r in range(rounds):
        logs = three_parts(sums_of_all(1 - r, 0))
        dots = three_parts(sums_of_all(1 - r, 1))
        upright = jnp.concatenate(logs + dots[:2], axis=0)
        picked = dot_nn(upright, partner_ref[r])
        picked_log = picked[:lane] + (picked[lane : 2 * lane] + picked[2 * lane : 3 * lane])
        picked_dot = picked[3 * lane : 4 * lane] + picked[4 * lane :]
        scales = []
        for group in range(per_device + 1):
            at = r * (per_device + 1) + group
            here = low_ref[at : at + 1, :] == low_column
            span = slice(group * cap, (group + 1) * cap)
            other_log = jnp.sum(jnp.where(here, picked_log[:, span], 0.0), axis=0, keepdims=True)
            other_dot = jnp.sum(jnp.where(here, picked_dot[:, span], 0.0), axis=0, keepdims=True)
            if group < per_device:
                row = r * per_device + group
                own_log = sums_ref[row : row + 1, :]
                own_dot = sums_ref[rounds * per_device + row : rounds * per_device + row + 1, :]
            else:
                own_log = ahead_sums(r, 0)
                own_dot = ahead_sums(r, 1)
                ahead_log = own_log
            weight = 1.0 / (1.0 + jnp.exp(other_log - own_log))
            other_weight = 1.0 / (1.0 + jnp.exp(own_log - other_log))
            mixture = weight * own_dot + other_weight * other_dot
            valid = slot < counts_ref[r, lax.rem(me * per_device + group, groups)]
            scales.append((jnp.where(valid, weight, 0.0), jnp.where(valid, mixture, 0.0)))

        def score_grads(prob, inner, scale):
            weighted = prob.astype(f32) * scale[0]
            score_grad = (weighted * (inner.astype(f32) - scale[1])).astype(bf16)
            return weighted.astype(bf16), score_grad

        query_grad = None
        unit_grad = None
        value_grad = None
        for group in range(per_device + 1):
            if group < per_device:
                queries = rows_ref[r, group][:, :size]
                cot = rows_ref[r, group][:, 2 * size :]
            else:
                queries = ahead_ref[r][:, :size]
                cot = ahead_ref[r][:, size:]
            if group == 0:
                probs = [first_prob_ref[r, :cap, :], first_prob_ref[r, cap:, :]]
                inners = [first_inner_ref[r, :cap, :], first_inner_ref[r, cap:, :]]
            elif group < per_device:
                probs = [prob_ref[r, group - 1, :cap, :], prob_ref[r, group - 1, cap:, :]]
                inners = [inner_ref[r, group - 1, :cap, :], inner_ref[r, group - 1, cap:, :]]
            else:
                fill = counts_ref[r, me * per_device + per_device - 1]
                score = scored(units_ref[r, per_device - 1], queries, fill, False)
                probs = [jnp.exp(score - ahead_log)]
                inners = [dot_nt(rows_ref[r, per_device - 1][:, size : 2 * size], cot)]
            weighted, score_grad = score_grads(probs[0], inners[0], scales[group])
            if group > 0:
                unit_grad = unit_grad + dot_nn(score_grad, queries)
                value_grad = value_grad + dot_nn(weighted, cot)
                key_part = key_grad(rows_ref[r, group - 1][:, :size], unit_grad)
                span = slice((group - 1) * cap, group * cap)
                grads_ref[span, :size] = (query_grad + key_part).astype(bf16)
                grads_ref[span, size:] = value_grad.astype(bf16)
            if group < per_device:
                unit_before = behind_unit_ref[r] if group == 0 else units_ref[r, group - 1]
                query_grad = dot_tn(score_grad, unit_before)
                weighted, score_grad = score_grads(probs[1], inners[1], scales[group])
                query_grad = query_grad + dot_tn(score_grad, units_ref[r, group])
                unit_grad = dot_nn(score_grad, queries)
                value_grad = dot_nn(weighted, cot)
        packed = dot_nn(spread_t_ref[r], grads_ref[...]).astype(bf16)
        send_ref[:, r * bound : (r + 1) * bound, :] = packed.reshape(devices, bound, 2 * size)


def home_kernel(home_ref, got_ref, qk_ref, value_ref):
    size = qk_ref.shape[1]
    total = dot_nn(home_ref[...], got_ref[...])
    qk_ref[...] = total[:, :size].astype(bf16)
    value_ref[...] = total[:, size:].astype(bf16)


def exchange(array):
    return lax.all_to_all(array, "seq", split_axis=0, concat_axis=0, tiled=True)


def shifted(array, by):
    devices = lax.axis_size("seq")
    order = [device_of(block, devices) for block in range(devices)]
    return lax.ppermute(array, "seq", [(order[i], order[(i + by) % devices]) for i in range(devices)])


def head_backward(qk, values, cot, members, counts):
    devices = lax.axis_size("seq")
    token_count, size = qk.shape
    rounds, groups, cap = members.shape
    per_device = groups // devices
    slots = per_device * cap
    bound = 2 * token_count // devices
    span = rounds * bound
    buffer_rows = devices * bound
    sum_rows = 2 * rounds * per_device
    listed = members.reshape(rounds * groups, cap)
    keys = [((per_device, rounds * devices, cap), f32)] * 2
    pick = ((devices * span, token_count), bf16)
    send, tokens = call(
        functools.partial(pack_kernel, rounds, devices, bound),
        [((devices * span, 3 * size), bf16), (keys[0][0], jnp.int32)],
        [counts, listed, qk, values, cot],
        [((devices * span, 3 * size), bf16)]
        + keys
        + [
            (counts.shape, jnp.int32),
            ((cap // lane, rounds * groups, lane), jnp.int32),
            ((token_count, 3 * size), bf16),
        ],
        remote=5,
        semaphores=cap // lane + 8,
        far=(0,),
        direct=(0,),
    )
    got = exchange(send).reshape(devices, span, 3 * size)
    place, spread_t, partner, low, home_pick = call(
        functools.partial(index_kernel, rounds, devices, bound, token_count),
        [
            ((rounds * per_device, cap), f32),
            ((rounds, buffer_rows, slots), bf16),
            ((rounds, devices * table_kept(slots // lane), slots + cap), bf16),
            ((rounds * (per_device + 1), cap), f32),
            ((token_count, devices * span), bf16),
        ],
        [tokens],
        [((rounds, 2 * devices * token_count // lane, lane), bf16), pick] + keys,
        far=(1, 2, 4),
    )
    (last,) = call(
        functools.partial(last_kernel, rounds), [((rounds, cap, 2 * size), bf16)], [got, place]
    )
    behind = shifted(last, 1)
    (first,) = call(
        functools.partial(first_kernel, rounds), [((rounds, cap, 2 * size), bf16)], [got, place]
    )
    ahead = shifted(first, -1)
    square = (rounds, cap, cap)
    rows, units, prob, inner, first_score, first_inner_now, inner_sums = call(
        functools.partial(forward_inner_kernel, rounds, devices),
        [
            ((rounds, per_device, cap, 3 * size), bf16),
            ((rounds, per_device, cap, size), bf16),
            ((rounds, per_device - 1, 2 * cap, cap), bf16),
            ((rounds, per_device - 1, 2 * cap, cap), bf16),
            (square, f32),
            (square, f32),
            ((sum_rows, cap), f32),
        ],
        [counts, got, place, last, first],
        scalars=1,
    )
    behind_unit, first_prob, first_inner, sums, sums_send = call(
        functools.partial(forward_first_kernel, rounds, devices),
        [
            ((rounds, cap, size), bf16),
            ((rounds, 2 * cap, cap), bf16),
            ((rounds, 2 * cap, cap), bf16),
            ((sum_rows, cap), f32),
            ((devices, sum_rows * cap // lane, lane), f32),
        ],
        [counts, rows, behind, first_score, first_inner_now, inner_sums],
        [((sum_rows * cap // lane, lane), f32)],
        scalars=1,
    )
    sums_send, ahead = lax.optimization_barrier((sums_send, ahead))
    everyone = exchange(sums_send)
    (grads_send,) = call(
        functools.partial(backward_kernel, rounds, devices, bound),
        [((devices, span, 2 * size), bf16)],
        [
            counts,
            everyone,
            partner,
            low,
            sums,
            rows,
            ahead,
            units,
            behind_unit,
            first_prob,
            first_inner,
            prob,
            inner,
            spread_t,
        ],
        [((slots, 2 * size), bf16)],
        scalars=1,
    )
    home = exchange(grads_send.reshape(devices * span, 2 * size))
    return call(
        home_kernel,
        [((token_count, size), bf16), ((token_count, size), bf16)],
        [home_pick, home],
    )


def on_device(qk, values, grad_out, members, counts):
    grad_qk, grad_v = head_backward(qk[0], values[0], grad_out[0], members[0], counts[0])
    return (grad_qk[None], grad_v[None])


def solution(mesh):
    in_specs = (
        P("head", "seq", None),
        P("head", "seq", None),
        P("head", "seq", None),
        P("head", None, None, None),
        P("head", None, None),
    )
    out_specs = (P("head", "seq", None), P("head", "seq", None))
    return jax.shard_map(
        on_device, mesh=mesh, in_specs=in_specs, out_specs=out_specs, check_vma=False
    )
```

```python
import functools
import math

import jax
import jax.numpy as jnp
from jax import lax
from jax.experimental import pallas as pl
from jax.experimental.pallas import tpu as pltpu
from jax.sharding import PartitionSpec as P

masked_score = -1e30
norm_eps = 1e-06
lane = 128
f32 = jnp.float32
bf16 = jnp.bfloat16


def iota(shape, axis):
    return lax.broadcasted_iota(jnp.int32, shape, axis)


def float_iota(shape, axis):
    return iota(shape, axis).astype(f32)


def dot_nn(a, b):
    return lax.dot_general(a, b, (((1,), (0,)), ((), ())), preferred_element_type=f32)


def dot_nt(a, b):
    return lax.dot_general(a, b, (((1,), (1,)), ((), ())), preferred_element_type=f32)


def dot_tn(a, b):
    return lax.dot_general(a, b, (((0,), (0,)), ((), ())), preferred_element_type=f32)


def one_hot(condition):
    return jnp.where(condition, 1.0, 0.0).astype(bf16)


def short_hot(index, shape, axis):
    place = iota(shape, axis).astype(jnp.int16)
    short = jnp.broadcast_to(index.astype(jnp.int32), shape).astype(jnp.int16)
    return jnp.where(short == place, jnp.ones(shape, bf16), jnp.zeros(shape, bf16))


def block_of(device, devices):
    if devices % 4:
        return device
    depth = devices // 4
    level, column = device // 4, device % 4
    turn = column ^ (column >> 1)
    step = level + (turn % 2) * (depth - 1 - 2 * level)
    return turn * depth + step


def device_of(block, devices):
    if devices % 4:
        return block
    depth = devices // 4
    turn, step = block // depth, block % depth
    level = step + (turn % 2) * (depth - 1 - 2 * step)
    return level * 4 + (turn ^ (turn >> 1))


def earlier(size):
    return one_hot(iota((size, size), 0) < iota((size, size), 1))


def call(kernel, out_shapes, operands, scratch=(), remote=0, semaphores=0, far=(), direct=()):
    count = len(operands)
    held = sum(array.size * array.dtype.itemsize for array in operands[: count - remote])
    for shape, dtype in list(out_shapes) + list(scratch):
        held += math.prod(shape) * jnp.dtype(dtype).itemsize
    spaces = [pltpu.VMEM] * (count - remote) + [pltpu.HBM] * remote
    operands = [
        pltpu.with_memory_space_constraint(array, space) if space is pltpu.HBM else array
        for array, space in zip(operands, spaces)
    ]
    return pl.pallas_call(
        kernel,
        out_shape=tuple(
            pltpu.HBM(shape, dtype) if at in far else jax.ShapeDtypeStruct(shape, dtype)
            for at, (shape, dtype) in enumerate(out_shapes)
        ),
        in_specs=[pl.BlockSpec(memory_space=space) for space in spaces],
        out_specs=tuple(
            pl.BlockSpec(memory_space=pltpu.HBM if at in direct else pltpu.VMEM)
            for at in range(len(out_shapes))
        ),
        scratch_shapes=[pltpu.VMEM(shape, dtype) for shape, dtype in scratch]
        + [pltpu.SemaphoreType.DMA((semaphores,))] * min(semaphores, 1),
        compiler_params=pltpu.CompilerParams(vmem_limit_bytes=held + 12 * 1024 * 1024),
    )(*operands)


def slot_tokens(members_ref, counts_ref, devices, group):
    rounds, groups = counts_ref.shape
    per_device = groups // devices
    rows = pl.ds(group, rounds * devices, stride=per_device)
    parts = [members_ref[half, rows, :] for half in range(members_ref.shape[0])]
    listed = jnp.concatenate(parts, axis=1)
    diagonal = iota((devices, groups), 1) == iota((devices, groups), 0) * per_device + group
    limits = [
        jnp.sum(
            jnp.where(diagonal, counts_ref[r : r + 1, :].astype(f32), 0.0), axis=1, keepdims=True
        )
        for r in range(rounds)
    ]
    limit = jnp.concatenate(limits, axis=0)
    return jnp.where(float_iota(listed.shape, 1) < limit, listed, -1)


def rank_slots(rounds, devices, token_count, tokens_ref, key_ref, value_ref):
    per_device, _, cap = key_ref.shape
    start = lax.axis_index("seq") * token_count
    before = earlier(cap)
    carry = jnp.zeros((rounds * devices, 1), f32)
    for group in range(per_device):
        local = tokens_ref[group] - start
        owned = (local >= 0) & (local < token_count)
        rank = dot_nn(one_hot(owned), before) + carry
        carry = carry + jnp.sum(jnp.where(owned, 1.0, 0.0), axis=1, keepdims=True)
        key_ref[group] = jnp.where(owned, rank, -1.0)
        value_ref[group] = jnp.where(owned, local + 1, 0).astype(f32)


def pick_rows(rounds, devices, bound, block, token_count, key_ref, value_ref):
    per_device, _, cap = key_ref.shape
    column = float_iota((bound, cap), 0)
    picks = []
    for r in range(rounds):
        row = r * devices + block
        total = jnp.zeros((bound, cap), f32)
        for group in range(per_device):
            ranks = key_ref[group, pl.ds(row, 1), :]
            values = value_ref[group, pl.ds(row, 1), :]
            total = total + jnp.where(ranks == column, values, 0.0)
        index = jnp.sum(total, axis=1, keepdims=True) - 1.0
        picks.append(short_hot(index, (bound, token_count), 1))
    return jnp.concatenate(picks, axis=0)


def pack_kernel(
    rounds,
    devices,
    bound,
    counts_hbm,
    members_hbm,
    q_hbm,
    v_hbm,
    g_hbm,
    send_hbm,
    tokens_ref,
    packed_ref,
    key_ref,
    value_ref,
    counts_ref,
    members_ref,
    rows_ref,
    sems,
):
    token_count, size = q_hbm.shape
    halves = members_ref.shape[0]
    copies = [pltpu.make_async_copy(counts_hbm, counts_ref, sems.at[halves + 3])]
    for half in range(halves):
        source = members_hbm.at[:, pl.ds(half * lane, lane)]
        copies.append(pltpu.make_async_copy(source, members_ref.at[half], sems.at[half]))
    for at, source in enumerate((q_hbm, v_hbm, g_hbm)):
        target = rows_ref.at[:, pl.ds(at * size, size)]
        copies.append(pltpu.make_async_copy(source, target, sems.at[halves + at]))
    for copy in copies:
        copy.start()
    for copy in copies[: halves + 1]:
        copy.wait()
    for group in range(tokens_ref.shape[0]):
        tokens_ref[group] = slot_tokens(members_ref, counts_ref, devices, group)
    rank_slots(rounds, devices, token_count, tokens_ref, key_ref, value_ref)
    parts = 4
    step = devices // parts
    sends = []
    for part in range(parts):
        picks = [
            pick_rows(
                rounds, devices, bound, block_of(device, devices), token_count, key_ref, value_ref
            )
            for device in range(part * step, (part + 1) * step)
        ]
        if part == 0:
            for copy in copies[halves + 1 :]:
                copy.wait()
        span = pl.ds(part * step * rounds * bound, step * rounds * bound)
        packed_ref[span, :] = dot_nn(jnp.concatenate(picks, axis=0), rows_ref[...]).astype(bf16)
        copy = pltpu.make_async_copy(
            packed_ref.at[span, :], send_hbm.at[span, :], sems.at[halves + 4 + part]
        )
        copy.start()
        sends.append(copy)
    for copy in sends:
        copy.wait()


def index_kernel(
    rounds,
    devices,
    bound,
    token_count,
    tokens_ref,
    place_ref,
    fill_ref,
    spread_t_ref,
    partner_ref,
    low_ref,
    home_ref,
    table_ref,
    pick_ref,
    key_ref,
    value_ref,
):
    per_device, _, cap = tokens_ref.shape
    me = block_of(lax.axis_index("seq"), devices)
    after = lax.rem(me + 1, devices)
    buffer_rows = devices * bound
    before = earlier(cap)
    source_start = iota((devices, cap), 0) * token_count
    source_place = float_iota((devices, cap), 0) * bound + 1.0
    place_column = float_iota((buffer_rows, cap), 0)
    for r in range(rounds):
        carry = jnp.zeros((devices, 1), f32)
        for group in range(per_device):
            tokens = tokens_ref[group, pl.ds(r * devices + me, 1), :]
            owned = (tokens >= source_start) & (tokens < source_start + token_count)
            rank = dot_nn(one_hot(owned), before) + carry
            carry = carry + jnp.sum(jnp.where(owned, 1.0, 0.0), axis=1, keepdims=True)
            place = (
                jnp.sum(jnp.where(owned, rank + source_place, 0.0), axis=0, keepdims=True) - 1.0
            )
            span = pl.ds(group * cap, cap)
            spread_t_ref[r, :, span] = one_hot(place == place_column)
            place_ref[pl.ds(r * per_device + group, 1), :] = place

    behind = lax.rem(me + devices - 1, devices)
    for r in range(rounds):
        for at in range(per_device + 2):
            block = behind if at == 0 else after if at > per_device else me
            group = (at - 1) % per_device
            tokens = tokens_ref[group, pl.ds(r * devices + block, 1), :]
            fill = jnp.sum(jnp.where(tokens >= 0, 1.0, 0.0), axis=1, keepdims=True)
            row = r * (per_device + 2) + at
            fill_ref[row : row + 1, :] = jnp.broadcast_to(fill, (1, cap))

    high_count = devices * token_count // lane
    high_start = iota((high_count, cap), 0) * lane
    low_index = iota((lane, cap), 0)
    slot = float_iota((high_count, cap), 1)

    def split(tokens):
        high = (tokens >= high_start) & (tokens < high_start + lane)
        low = jnp.bitwise_and(tokens, lane - 1) == low_index
        return high, low

    for r in range(rounds):

        def one_block(block, total):
            device = device_of(block, devices)
            for group in range(per_device):
                tokens = tokens_ref[group, pl.ds(r * devices + block, 1), :]
                high, low = split(tokens)
                group_index = (device * per_device + group).astype(f32)
                sides = jnp.concatenate(
                    [
                        jnp.where(high, group_index, 0.0).astype(bf16),
                        jnp.where(high, slot, 0.0).astype(bf16),
                    ],
                    axis=0,
                )
                total = total + dot_nt(sides, one_hot(low))
            return total

        total = lax.fori_loop(
            0, devices, one_block, jnp.zeros((2 * high_count, lane), f32), unroll=2
        )
        table_ref[r] = total.astype(bf16)

    halves = cap // lane
    kept = table_kept(per_device * halves)
    row_column = float_iota((devices * kept, cap), 0)
    for r in range(rounds):
        other = 1 - r
        for group in range(per_device + 1):
            if group < per_device:
                tokens = tokens_ref[group, pl.ds(r * devices + me, 1), :]
            else:
                tokens = tokens_ref[0, pl.ds(r * devices + after, 1), :]
            high, low = split(tokens)
            high_hot = one_hot(high)
            found = []
            for part in range(2):
                table = table_ref[other, part * high_count : (part + 1) * high_count, :]
                picked = dot_tn(table, high_hot)
                found.append(jnp.sum(jnp.where(low, picked, 0.0), axis=0, keepdims=True))
            group_index, position = found
            device = jnp.floor((group_index + 0.5) * (1.0 / per_device))
            half = jnp.floor((position + 0.5) * (1.0 / lane))
            row = device * kept + (group_index - device * per_device) * halves + half
            span = pl.ds(group * cap, cap)
            partner_ref[r, :, span] = one_hot(row == row_column)
            low_ref[pl.ds(r * (per_device + 1) + group, 1), :] = position - half * lane

    rank_slots(rounds, devices, token_count, tokens_ref, key_ref, value_ref)

    def pick_device(device, carried):
        at = pl.multiple_of(device * rounds * bound, rounds * bound)
        pick_ref[pl.ds(at, rounds * bound), :] = pick_rows(
            rounds, devices, bound, block_of(device, devices), token_count, key_ref, value_ref
        )
        return carried

    lax.fori_loop(0, devices, pick_device, 0, unroll=2)
    home_ref[...] = jnp.transpose(pick_ref[...])


def table_kept(count):
    return (count + 7) // 8 * 8


def spread_of(place_ref, r, group, rounds, buffer_rows):
    row = r * (place_ref.shape[0] // rounds) + group
    cap = place_ref.shape[1]
    return short_hot(place_ref[row : row + 1, :], (buffer_rows, cap), 0)


def received_rows(got_ref, r, rounds):
    devices, span, width = got_ref.shape
    bound = span // rounds
    return got_ref[:, r * bound : (r + 1) * bound, :].reshape(devices * bound, width)


def ends_kernel(rounds, got_ref, place_ref, last_ref, first_ref):
    size = got_ref.shape[2] // 3
    per_device = place_ref.shape[0] // rounds
    for r in range(rounds):
        received = received_rows(got_ref, r, rounds)
        spread = spread_of(place_ref, r, per_device - 1, rounds, received.shape[0])
        last_ref[r] = dot_tn(spread, received[:, : 2 * size]).astype(bf16)
        spread = spread_of(place_ref, r, 0, rounds, received.shape[0])
        wanted = jnp.concatenate([received[:, :size], received[:, 2 * size :]], axis=1)
        first_ref[r] = dot_tn(spread, wanted).astype(bf16)


def inverse_norm(rows):
    wide = rows.astype(f32)
    return lax.rsqrt(jnp.sum(wide * wide, axis=1, keepdims=True) + norm_eps)


def unit_rows(rows):
    return (rows.astype(f32) * inverse_norm(rows)).astype(bf16)


def fill_row(fill_ref, r, at, rounds):
    row = r * (fill_ref.shape[0] // rounds) + at
    return fill_ref[row : row + 1, :]


def scored(unit, queries, fill, own):
    cap = queries.shape[0]
    key = float_iota((cap, cap), 0)
    allowed = key < fill
    if own:
        allowed = allowed & (key != float_iota((cap, cap), 1))
    return jnp.where(allowed, dot_nt(unit, queries), masked_score)


def normalised(scores, inners):
    highest = jnp.maximum(
        jnp.max(scores[0], axis=0, keepdims=True), jnp.max(scores[1], axis=0, keepdims=True)
    )
    exps = [jnp.exp(score - highest) for score in scores]
    total = jnp.sum(exps[0], axis=0, keepdims=True) + jnp.sum(exps[1], axis=0, keepdims=True)
    inverse = 1.0 / total
    probs = [part * inverse for part in exps]
    dots = jnp.sum(probs[0] * inners[0], axis=0, keepdims=True) + jnp.sum(
        probs[1] * inners[1], axis=0, keepdims=True
    )
    return highest + jnp.log(total), dots, [prob.astype(bf16) for prob in probs]


def forward_inner_kernel(
    rounds,
    fill_ref,
    got_ref,
    place_ref,
    last_ref,
    first_ref,
    rows_ref,
    units_ref,
    prob_ref,
    inner_ref,
    first_score_ref,
    first_inner_ref,
    sums_ref,
):
    cap = prob_ref.shape[3]
    per_device = rows_ref.shape[1]
    size = rows_ref.shape[3] // 3
    for r in range(rounds):
        received = received_rows(got_ref, r, rounds)
        for group in range(per_device):
            spread = spread_of(place_ref, r, group, rounds, received.shape[0])
            if group == 0:
                values = dot_tn(spread, received[:, size : 2 * size]).astype(bf16)
                rows_ref[r, group, :, :size] = first_ref[r, :, :size]
                rows_ref[r, group, :, size : 2 * size] = values
                rows_ref[r, group, :, 2 * size :] = first_ref[r, :, size:]
            elif group < per_device - 1:
                rows_ref[r, group] = dot_tn(spread, received).astype(bf16)
            else:
                rows_ref[r, group, :, : 2 * size] = last_ref[r]
                cots = dot_tn(spread, received[:, 2 * size :]).astype(bf16)
                rows_ref[r, group, :, 2 * size :] = cots
        units = [unit_rows(rows_ref[r, group, :, :size]) for group in range(per_device)]
        for group in range(per_device):
            units_ref[r, group] = units[group]
        for group in range(per_device):
            queries = rows_ref[r, group, :, :size]
            cot = rows_ref[r, group, :, 2 * size :]
            values = rows_ref[r, group, :, size : 2 * size]
            score_now = scored(
                units[group], queries, fill_row(fill_ref, r, group + 1, rounds), True
            )
            inner_now = dot_nt(values, cot)
            if group == 0:
                first_score_ref[r] = score_now
                first_inner_ref[r] = inner_now
                continue
            values = rows_ref[r, group - 1, :, size : 2 * size]
            inner_before = dot_nt(values, cot)
            score_before = scored(
                units[group - 1], queries, fill_row(fill_ref, r, group, rounds), False
            )
            inners = [inner_before, inner_now]
            log_total, dots, probs = normalised([score_before, score_now], inners)
            for side in range(2):
                span = slice(side * cap, (side + 1) * cap)
                prob_ref[r, group - 1, span, :] = probs[side]
                inner_ref[r, group - 1, span, :] = inners[side].astype(bf16)
            row = r * per_device + group
            sums_ref[row : row + 1, :] = log_total
            row = (rounds + r) * per_device + group
            sums_ref[row : row + 1, :] = dots


def forward_first_kernel(
    rounds,
    devices,
    fill_ref,
    rows_ref,
    behind_ref,
    score_ref,
    inner_now_ref,
    inner_sums_ref,
    unit_ref,
    prob_ref,
    inner_ref,
    sums_ref,
    send_ref,
    block_ref,
):
    cap = prob_ref.shape[2]
    per_device = rows_ref.shape[1]
    size = rows_ref.shape[3] // 3
    sums_ref[...] = inner_sums_ref[...]
    for r in range(rounds):
        behind_unit = unit_rows(behind_ref[r, :, :size])
        unit_ref[r] = behind_unit
        queries = rows_ref[r, 0, :, :size]
        cot = rows_ref[r, 0, :, 2 * size :]
        score_before = scored(behind_unit, queries, fill_row(fill_ref, r, 0, rounds), False)
        inners = [dot_nt(behind_ref[r, :, size:], cot), inner_now_ref[r]]
        log_total, dots, probs = normalised([score_before, score_ref[r]], inners)
        for side in range(2):
            span = slice(side * cap, (side + 1) * cap)
            prob_ref[r, span, :] = probs[side]
            inner_ref[r, span, :] = inners[side].astype(bf16)
        row = r * per_device
        sums_ref[row : row + 1, :] = log_total
        row = (rounds + r) * per_device
        sums_ref[row : row + 1, :] = dots
    halves = cap // lane
    count = per_device * halves
    for r in range(rounds):
        for kind in range(2):
            for group in range(per_device):
                row = (kind * rounds + r) * per_device + group
                for half in range(halves):
                    at = (2 * r + kind) * count + group * halves + half
                    block_ref[at : at + 1, :] = sums_ref[
                        row : row + 1, half * lane : (half + 1) * lane
                    ]
    block = block_ref[...]
    for device in range(devices):
        send_ref[device] = block


def key_grad(rows, unit_grad):
    wide = rows.astype(f32)
    inverse = inverse_norm(rows)
    along = jnp.sum(wide * unit_grad, axis=1, keepdims=True)
    return inverse * unit_grad - wide * (inverse * inverse * inverse * along)


def three_parts(values):
    high = values.astype(bf16)
    rest = values - high.astype(f32)
    middle = rest.astype(bf16)
    return high, middle, (rest - middle.astype(f32)).astype(bf16)


def backward_kernel(
    rounds,
    devices,
    bound,
    fill_ref,
    everyone_ref,
    partner_ref,
    low_ref,
    sums_ref,
    rows_ref,
    ahead_ref,
    units_ref,
    behind_unit_ref,
    first_prob_ref,
    first_inner_ref,
    prob_ref,
    inner_ref,
    spread_t_ref,
    send_ref,
    grads_ref,
):
    cap = rows_ref.shape[2]
    per_device = rows_ref.shape[1]
    size = rows_ref.shape[3] // 3
    me = block_of(lax.axis_index("seq"), devices)
    ahead_device = device_of(lax.rem(me + 1, devices), devices)
    halves = cap // lane
    count = per_device * halves
    kept = table_kept(count)
    low_column = float_iota((lane, cap), 0)
    slot = float_iota((1, cap), 1)

    def sums_of_all(r, kind):
        start = (2 * r + kind) * count
        held = min(start, everyone_ref.shape[1] - kept)
        rows = everyone_ref[:, held : held + kept, :]
        if start > held:
            rows = jnp.concatenate(
                [rows[:, start - held :], jnp.zeros((devices, start - held, lane), f32)], axis=1
            )
        return jnp.transpose(rows.reshape(devices * kept, lane))

    def ahead_sums(r, kind):
        start = (2 * r + kind) * count
        rows = [everyone_ref[ahead_device, start + h : start + h + 1, :] for h in range(halves)]
        return jnp.concatenate(rows, axis=1)

    for r in range(rounds):
        logs = three_parts(sums_of_all(1 - r, 0))
        dots = three_parts(sums_of_all(1 - r, 1))
        upright = jnp.concatenate(logs + dots[:2], axis=0)
        picked = dot_nn(upright, partner_ref[r])
        picked_log = picked[:lane] + (picked[lane : 2 * lane] + picked[2 * lane : 3 * lane])
        picked_dot = picked[3 * lane : 4 * lane] + picked[4 * lane :]
        scales = []
        for group in range(per_device + 1):
            at = r * (per_device + 1) + group
            here = low_ref[at : at + 1, :] == low_column
            span = slice(group * cap, (group + 1) * cap)
            other_log = jnp.sum(jnp.where(here, picked_log[:, span], 0.0), axis=0, keepdims=True)
            other_dot = jnp.sum(jnp.where(here, picked_dot[:, span], 0.0), axis=0, keepdims=True)
            if group < per_device:
                row = r * per_device + group
                own_log = sums_ref[row : row + 1, :]
                own_dot = sums_ref[rounds * per_device + row : rounds * per_device + row + 1, :]
            else:
                own_log = ahead_sums(r, 0)
                own_dot = ahead_sums(r, 1)
                ahead_log = own_log
            weight = 1.0 / (1.0 + jnp.exp(other_log - own_log))
            other_weight = 1.0 / (1.0 + jnp.exp(own_log - other_log))
            mixture = weight * own_dot + other_weight * other_dot
            valid = slot < fill_row(fill_ref, r, group + 1, rounds)
            scales.append((jnp.where(valid, weight, 0.0), jnp.where(valid, mixture, 0.0)))

        def score_grads(prob, inner, scale):
            weighted = prob.astype(f32) * scale[0]
            score_grad = (weighted * (inner.astype(f32) - scale[1])).astype(bf16)
            return weighted.astype(bf16), score_grad

        query_grad = None
        unit_grad = None
        value_grad = None
        for group in range(per_device + 1):
            if group < per_device:
                queries = rows_ref[r, group][:, :size]
                cot = rows_ref[r, group][:, 2 * size :]
            else:
                queries = ahead_ref[r][:, :size]
                cot = ahead_ref[r][:, size:]
            if group == 0:
                probs = [first_prob_ref[r, :cap, :], first_prob_ref[r, cap:, :]]
                inners = [first_inner_ref[r, :cap, :], first_inner_ref[r, cap:, :]]
            elif group < per_device:
                probs = [prob_ref[r, group - 1, :cap, :], prob_ref[r, group - 1, cap:, :]]
                inners = [inner_ref[r, group - 1, :cap, :], inner_ref[r, group - 1, cap:, :]]
            else:
                fill = fill_row(fill_ref, r, per_device, rounds)
                score = scored(units_ref[r, per_device - 1], queries, fill, False)
                probs = [jnp.exp(score - ahead_log)]
                inners = [dot_nt(rows_ref[r, per_device - 1][:, size : 2 * size], cot)]
            weighted, score_grad = score_grads(probs[0], inners[0], scales[group])
            if group > 0:
                unit_grad = unit_grad + dot_nn(score_grad, queries)
                value_grad = value_grad + dot_nn(weighted, cot)
                key_part = key_grad(rows_ref[r, group - 1][:, :size], unit_grad)
                span = slice((group - 1) * cap, group * cap)
                grads_ref[span, :size] = (query_grad + key_part).astype(bf16)
                grads_ref[span, size:] = value_grad.astype(bf16)
            if group < per_device:
                unit_before = behind_unit_ref[r] if group == 0 else units_ref[r, group - 1]
                query_grad = dot_tn(score_grad, unit_before)
                weighted, score_grad = score_grads(probs[1], inners[1], scales[group])
                query_grad = query_grad + dot_tn(score_grad, units_ref[r, group])
                unit_grad = dot_nn(score_grad, queries)
                value_grad = dot_nn(weighted, cot)
        packed = dot_nn(spread_t_ref[r], grads_ref[...]).astype(bf16)
        send_ref[:, r * bound : (r + 1) * bound, :] = packed.reshape(devices, bound, 2 * size)


def home_kernel(home_ref, got_ref, qk_ref, value_ref):
    size = qk_ref.shape[1]
    total = dot_nn(home_ref[...], got_ref[...])
    qk_ref[...] = total[:, :size].astype(bf16)
    value_ref[...] = total[:, size:].astype(bf16)


def exchange(array):
    return lax.all_to_all(array, "seq", split_axis=0, concat_axis=0, tiled=True)


def shifted(array, by):
    devices = lax.axis_size("seq")
    order = [device_of(block, devices) for block in range(devices)]
    return lax.ppermute(array, "seq", [(order[i], order[(i + by) % devices]) for i in range(devices)])


def head_backward(qk, values, cot, members, counts):
    devices = lax.axis_size("seq")
    token_count, size = qk.shape
    rounds, groups, cap = members.shape
    per_device = groups // devices
    slots = per_device * cap
    bound = 2 * token_count // devices
    span = rounds * bound
    buffer_rows = devices * bound
    sum_rows = 2 * rounds * per_device
    listed = members.reshape(rounds * groups, cap)
    keys = [((per_device, rounds * devices, cap), f32)] * 2
    pick = ((devices * span, token_count), bf16)
    send, tokens = call(
        functools.partial(pack_kernel, rounds, devices, bound),
        [((devices * span, 3 * size), bf16), (keys[0][0], jnp.int32)],
        [counts, listed, qk, values, cot],
        [((devices * span, 3 * size), bf16)]
        + keys
        + [
            (counts.shape, jnp.int32),
            ((cap // lane, rounds * groups, lane), jnp.int32),
            ((token_count, 3 * size), bf16),
        ],
        remote=5,
        semaphores=cap // lane + 8,
        far=(0,),
        direct=(0,),
    )
    got = exchange(send).reshape(devices, span, 3 * size)
    place, fill, spread_t, partner, low, home_pick = call(
        functools.partial(index_kernel, rounds, devices, bound, token_count),
        [
            ((rounds * per_device, cap), f32),
            ((rounds * (per_device + 2), cap), f32),
            ((rounds, buffer_rows, slots), bf16),
            ((rounds, devices * table_kept(slots // lane), slots + cap), bf16),
            ((rounds * (per_device + 1), cap), f32),
            ((token_count, devices * span), bf16),
        ],
        [tokens],
        [((rounds, 2 * devices * token_count // lane, lane), bf16), pick] + keys,
        far=(2, 3, 5),
    )
    last, first = call(
        functools.partial(ends_kernel, rounds),
        [((rounds, cap, 2 * size), bf16)] * 2,
        [got, place],
    )
    behind = shifted(last, 1)
    ahead = shifted(first, -1)
    square = (rounds, cap, cap)
    rows, units, prob, inner, first_score, first_inner_now, inner_sums = call(
        functools.partial(forward_inner_kernel, rounds),
        [
            ((rounds, per_device, cap, 3 * size), bf16),
            ((rounds, per_device, cap, size), bf16),
            ((rounds, per_device - 1, 2 * cap, cap), bf16),
            ((rounds, per_device - 1, 2 * cap, cap), bf16),
            (square, f32),
            (square, f32),
            ((sum_rows, cap), f32),
        ],
        [fill, got, place, last, first],
    )
    behind_unit, first_prob, first_inner, sums, sums_send = call(
        functools.partial(forward_first_kernel, rounds, devices),
        [
            ((rounds, cap, size), bf16),
            ((rounds, 2 * cap, cap), bf16),
            ((rounds, 2 * cap, cap), bf16),
            ((sum_rows, cap), f32),
            ((devices, sum_rows * cap // lane, lane), f32),
        ],
        [fill, rows, behind, first_score, first_inner_now, inner_sums],
        [((sum_rows * cap // lane, lane), f32)],
    )
    sums_send, ahead = lax.optimization_barrier((sums_send, ahead))
    everyone = exchange(sums_send)
    (grads_send,) = call(
        functools.partial(backward_kernel, rounds, devices, bound),
        [((devices, span, 2 * size), bf16)],
        [
            fill,
            everyone,
            partner,
            low,
            sums,
            rows,
            ahead,
            units,
            behind_unit,
            first_prob,
            first_inner,
            prob,
            inner,
            spread_t,
        ],
        [((slots, 2 * size), bf16)],
    )
    home = exchange(grads_send.reshape(devices * span, 2 * size))
    return call(
        home_kernel,
        [((token_count, size), bf16), ((token_count, size), bf16)],
        [home_pick, home],
    )


def on_device(qk, values, grad_out, members, counts):
    grad_qk, grad_v = head_backward(qk[0], values[0], grad_out[0], members[0], counts[0])
    return (grad_qk[None], grad_v[None])


def solution(mesh):
    in_specs = (
        P("head", "seq", None),
        P("head", "seq", None),
        P("head", "seq", None),
        P("head", None, None, None),
        P("head", None, None),
    )
    out_specs = (P("head", "seq", None), P("head", "seq", None))
    return jax.shard_map(
        on_device, mesh=mesh, in_specs=in_specs, out_specs=out_specs, check_vma=False
    )
```

```python
import functools
import math

import jax
import jax.numpy as jnp
from jax import lax
from jax.experimental import pallas as pl
from jax.experimental.pallas import tpu as pltpu
from jax.sharding import PartitionSpec as P

masked_score = -1e30
norm_eps = 1e-06
lane = 128
f32 = jnp.float32
bf16 = jnp.bfloat16


def iota(shape, axis):
    return lax.broadcasted_iota(jnp.int32, shape, axis)


def float_iota(shape, axis):
    return iota(shape, axis).astype(f32)


def dot_nn(a, b):
    return lax.dot_general(a, b, (((1,), (0,)), ((), ())), preferred_element_type=f32)


def dot_nt(a, b):
    return lax.dot_general(a, b, (((1,), (1,)), ((), ())), preferred_element_type=f32)


def dot_tn(a, b):
    return lax.dot_general(a, b, (((0,), (0,)), ((), ())), preferred_element_type=f32)


def one_hot(condition):
    return jnp.where(condition, 1.0, 0.0).astype(bf16)


def short_hot(index, shape, axis):
    place = iota(shape, axis).astype(jnp.int16)
    short = jnp.broadcast_to(index.astype(jnp.int32), shape).astype(jnp.int16)
    return jnp.where(short == place, jnp.ones(shape, bf16), jnp.zeros(shape, bf16))


def block_of(device, devices):
    if devices % 4:
        return device
    depth = devices // 4
    level, column = device // 4, device % 4
    turn = column ^ (column >> 1)
    step = level + (turn % 2) * (depth - 1 - 2 * level)
    return turn * depth + step


def device_of(block, devices):
    if devices % 4:
        return block
    depth = devices // 4
    turn, step = block // depth, block % depth
    level = step + (turn % 2) * (depth - 1 - 2 * step)
    return level * 4 + (turn ^ (turn >> 1))


def earlier(size):
    return one_hot(iota((size, size), 0) < iota((size, size), 1))


def call(kernel, out_shapes, operands, scratch=(), remote=0, semaphores=0, far=(), direct=()):
    count = len(operands)
    held = sum(array.size * array.dtype.itemsize for array in operands[: count - remote])
    for shape, dtype in list(out_shapes) + list(scratch):
        held += math.prod(shape) * jnp.dtype(dtype).itemsize
    spaces = [pltpu.VMEM] * (count - remote) + [pltpu.HBM] * remote
    operands = [
        pltpu.with_memory_space_constraint(array, space) if space is pltpu.HBM else array
        for array, space in zip(operands, spaces)
    ]
    return pl.pallas_call(
        kernel,
        out_shape=tuple(
            pltpu.HBM(shape, dtype) if at in far else jax.ShapeDtypeStruct(shape, dtype)
            for at, (shape, dtype) in enumerate(out_shapes)
        ),
        in_specs=[pl.BlockSpec(memory_space=space) for space in spaces],
        out_specs=tuple(
            pl.BlockSpec(memory_space=pltpu.HBM if at in direct else pltpu.VMEM)
            for at in range(len(out_shapes))
        ),
        scratch_shapes=[pltpu.VMEM(shape, dtype) for shape, dtype in scratch]
        + [pltpu.SemaphoreType.DMA((semaphores,))] * min(semaphores, 1),
        compiler_params=pltpu.CompilerParams(vmem_limit_bytes=held + 12 * 1024 * 1024),
    )(*operands)


def slot_tokens(members_ref, counts_ref, devices, group):
    rounds, groups = counts_ref.shape
    per_device = groups // devices
    rows = pl.ds(group, rounds * devices, stride=per_device)
    parts = [members_ref[half, rows, :] for half in range(members_ref.shape[0])]
    listed = jnp.concatenate(parts, axis=1)
    diagonal = iota((devices, groups), 1) == iota((devices, groups), 0) * per_device + group
    limits = [
        jnp.sum(
            jnp.where(diagonal, counts_ref[r : r + 1, :].astype(f32), 0.0), axis=1, keepdims=True
        )
        for r in range(rounds)
    ]
    limit = jnp.concatenate(limits, axis=0)
    return jnp.where(float_iota(listed.shape, 1) < limit, listed, -1)


def rank_slots(rounds, devices, token_count, tokens_ref, key_ref, value_ref):
    per_device, _, cap = key_ref.shape
    start = lax.axis_index("seq") * token_count
    before = earlier(cap)
    carry = jnp.zeros((rounds * devices, 1), f32)
    for group in range(per_device):
        local = tokens_ref[group] - start
        owned = (local >= 0) & (local < token_count)
        rank = dot_nn(one_hot(owned), before) + carry
        carry = carry + jnp.sum(jnp.where(owned, 1.0, 0.0), axis=1, keepdims=True)
        key_ref[group] = jnp.where(owned, rank, -1.0)
        value_ref[group] = jnp.where(owned, local + 1, 0).astype(f32)


def pick_rows(rounds, devices, bound, block, token_count, key_ref, value_ref):
    per_device, _, cap = key_ref.shape
    column = float_iota((bound, cap), 0)
    picks = []
    for r in range(rounds):
        row = r * devices + block
        total = jnp.zeros((bound, cap), f32)
        for group in range(per_device):
            ranks = key_ref[group, pl.ds(row, 1), :]
            values = value_ref[group, pl.ds(row, 1), :]
            total = total + jnp.where(ranks == column, values, 0.0)
        index = jnp.sum(total, axis=1, keepdims=True) - 1.0
        picks.append(short_hot(index, (bound, token_count), 1))
    return jnp.concatenate(picks, axis=0)


def pack_kernel(
    rounds,
    devices,
    bound,
    counts_hbm,
    members_hbm,
    q_hbm,
    v_hbm,
    g_hbm,
    send_hbm,
    tokens_ref,
    packed_ref,
    key_ref,
    value_ref,
    counts_ref,
    members_ref,
    rows_ref,
    sems,
):
    token_count, size = q_hbm.shape
    halves = members_ref.shape[0]
    copies = [pltpu.make_async_copy(counts_hbm, counts_ref, sems.at[halves + 3])]
    for half in range(halves):
        source = members_hbm.at[:, pl.ds(half * lane, lane)]
        copies.append(pltpu.make_async_copy(source, members_ref.at[half], sems.at[half]))
    for at, source in enumerate((q_hbm, v_hbm, g_hbm)):
        target = rows_ref.at[:, pl.ds(at * size, size)]
        copies.append(pltpu.make_async_copy(source, target, sems.at[halves + at]))
    for copy in copies:
        copy.start()
    for copy in copies[: halves + 1]:
        copy.wait()
    for group in range(tokens_ref.shape[0]):
        tokens_ref[group] = slot_tokens(members_ref, counts_ref, devices, group)
    rank_slots(rounds, devices, token_count, tokens_ref, key_ref, value_ref)
    parts = 4
    step = devices // parts
    sends = []
    for part in range(parts):
        picks = [
            pick_rows(
                rounds, devices, bound, block_of(device, devices), token_count, key_ref, value_ref
            )
            for device in range(part * step, (part + 1) * step)
        ]
        if part == 0:
            for copy in copies[halves + 1 :]:
                copy.wait()
        span = pl.ds(part * step * rounds * bound, step * rounds * bound)
        packed_ref[span, :] = dot_nn(jnp.concatenate(picks, axis=0), rows_ref[...]).astype(bf16)
        copy = pltpu.make_async_copy(
            packed_ref.at[span, :], send_hbm.at[span, :], sems.at[halves + 4 + part]
        )
        copy.start()
        sends.append(copy)
    for copy in sends:
        copy.wait()


def index_kernel(
    rounds,
    devices,
    bound,
    token_count,
    tokens_ref,
    place_ref,
    fill_ref,
    spread_t_ref,
    partner_ref,
    low_ref,
    home_ref,
    table_ref,
    pick_ref,
    key_ref,
    value_ref,
):
    per_device, _, cap = tokens_ref.shape
    me = block_of(lax.axis_index("seq"), devices)
    after = lax.rem(me + 1, devices)
    buffer_rows = devices * bound
    before = earlier(cap)
    source_start = iota((devices, cap), 0) * token_count
    source_place = float_iota((devices, cap), 0) * bound + 1.0
    place_column = float_iota((buffer_rows, cap), 0)
    for r in range(rounds):
        carry = jnp.zeros((devices, 1), f32)
        for group in range(per_device):
            tokens = tokens_ref[group, pl.ds(r * devices + me, 1), :]
            owned = (tokens >= source_start) & (tokens < source_start + token_count)
            rank = dot_nn(one_hot(owned), before) + carry
            carry = carry + jnp.sum(jnp.where(owned, 1.0, 0.0), axis=1, keepdims=True)
            place = (
                jnp.sum(jnp.where(owned, rank + source_place, 0.0), axis=0, keepdims=True) - 1.0
            )
            span = pl.ds(group * cap, cap)
            spread_t_ref[r, :, span] = one_hot(place == place_column)
            place_ref[pl.ds(r * per_device + group, 1), :] = place

    behind = lax.rem(me + devices - 1, devices)
    for r in range(rounds):
        for at in range(per_device + 2):
            block = behind if at == 0 else after if at > per_device else me
            group = (at - 1) % per_device
            tokens = tokens_ref[group, pl.ds(r * devices + block, 1), :]
            fill = jnp.sum(jnp.where(tokens >= 0, 1.0, 0.0), axis=1, keepdims=True)
            row = r * (per_device + 2) + at
            fill_ref[row : row + 1, :] = jnp.broadcast_to(fill, (1, cap))

    high_count = devices * token_count // lane
    high_start = iota((high_count, cap), 0) * lane
    low_index = iota((lane, cap), 0)
    slot = float_iota((high_count, cap), 1)

    def split(tokens):
        high = (tokens >= high_start) & (tokens < high_start + lane)
        low = jnp.bitwise_and(tokens, lane - 1) == low_index
        return high, low

    for r in range(rounds):

        def one_block(block, total):
            device = device_of(block, devices)
            for group in range(per_device):
                tokens = tokens_ref[group, pl.ds(r * devices + block, 1), :]
                high, low = split(tokens)
                group_index = (device * per_device + group).astype(f32)
                sides = jnp.concatenate(
                    [
                        jnp.where(high, group_index, 0.0).astype(bf16),
                        jnp.where(high, slot, 0.0).astype(bf16),
                    ],
                    axis=0,
                )
                total = total + dot_nt(sides, one_hot(low))
            return total

        total = lax.fori_loop(
            0, devices, one_block, jnp.zeros((2 * high_count, lane), f32), unroll=2
        )
        table_ref[r] = total.astype(bf16)

    halves = cap // lane
    kept = table_kept(per_device * halves)
    row_column = float_iota((devices * kept, cap), 0)
    for r in range(rounds):
        other = 1 - r
        for group in range(per_device + 1):
            if group < per_device:
                tokens = tokens_ref[group, pl.ds(r * devices + me, 1), :]
            else:
                tokens = tokens_ref[0, pl.ds(r * devices + after, 1), :]
            high, low = split(tokens)
            high_hot = one_hot(high)
            found = []
            for part in range(2):
                table = table_ref[other, part * high_count : (part + 1) * high_count, :]
                picked = dot_tn(table, high_hot)
                found.append(jnp.sum(jnp.where(low, picked, 0.0), axis=0, keepdims=True))
            group_index, position = found
            device = jnp.floor((group_index + 0.5) * (1.0 / per_device))
            half = jnp.floor((position + 0.5) * (1.0 / lane))
            row = device * kept + (group_index - device * per_device) * halves + half
            span = pl.ds(group * cap, cap)
            partner_ref[r, :, span] = one_hot(row == row_column)
            low_ref[pl.ds(r * (per_device + 1) + group, 1), :] = position - half * lane

    rank_slots(rounds, devices, token_count, tokens_ref, key_ref, value_ref)

    def pick_device(device, carried):
        at = pl.multiple_of(device * rounds * bound, rounds * bound)
        pick_ref[pl.ds(at, rounds * bound), :] = pick_rows(
            rounds, devices, bound, block_of(device, devices), token_count, key_ref, value_ref
        )
        return carried

    lax.fori_loop(0, devices, pick_device, 0, unroll=2)
    home_ref[...] = jnp.transpose(pick_ref[...])


def table_kept(count):
    return (count + 7) // 8 * 8


def spread_of(place_ref, r, group, rounds, buffer_rows):
    row = r * (place_ref.shape[0] // rounds) + group
    cap = place_ref.shape[1]
    return short_hot(place_ref[row : row + 1, :], (buffer_rows, cap), 0)


def received_rows(got_ref, r, rounds):
    devices, span, width = got_ref.shape
    bound = span // rounds
    return got_ref[:, r * bound : (r + 1) * bound, :].reshape(devices * bound, width)


def ends_kernel(rounds, got_ref, place_ref, last_ref, first_ref):
    size = got_ref.shape[2] // 3
    per_device = place_ref.shape[0] // rounds
    for r in range(rounds):
        received = received_rows(got_ref, r, rounds)
        spread = spread_of(place_ref, r, per_device - 1, rounds, received.shape[0])
        last_ref[r] = dot_tn(spread, received[:, : 2 * size]).astype(bf16)
        spread = spread_of(place_ref, r, 0, rounds, received.shape[0])
        wanted = jnp.concatenate([received[:, :size], received[:, 2 * size :]], axis=1)
        first_ref[r] = dot_tn(spread, wanted).astype(bf16)


def inverse_norm(rows):
    wide = rows.astype(f32)
    return lax.rsqrt(jnp.sum(wide * wide, axis=1, keepdims=True) + norm_eps)


def unit_rows(rows):
    return (rows.astype(f32) * inverse_norm(rows)).astype(bf16)


def fill_row(fill_ref, r, at, rounds):
    row = r * (fill_ref.shape[0] // rounds) + at
    return fill_ref[row : row + 1, :]


def scored(unit, queries, fill, own):
    cap = queries.shape[0]
    key = float_iota((cap, cap), 0)
    allowed = key < fill
    if own:
        allowed = allowed & (key != float_iota((cap, cap), 1))
    return jnp.where(allowed, dot_nt(unit, queries), masked_score)


def normalised(scores, inners):
    highest = jnp.maximum(
        jnp.max(scores[0], axis=0, keepdims=True), jnp.max(scores[1], axis=0, keepdims=True)
    )
    exps = [jnp.exp(score - highest) for score in scores]
    total = jnp.sum(exps[0], axis=0, keepdims=True) + jnp.sum(exps[1], axis=0, keepdims=True)
    inverse = 1.0 / total
    probs = [part * inverse for part in exps]
    dots = jnp.sum(probs[0] * inners[0], axis=0, keepdims=True) + jnp.sum(
        probs[1] * inners[1], axis=0, keepdims=True
    )
    return highest + jnp.log(total), dots, [prob.astype(bf16) for prob in probs]


def forward_inner_kernel(
    rounds,
    fill_ref,
    got_ref,
    place_ref,
    last_ref,
    first_ref,
    rows_ref,
    units_ref,
    prob_ref,
    inner_ref,
    first_score_ref,
    first_inner_ref,
    sums_ref,
):
    cap = prob_ref.shape[3]
    per_device = rows_ref.shape[1]
    size = rows_ref.shape[3] // 3
    for r in range(rounds):
        received = received_rows(got_ref, r, rounds)
        for group in range(per_device):
            spread = spread_of(place_ref, r, group, rounds, received.shape[0])
            if group == 0:
                values = dot_tn(spread, received[:, size : 2 * size]).astype(bf16)
                rows_ref[r, group, :, :size] = first_ref[r, :, :size]
                rows_ref[r, group, :, size : 2 * size] = values
                rows_ref[r, group, :, 2 * size :] = first_ref[r, :, size:]
            elif group < per_device - 1:
                rows_ref[r, group] = dot_tn(spread, received).astype(bf16)
            else:
                rows_ref[r, group, :, : 2 * size] = last_ref[r]
                cots = dot_tn(spread, received[:, 2 * size :]).astype(bf16)
                rows_ref[r, group, :, 2 * size :] = cots
        units = [unit_rows(rows_ref[r, group, :, :size]) for group in range(per_device)]
        for group in range(per_device):
            units_ref[r, group] = units[group]
        for group in range(per_device):
            queries = rows_ref[r, group, :, :size]
            cot = rows_ref[r, group, :, 2 * size :]
            values = rows_ref[r, group, :, size : 2 * size]
            score_now = scored(
                units[group], queries, fill_row(fill_ref, r, group + 1, rounds), True
            )
            inner_now = dot_nt(values, cot)
            if group == 0:
                first_score_ref[r] = score_now
                first_inner_ref[r] = inner_now
                continue
            values = rows_ref[r, group - 1, :, size : 2 * size]
            inner_before = dot_nt(values, cot)
            score_before = scored(
                units[group - 1], queries, fill_row(fill_ref, r, group, rounds), False
            )
            inners = [inner_before, inner_now]
            log_total, dots, probs = normalised([score_before, score_now], inners)
            for side in range(2):
                span = slice(side * cap, (side + 1) * cap)
                prob_ref[r, group - 1, span, :] = probs[side]
                inner_ref[r, group - 1, span, :] = inners[side].astype(bf16)
            row = r * per_device + group
            sums_ref[row : row + 1, :] = log_total
            row = (rounds + r) * per_device + group
            sums_ref[row : row + 1, :] = dots


def forward_first_kernel(
    rounds,
    devices,
    fill_ref,
    rows_ref,
    behind_ref,
    score_ref,
    inner_now_ref,
    inner_sums_ref,
    unit_ref,
    prob_ref,
    inner_ref,
    sums_ref,
    send_ref,
    block_ref,
):
    cap = prob_ref.shape[2]
    per_device = rows_ref.shape[1]
    size = rows_ref.shape[3] // 3
    sums_ref[...] = inner_sums_ref[...]
    for r in range(rounds):
        behind_unit = unit_rows(behind_ref[r, :, :size])
        unit_ref[r] = behind_unit
        queries = rows_ref[r, 0, :, :size]
        cot = rows_ref[r, 0, :, 2 * size :]
        score_before = scored(behind_unit, queries, fill_row(fill_ref, r, 0, rounds), False)
        inners = [dot_nt(behind_ref[r, :, size:], cot), inner_now_ref[r]]
        log_total, dots, probs = normalised([score_before, score_ref[r]], inners)
        for side in range(2):
            span = slice(side * cap, (side + 1) * cap)
            prob_ref[r, span, :] = probs[side]
            inner_ref[r, span, :] = inners[side].astype(bf16)
        row = r * per_device
        sums_ref[row : row + 1, :] = log_total
        row = (rounds + r) * per_device
        sums_ref[row : row + 1, :] = dots
    halves = cap // lane
    count = per_device * halves
    for r in range(rounds):
        for kind in range(2):
            for group in range(per_device):
                row = (kind * rounds + r) * per_device + group
                for half in range(halves):
                    at = (2 * r + kind) * count + group * halves + half
                    block_ref[at : at + 1, :] = sums_ref[
                        row : row + 1, half * lane : (half + 1) * lane
                    ]
    block = block_ref[...]
    for device in range(devices):
        send_ref[device] = block


def key_grad(rows, unit_grad):
    wide = rows.astype(f32)
    inverse = inverse_norm(rows)
    along = jnp.sum(wide * unit_grad, axis=1, keepdims=True)
    return inverse * unit_grad - wide * (inverse * inverse * inverse * along)


def three_parts(values):
    high = values.astype(bf16)
    rest = values - high.astype(f32)
    middle = rest.astype(bf16)
    return high, middle, (rest - middle.astype(f32)).astype(bf16)


def backward_kernel(
    rounds,
    devices,
    bound,
    fill_ref,
    everyone_ref,
    partner_ref,
    low_ref,
    sums_ref,
    rows_ref,
    ahead_ref,
    units_ref,
    behind_unit_ref,
    first_prob_ref,
    first_inner_ref,
    prob_ref,
    inner_ref,
    spread_t_ref,
    send_ref,
    grads_ref,
):
    cap = rows_ref.shape[2]
    per_device = rows_ref.shape[1]
    size = rows_ref.shape[3] // 3
    me = block_of(lax.axis_index("seq"), devices)
    ahead_device = device_of(lax.rem(me + 1, devices), devices)
    halves = cap // lane
    count = per_device * halves
    kept = table_kept(count)
    low_column = float_iota((lane, cap), 0)
    slot = float_iota((1, cap), 1)

    def sums_of_all(r, kind):
        start = (2 * r + kind) * count
        held = min(start, everyone_ref.shape[1] - kept)
        rows = everyone_ref[:, held : held + kept, :]
        if start > held:
            rows = jnp.concatenate(
                [rows[:, start - held :], jnp.zeros((devices, start - held, lane), f32)], axis=1
            )
        return jnp.transpose(rows.reshape(devices * kept, lane))

    def ahead_sums(r, kind):
        start = (2 * r + kind) * count
        rows = [everyone_ref[ahead_device, start + h : start + h + 1, :] for h in range(halves)]
        return jnp.concatenate(rows, axis=1)

    def scales_of(r):
        logs = three_parts(sums_of_all(1 - r, 0))
        dots = three_parts(sums_of_all(1 - r, 1))
        upright = jnp.concatenate(logs + dots[:2], axis=0)
        picked = dot_nn(upright, partner_ref[r])
        picked_log = picked[:lane] + (picked[lane : 2 * lane] + picked[2 * lane : 3 * lane])
        picked_dot = picked[3 * lane : 4 * lane] + picked[4 * lane :]
        scales = []
        for group in range(per_device + 1):
            at = r * (per_device + 1) + group
            here = low_ref[at : at + 1, :] == low_column
            span = slice(group * cap, (group + 1) * cap)
            other_log = jnp.sum(jnp.where(here, picked_log[:, span], 0.0), axis=0, keepdims=True)
            other_dot = jnp.sum(jnp.where(here, picked_dot[:, span], 0.0), axis=0, keepdims=True)
            if group < per_device:
                row = r * per_device + group
                own_log = sums_ref[row : row + 1, :]
                own_dot = sums_ref[rounds * per_device + row : rounds * per_device + row + 1, :]
            else:
                own_log = ahead_sums(r, 0)
                own_dot = ahead_sums(r, 1)
            weight = 1.0 / (1.0 + jnp.exp(other_log - own_log))
            other_weight = 1.0 / (1.0 + jnp.exp(own_log - other_log))
            mixture = weight * own_dot + other_weight * other_dot
            valid = slot < fill_row(fill_ref, r, group + 1, rounds)
            scales.append((jnp.where(valid, weight, 0.0), jnp.where(valid, mixture, 0.0)))
        return scales

    def score_grads(prob, inner, scale):
        weighted = prob.astype(f32) * scale[0]
        score_grad = (weighted * (inner.astype(f32) - scale[1])).astype(bf16)
        return weighted.astype(bf16), score_grad

    scales = [scales_of(r) for r in range(rounds)]
    carried = [None] * rounds
    for group in range(per_device + 1):
        for r in range(rounds):
            if group < per_device:
                queries = rows_ref[r, group, :, :size]
                cot = rows_ref[r, group, :, 2 * size :]
            else:
                queries = ahead_ref[r, :, :size]
                cot = ahead_ref[r, :, size:]
            if group == 0:
                probs = [first_prob_ref[r, :cap, :], first_prob_ref[r, cap:, :]]
                inners = [first_inner_ref[r, :cap, :], first_inner_ref[r, cap:, :]]
            elif group < per_device:
                probs = [prob_ref[r, group - 1, :cap, :], prob_ref[r, group - 1, cap:, :]]
                inners = [inner_ref[r, group - 1, :cap, :], inner_ref[r, group - 1, cap:, :]]
            else:
                fill = fill_row(fill_ref, r, per_device, rounds)
                score = scored(units_ref[r, per_device - 1], queries, fill, False)
                probs = [jnp.exp(score - ahead_sums(r, 0))]
                inners = [dot_nt(rows_ref[r, per_device - 1, :, size : 2 * size], cot)]
            scale = scales[r][group]
            weighted, score_grad = score_grads(probs[0], inners[0], scale)
            if group > 0:
                query_grad, unit_grad, value_grad = carried[r]
                unit_grad = unit_grad + dot_nn(score_grad, queries)
                value_grad = value_grad + dot_nn(weighted, cot)
                key_part = key_grad(rows_ref[r, group - 1, :, :size], unit_grad)
                span = slice((group - 1) * cap, group * cap)
                grads_ref[r, span, :size] = (query_grad + key_part).astype(bf16)
                grads_ref[r, span, size:] = value_grad.astype(bf16)
            if group < per_device:
                unit_before = behind_unit_ref[r] if group == 0 else units_ref[r, group - 1]
                query_grad = dot_tn(score_grad, unit_before)
                weighted, score_grad = score_grads(probs[1], inners[1], scale)
                query_grad = query_grad + dot_tn(score_grad, units_ref[r, group])
                unit_grad = dot_nn(score_grad, queries)
                carried[r] = (query_grad, unit_grad, dot_nn(weighted, cot))
    for r in range(rounds):
        packed = dot_nn(spread_t_ref[r], grads_ref[r]).astype(bf16)
        send_ref[:, r * bound : (r + 1) * bound, :] = packed.reshape(devices, bound, 2 * size)


def home_kernel(home_ref, got_ref, qk_ref, value_ref):
    size = qk_ref.shape[1]
    total = dot_nn(home_ref[...], got_ref[...])
    qk_ref[...] = total[:, :size].astype(bf16)
    value_ref[...] = total[:, size:].astype(bf16)


def exchange(array):
    return lax.all_to_all(array, "seq", split_axis=0, concat_axis=0, tiled=True)


def shifted(array, by):
    devices = lax.axis_size("seq")
    order = [device_of(block, devices) for block in range(devices)]
    return lax.ppermute(array, "seq", [(order[i], order[(i + by) % devices]) for i in range(devices)])


def head_backward(qk, values, cot, members, counts):
    devices = lax.axis_size("seq")
    token_count, size = qk.shape
    rounds, groups, cap = members.shape
    per_device = groups // devices
    slots = per_device * cap
    bound = 2 * token_count // devices
    span = rounds * bound
    buffer_rows = devices * bound
    sum_rows = 2 * rounds * per_device
    listed = members.reshape(rounds * groups, cap)
    keys = [((per_device, rounds * devices, cap), f32)] * 2
    pick = ((devices * span, token_count), bf16)
    send, tokens = call(
        functools.partial(pack_kernel, rounds, devices, bound),
        [((devices * span, 3 * size), bf16), (keys[0][0], jnp.int32)],
        [counts, listed, qk, values, cot],
        [((devices * span, 3 * size), bf16)]
        + keys
        + [
            (counts.shape, jnp.int32),
            ((cap // lane, rounds * groups, lane), jnp.int32),
            ((token_count, 3 * size), bf16),
        ],
        remote=5,
        semaphores=cap // lane + 8,
        far=(0,),
        direct=(0,),
    )
    got = exchange(send).reshape(devices, span, 3 * size)
    place, fill, spread_t, partner, low, home_pick = call(
        functools.partial(index_kernel, rounds, devices, bound, token_count),
        [
            ((rounds * per_device, cap), f32),
            ((rounds * (per_device + 2), cap), f32),
            ((rounds, buffer_rows, slots), bf16),
            ((rounds, devices * table_kept(slots // lane), slots + cap), bf16),
            ((rounds * (per_device + 1), cap), f32),
            ((token_count, devices * span), bf16),
        ],
        [tokens],
        [((rounds, 2 * devices * token_count // lane, lane), bf16), pick] + keys,
        far=(2, 3, 5),
    )
    last, first = call(
        functools.partial(ends_kernel, rounds),
        [((rounds, cap, 2 * size), bf16)] * 2,
        [got, place],
    )
    behind = shifted(last, 1)
    ahead = shifted(first, -1)
    square = (rounds, cap, cap)
    rows, units, prob, inner, first_score, first_inner_now, inner_sums = call(
        functools.partial(forward_inner_kernel, rounds),
        [
            ((rounds, per_device, cap, 3 * size), bf16),
            ((rounds, per_device, cap, size), bf16),
            ((rounds, per_device - 1, 2 * cap, cap), bf16),
            ((rounds, per_device - 1, 2 * cap, cap), bf16),
            (square, f32),
            (square, f32),
            ((sum_rows, cap), f32),
        ],
        [fill, got, place, last, first],
    )
    behind_unit, first_prob, first_inner, sums, sums_send = call(
        functools.partial(forward_first_kernel, rounds, devices),
        [
            ((rounds, cap, size), bf16),
            ((rounds, 2 * cap, cap), bf16),
            ((rounds, 2 * cap, cap), bf16),
            ((sum_rows, cap), f32),
            ((devices, sum_rows * cap // lane, lane), f32),
        ],
        [fill, rows, behind, first_score, first_inner_now, inner_sums],
        [((sum_rows * cap // lane, lane), f32)],
    )
    sums_send, ahead = lax.optimization_barrier((sums_send, ahead))
    everyone = exchange(sums_send)
    (grads_send,) = call(
        functools.partial(backward_kernel, rounds, devices, bound),
        [((devices, span, 2 * size), bf16)],
        [
            fill,
            everyone,
            partner,
            low,
            sums,
            rows,
            ahead,
            units,
            behind_unit,
            first_prob,
            first_inner,
            prob,
            inner,
            spread_t,
        ],
        [((rounds, slots, 2 * size), bf16)],
    )
    home = exchange(grads_send.reshape(devices * span, 2 * size))
    return call(
        home_kernel,
        [((token_count, size), bf16), ((token_count, size), bf16)],
        [home_pick, home],
    )


def on_device(qk, values, grad_out, members, counts):
    grad_qk, grad_v = head_backward(qk[0], values[0], grad_out[0], members[0], counts[0])
    return (grad_qk[None], grad_v[None])


def solution(mesh):
    in_specs = (
        P("head", "seq", None),
        P("head", "seq", None),
        P("head", "seq", None),
        P("head", None, None, None),
        P("head", None, None),
    )
    out_specs = (P("head", "seq", None), P("head", "seq", None))
    return jax.shard_map(
        on_device, mesh=mesh, in_specs=in_specs, out_specs=out_specs, check_vma=False
    )
```

```python
import functools
import math

import jax
import jax.numpy as jnp
from jax import lax
from jax.experimental import pallas as pl
from jax.experimental.pallas import tpu as pltpu
from jax.sharding import PartitionSpec as P

masked_score = -1e30
norm_eps = 1e-06
lane = 128
f32 = jnp.float32
bf16 = jnp.bfloat16


def iota(shape, axis):
    return lax.broadcasted_iota(jnp.int32, shape, axis)


def float_iota(shape, axis):
    return iota(shape, axis).astype(f32)


def dot_nn(a, b):
    return lax.dot_general(a, b, (((1,), (0,)), ((), ())), preferred_element_type=f32)


def dot_nt(a, b):
    return lax.dot_general(a, b, (((1,), (1,)), ((), ())), preferred_element_type=f32)


def dot_tn(a, b):
    return lax.dot_general(a, b, (((0,), (0,)), ((), ())), preferred_element_type=f32)


def one_hot(condition):
    return jnp.where(condition, 1.0, 0.0).astype(bf16)


def short_hot(index, shape, axis):
    place = iota(shape, axis).astype(jnp.int16)
    short = jnp.broadcast_to(index.astype(jnp.int32), shape).astype(jnp.int16)
    return jnp.where(short == place, jnp.ones(shape, bf16), jnp.zeros(shape, bf16))


def block_of(device, devices):
    if devices % 4:
        return device
    depth = devices // 4
    level, column = device // 4, device % 4
    turn = column ^ (column >> 1)
    step = level + (turn % 2) * (depth - 1 - 2 * level)
    return turn * depth + step


def device_of(block, devices):
    if devices % 4:
        return block
    depth = devices // 4
    turn, step = block // depth, block % depth
    level = step + (turn % 2) * (depth - 1 - 2 * step)
    return level * 4 + (turn ^ (turn >> 1))


def earlier(size):
    return one_hot(iota((size, size), 0) < iota((size, size), 1))


def call(
    kernel,
    out_shapes,
    operands,
    scratch=(),
    remote=0,
    semaphores=0,
    far=(),
    direct=(),
    cost=0,
):
    count = len(operands)
    held = sum(array.size * array.dtype.itemsize for array in operands[: count - remote])
    for shape, dtype in list(out_shapes) + list(scratch):
        held += math.prod(shape) * jnp.dtype(dtype).itemsize
    spaces = [pltpu.VMEM] * (count - remote) + [pltpu.HBM] * remote
    operands = [
        pltpu.with_memory_space_constraint(array, space) if space is pltpu.HBM else array
        for array, space in zip(operands, spaces)
    ]
    return pl.pallas_call(
        kernel,
        out_shape=tuple(
            pltpu.HBM(shape, dtype) if at in far else jax.ShapeDtypeStruct(shape, dtype)
            for at, (shape, dtype) in enumerate(out_shapes)
        ),
        in_specs=[pl.BlockSpec(memory_space=space) for space in spaces],
        out_specs=tuple(
            pl.BlockSpec(memory_space=pltpu.HBM if at in direct else pltpu.VMEM)
            for at in range(len(out_shapes))
        ),
        scratch_shapes=[pltpu.VMEM(shape, dtype) for shape, dtype in scratch]
        + [pltpu.SemaphoreType.DMA((semaphores,))] * min(semaphores, 1),
        cost_estimate=pl.CostEstimate(flops=cost, transcendentals=0, bytes_accessed=0),
        compiler_params=pltpu.CompilerParams(vmem_limit_bytes=held + 12 * 1024 * 1024),
    )(*operands)


def slot_tokens(members_ref, counts_ref, devices, group):
    rounds, groups = counts_ref.shape
    per_device = groups // devices
    rows = pl.ds(group, rounds * devices, stride=per_device)
    parts = [members_ref[half, rows, :] for half in range(members_ref.shape[0])]
    listed = jnp.concatenate(parts, axis=1)
    diagonal = iota((devices, groups), 1) == iota((devices, groups), 0) * per_device + group
    limits = [
        jnp.sum(
            jnp.where(diagonal, counts_ref[r : r + 1, :].astype(f32), 0.0), axis=1, keepdims=True
        )
        for r in range(rounds)
    ]
    limit = jnp.concatenate(limits, axis=0)
    return jnp.where(float_iota(listed.shape, 1) < limit, listed, -1)


def rank_slots(rounds, devices, token_count, source, tokens_ref, key_ref, value_ref):
    per_device, _, cap = key_ref.shape
    start = source * token_count
    before = earlier(cap)
    carry = jnp.zeros((rounds * devices, 1), f32)
    for group in range(per_device):
        local = tokens_ref[group] - start
        owned = (local >= 0) & (local < token_count)
        rank = dot_nn(one_hot(owned), before) + carry
        carry = carry + jnp.sum(jnp.where(owned, 1.0, 0.0), axis=1, keepdims=True)
        key_ref[group] = jnp.where(owned, rank, -1.0)
        value_ref[group] = jnp.where(owned, local + 1, 0).astype(f32)


def pick_rows(rounds, devices, bound, block, token_count, key_ref, value_ref):
    per_device, _, cap = key_ref.shape
    column = float_iota((bound, cap), 0)
    picks = []
    for r in range(rounds):
        row = r * devices + block
        total = jnp.zeros((bound, cap), f32)
        for group in range(per_device):
            ranks = key_ref[group, pl.ds(row, 1), :]
            values = value_ref[group, pl.ds(row, 1), :]
            total = total + jnp.where(ranks == column, values, 0.0)
        index = jnp.sum(total, axis=1, keepdims=True) - 1.0
        picks.append(short_hot(index, (bound, token_count), 1))
    return jnp.concatenate(picks, axis=0)


def pack_kernel(
    rounds,
    devices,
    bound,
    counts_hbm,
    members_hbm,
    q_hbm,
    v_hbm,
    g_hbm,
    send_hbm,
    tokens_ref,
    packed_ref,
    key_ref,
    value_ref,
    counts_ref,
    members_ref,
    rows_ref,
    sems,
):
    token_count, size = q_hbm.shape
    halves = members_ref.shape[0]
    copies = [pltpu.make_async_copy(counts_hbm, counts_ref, sems.at[halves + 3])]
    for half in range(halves):
        source = members_hbm.at[:, pl.ds(half * lane, lane)]
        copies.append(pltpu.make_async_copy(source, members_ref.at[half], sems.at[half]))
    for at, source in enumerate((q_hbm, v_hbm, g_hbm)):
        target = rows_ref.at[:, pl.ds(at * size, size)]
        copies.append(pltpu.make_async_copy(source, target, sems.at[halves + at]))
    for copy in copies:
        copy.start()
    for copy in copies[: halves + 1]:
        copy.wait()
    for group in range(tokens_ref.shape[0]):
        tokens_ref[group] = slot_tokens(members_ref, counts_ref, devices, group)
    me = lax.axis_index("seq")
    rank_slots(rounds, devices, token_count, me, tokens_ref, key_ref, value_ref)
    half = devices // 2
    first = me // half * half
    parts = 4
    step = half // parts
    sends = []
    for part in range(parts):
        picks = [
            pick_rows(
                rounds,
                devices,
                bound,
                block_of(first + at, devices),
                token_count,
                key_ref,
                value_ref,
            )
            for at in range(part * step, (part + 1) * step)
        ]
        if part == 0:
            for copy in copies[halves + 1 :]:
                copy.wait()
        span = pl.ds(part * step * rounds * bound, step * rounds * bound)
        packed_ref[span, :] = dot_nn(jnp.concatenate(picks, axis=0), rows_ref[...]).astype(bf16)
        copy = pltpu.make_async_copy(
            packed_ref.at[span, :], send_hbm.at[span, :], sems.at[halves + 4 + part]
        )
        copy.start()
        sends.append(copy)
    for copy in sends:
        copy.wait()


def far_pick_kernel(rounds, devices, bound, token_count, tokens_ref, pick_ref, key_ref, value_ref):
    me = lax.axis_index("seq")
    half = devices // 2
    first = me // half * half
    source = lax.rem(me + half, devices)
    rank_slots(rounds, devices, token_count, source, tokens_ref, key_ref, value_ref)
    size = rounds * bound
    for at in range(half):
        block = block_of(first + jnp.bitwise_xor(me - first, at), devices)
        pick_ref[at * size : (at + 1) * size, :] = pick_rows(
            rounds, devices, bound, block, token_count, key_ref, value_ref
        )


def far_pack_kernel(pick_ref, q_ref, v_ref, g_ref, *send_refs):
    rows = jnp.concatenate([q_ref[...], v_ref[...], g_ref[...]], axis=1)
    span = send_refs[0].shape[0]
    parts = 4
    count = len(send_refs) // parts
    for part in range(parts):
        first = part * count
        packed = dot_nn(pick_ref[pl.ds(first * span, count * span), :], rows).astype(bf16)
        for at in range(count):
            send_refs[first + at][...] = packed[at * span : (at + 1) * span]


def place_kernel(rounds, devices, bound, token_count, tokens_ref, place_ref, home_place_ref, fill_ref):
    per_device, _, cap = tokens_ref.shape
    seat = lax.axis_index("seq")
    me = block_of(seat, devices)
    half = devices // 2
    before = earlier(cap)
    source = iota((devices, cap), 0)
    source_start = source * token_count
    home_place = source.astype(f32) * bound + 1.0
    first = seat // half * half
    near = (source >= first) & (source < first + half)
    crossed = half + jnp.bitwise_xor(source % half, seat - first)
    source_place = jnp.where(near, source - first, crossed).astype(f32) * bound + 1.0
    for r in range(rounds):
        carry = jnp.zeros((devices, 1), f32)
        for group in range(per_device):
            tokens = tokens_ref[group, pl.ds(r * devices + me, 1), :]
            owned = (tokens >= source_start) & (tokens < source_start + token_count)
            rank = dot_nn(one_hot(owned), before) + carry
            carry = carry + jnp.sum(jnp.where(owned, 1.0, 0.0), axis=1, keepdims=True)
            for target, base in ((place_ref, source_place), (home_place_ref, home_place)):
                place = jnp.sum(jnp.where(owned, rank + base, 0.0), axis=0, keepdims=True) - 1.0
                row = r * per_device + group
                target[row : row + 1, :] = place
    after = lax.rem(me + 1, devices)
    behind = lax.rem(me + devices - 1, devices)
    for r in range(rounds):
        for at in range(per_device + 2):
            block = behind if at == 0 else after if at > per_device else me
            group = (at - 1) % per_device
            tokens = tokens_ref[group, pl.ds(r * devices + block, 1), :]
            fill = jnp.sum(jnp.where(tokens >= 0, 1.0, 0.0), axis=1, keepdims=True)
            row = r * (per_device + 2) + at
            fill_ref[row : row + 1, :] = jnp.broadcast_to(fill, (1, cap))


def index_kernel(
    rounds,
    devices,
    bound,
    token_count,
    tokens_ref,
    partner_ref,
    low_ref,
    table_ref,
):
    per_device, _, cap = tokens_ref.shape
    me = block_of(lax.axis_index("seq"), devices)
    after = lax.rem(me + 1, devices)
    high_count = devices * token_count // lane
    high_start = iota((high_count, cap), 0) * lane
    low_index = iota((lane, cap), 0)
    slot = float_iota((high_count, cap), 1)

    def split(tokens):
        high = (tokens >= high_start) & (tokens < high_start + lane)
        low = jnp.bitwise_and(tokens, lane - 1) == low_index
        return high, low

    for r in range(rounds):

        def one_block(block, total):
            device = device_of(block, devices)
            for group in range(per_device):
                tokens = tokens_ref[group, pl.ds(r * devices + block, 1), :]
                high, low = split(tokens)
                group_index = (device * per_device + group).astype(f32)
                sides = jnp.concatenate(
                    [
                        jnp.where(high, group_index, 0.0).astype(bf16),
                        jnp.where(high, slot, 0.0).astype(bf16),
                    ],
                    axis=0,
                )
                total = total + dot_nt(sides, one_hot(low))
            return total

        total = lax.fori_loop(
            0, devices, one_block, jnp.zeros((2 * high_count, lane), f32), unroll=2
        )
        table_ref[r] = total.astype(bf16)

    halves = cap // lane
    kept = table_kept(per_device * halves)
    row_column = float_iota((devices * kept, cap), 0)
    for r in range(rounds):
        other = 1 - r
        for group in range(per_device + 1):
            if group < per_device:
                tokens = tokens_ref[group, pl.ds(r * devices + me, 1), :]
            else:
                tokens = tokens_ref[0, pl.ds(r * devices + after, 1), :]
            high, low = split(tokens)
            high_hot = one_hot(high)
            found = []
            for part in range(2):
                table = table_ref[other, part * high_count : (part + 1) * high_count, :]
                picked = dot_tn(table, high_hot)
                found.append(jnp.sum(jnp.where(low, picked, 0.0), axis=0, keepdims=True))
            group_index, position = found
            device = jnp.floor((group_index + 0.5) * (1.0 / per_device))
            half = jnp.floor((position + 0.5) * (1.0 / lane))
            row = device * kept + (group_index - device * per_device) * halves + half
            span = pl.ds(group * cap, cap)
            partner_ref[r, :, span] = one_hot(row == row_column)
            low_ref[pl.ds(r * (per_device + 1) + group, 1), :] = position - half * lane


def return_index_kernel(
    rounds,
    devices,
    bound,
    token_count,
    tokens_ref,
    home_place_ref,
    spread_t_ref,
    home_ref,
    pick_ref,
    key_ref,
    value_ref,
):
    per_device, _, cap = tokens_ref.shape
    place_column = float_iota((devices * bound, cap), 0)
    for r in range(rounds):
        for group in range(per_device):
            row = r * per_device + group
            place = home_place_ref[row : row + 1, :]
            spread_t_ref[r, :, pl.ds(group * cap, cap)] = one_hot(place == place_column)
    seat = lax.axis_index("seq")
    rank_slots(rounds, devices, token_count, seat, tokens_ref, key_ref, value_ref)

    def pick_device(device, carried):
        at = pl.multiple_of(device * rounds * bound, rounds * bound)
        pick_ref[pl.ds(at, rounds * bound), :] = pick_rows(
            rounds, devices, bound, block_of(device, devices), token_count, key_ref, value_ref
        )
        return carried

    lax.fori_loop(0, devices, pick_device, 0, unroll=2)
    home_ref[...] = jnp.transpose(pick_ref[...])


def table_kept(count):
    return (count + 7) // 8 * 8


def spread_of(place_ref, r, group, rounds, buffer_rows):
    row = r * (place_ref.shape[0] // rounds) + group
    cap = place_ref.shape[1]
    return short_hot(place_ref[row : row + 1, :], (buffer_rows, cap), 0)


def received_rows(near_ref, far_refs, r, rounds):
    half, span, width = near_ref.shape
    bound = span // rounds
    rows = slice(r * bound, (r + 1) * bound)
    parts = [near_ref[:, rows, :].reshape(half * bound, width)]
    parts += [far_ref[rows, :] for far_ref in far_refs]
    return jnp.concatenate(parts, axis=0)


def ends_kernel(rounds, near_ref, place_ref, *refs):
    far_refs, (last_ref, first_ref) = refs[:-2], refs[-2:]
    size = near_ref.shape[2] // 3
    per_device = place_ref.shape[0] // rounds
    for r in range(rounds):
        received = received_rows(near_ref, far_refs, r, rounds)
        spread = spread_of(place_ref, r, per_device - 1, rounds, received.shape[0])
        last_ref[r] = dot_tn(spread, received[:, : 2 * size]).astype(bf16)
        spread = spread_of(place_ref, r, 0, rounds, received.shape[0])
        wanted = jnp.concatenate([received[:, :size], received[:, 2 * size :]], axis=1)
        first_ref[r] = dot_tn(spread, wanted).astype(bf16)


def inverse_norm(rows):
    wide = rows.astype(f32)
    return lax.rsqrt(jnp.sum(wide * wide, axis=1, keepdims=True) + norm_eps)


def unit_rows(rows):
    return (rows.astype(f32) * inverse_norm(rows)).astype(bf16)


def fill_row(fill_ref, r, at, rounds):
    row = r * (fill_ref.shape[0] // rounds) + at
    return fill_ref[row : row + 1, :]


def scored(unit, queries, fill, own):
    cap = queries.shape[0]
    key = float_iota((cap, cap), 0)
    allowed = key < fill
    if own:
        allowed = allowed & (key != float_iota((cap, cap), 1))
    return jnp.where(allowed, dot_nt(unit, queries), masked_score)


def normalised(scores, inners):
    highest = jnp.maximum(
        jnp.max(scores[0], axis=0, keepdims=True), jnp.max(scores[1], axis=0, keepdims=True)
    )
    exps = [jnp.exp(score - highest) for score in scores]
    total = jnp.sum(exps[0], axis=0, keepdims=True) + jnp.sum(exps[1], axis=0, keepdims=True)
    inverse = 1.0 / total
    probs = [part * inverse for part in exps]
    dots = jnp.sum(probs[0] * inners[0], axis=0, keepdims=True) + jnp.sum(
        probs[1] * inners[1], axis=0, keepdims=True
    )
    centred = [(inner - dots).astype(bf16) for inner in inners]
    return highest + jnp.log(total), dots, [prob.astype(bf16) for prob in probs], centred


def forward_inner_kernel(
    rounds,
    fill_ref,
    near_ref,
    place_ref,
    last_ref,
    first_ref,
    *refs,
):
    far_refs, refs = refs[:-7], refs[-7:]
    rows_ref, units_ref, prob_ref, inner_ref, first_score_ref, first_inner_ref, sums_ref = refs
    cap = prob_ref.shape[3]
    per_device = rows_ref.shape[1]
    size = rows_ref.shape[3] // 3
    for r in range(rounds):
        received = received_rows(near_ref, far_refs, r, rounds)
        for group in range(per_device):
            spread = spread_of(place_ref, r, group, rounds, received.shape[0])
            if group == 0:
                values = dot_tn(spread, received[:, size : 2 * size]).astype(bf16)
                rows_ref[r, group, :, :size] = first_ref[r, :, :size]
                rows_ref[r, group, :, size : 2 * size] = values
                rows_ref[r, group, :, 2 * size :] = first_ref[r, :, size:]
            elif group < per_device - 1:
                rows_ref[r, group] = dot_tn(spread, received).astype(bf16)
            else:
                rows_ref[r, group, :, : 2 * size] = last_ref[r]
                cots = dot_tn(spread, received[:, 2 * size :]).astype(bf16)
                rows_ref[r, group, :, 2 * size :] = cots
        units = [unit_rows(rows_ref[r, group, :, :size]) for group in range(per_device)]
        for group in range(per_device):
            units_ref[r, group] = units[group]
        for group in range(per_device):
            queries = rows_ref[r, group, :, :size]
            cot = rows_ref[r, group, :, 2 * size :]
            values = rows_ref[r, group, :, size : 2 * size]
            score_now = scored(
                units[group], queries, fill_row(fill_ref, r, group + 1, rounds), True
            )
            inner_now = dot_nt(values, cot)
            if group == 0:
                first_score_ref[r] = score_now
                first_inner_ref[r] = inner_now
                continue
            values = rows_ref[r, group - 1, :, size : 2 * size]
            inner_before = dot_nt(values, cot)
            score_before = scored(
                units[group - 1], queries, fill_row(fill_ref, r, group, rounds), False
            )
            inners = [inner_before, inner_now]
            log_total, dots, probs, centred = normalised([score_before, score_now], inners)
            for side in range(2):
                span = slice(side * cap, (side + 1) * cap)
                prob_ref[r, group - 1, span, :] = probs[side]
                inner_ref[r, group - 1, span, :] = centred[side]
            row = r * per_device + group
            sums_ref[row : row + 1, :] = log_total
            row = (rounds + r) * per_device + group
            sums_ref[row : row + 1, :] = dots


def forward_first_kernel(
    rounds,
    devices,
    fill_ref,
    rows_ref,
    behind_ref,
    score_ref,
    inner_now_ref,
    inner_sums_ref,
    unit_ref,
    prob_ref,
    inner_ref,
    sums_ref,
    send_ref,
    block_ref,
):
    cap = prob_ref.shape[2]
    per_device = rows_ref.shape[1]
    size = rows_ref.shape[3] // 3
    sums_ref[...] = inner_sums_ref[...]
    for r in range(rounds):
        behind_unit = unit_rows(behind_ref[r, :, :size])
        unit_ref[r] = behind_unit
        queries = rows_ref[r, 0, :, :size]
        cot = rows_ref[r, 0, :, 2 * size :]
        score_before = scored(behind_unit, queries, fill_row(fill_ref, r, 0, rounds), False)
        inners = [dot_nt(behind_ref[r, :, size:], cot), inner_now_ref[r]]
        log_total, dots, probs, centred = normalised([score_before, score_ref[r]], inners)
        for side in range(2):
            span = slice(side * cap, (side + 1) * cap)
            prob_ref[r, span, :] = probs[side]
            inner_ref[r, span, :] = centred[side]
        row = r * per_device
        sums_ref[row : row + 1, :] = log_total
        row = (rounds + r) * per_device
        sums_ref[row : row + 1, :] = dots
    halves = cap // lane
    count = per_device * halves
    for r in range(rounds):
        for kind in range(2):
            for group in range(per_device):
                row = (kind * rounds + r) * per_device + group
                for half in range(halves):
                    at = (2 * r + kind) * count + group * halves + half
                    block_ref[at : at + 1, :] = sums_ref[
                        row : row + 1, half * lane : (half + 1) * lane
                    ]
    block = block_ref[...]
    for device in range(devices):
        send_ref[device] = block


def key_grad(rows, unit_grad):
    wide = rows.astype(f32)
    inverse = inverse_norm(rows)
    along = jnp.sum(wide * unit_grad, axis=1, keepdims=True)
    return inverse * unit_grad - wide * (inverse * inverse * inverse * along)


def three_parts(values):
    high = values.astype(bf16)
    rest = values - high.astype(f32)
    middle = rest.astype(bf16)
    return high, middle, (rest - middle.astype(f32)).astype(bf16)


def backward_kernel(
    rounds,
    devices,
    bound,
    fill_ref,
    everyone_ref,
    partner_ref,
    low_ref,
    sums_ref,
    rows_ref,
    ahead_ref,
    units_ref,
    behind_unit_ref,
    first_prob_ref,
    first_inner_ref,
    prob_ref,
    inner_ref,
    spread_t_ref,
    send_ref,
    grads_ref,
):
    cap = rows_ref.shape[2]
    per_device = rows_ref.shape[1]
    size = rows_ref.shape[3] // 3
    me = block_of(lax.axis_index("seq"), devices)
    ahead_device = device_of(lax.rem(me + 1, devices), devices)
    halves = cap // lane
    count = per_device * halves
    kept = table_kept(count)
    low_column = float_iota((lane, cap), 0)
    slot = float_iota((1, cap), 1)

    def sums_of_all(r, kind):
        start = (2 * r + kind) * count
        held = min(start, everyone_ref.shape[1] - kept)
        rows = everyone_ref[:, held : held + kept, :]
        if start > held:
            rows = jnp.concatenate(
                [rows[:, start - held :], jnp.zeros((devices, start - held, lane), f32)], axis=1
            )
        return jnp.transpose(rows.reshape(devices * kept, lane))

    def ahead_sums(r, kind):
        start = (2 * r + kind) * count
        rows = [everyone_ref[ahead_device, start + h : start + h + 1, :] for h in range(halves)]
        return jnp.concatenate(rows, axis=1)

    def scales_of(r):
        logs = three_parts(sums_of_all(1 - r, 0))
        dots = three_parts(sums_of_all(1 - r, 1))
        upright = jnp.concatenate(logs + dots[:2], axis=0)
        picked = dot_nn(upright, partner_ref[r])
        picked_log = picked[:lane] + (picked[lane : 2 * lane] + picked[2 * lane : 3 * lane])
        picked_dot = picked[3 * lane : 4 * lane] + picked[4 * lane :]
        scales = []
        for group in range(per_device + 1):
            at = r * (per_device + 1) + group
            here = low_ref[at : at + 1, :] == low_column
            span = slice(group * cap, (group + 1) * cap)
            other_log = jnp.sum(jnp.where(here, picked_log[:, span], 0.0), axis=0, keepdims=True)
            other_dot = jnp.sum(jnp.where(here, picked_dot[:, span], 0.0), axis=0, keepdims=True)
            if group < per_device:
                row = r * per_device + group
                own_log = sums_ref[row : row + 1, :]
                own_dot = sums_ref[rounds * per_device + row : rounds * per_device + row + 1, :]
            else:
                own_log = ahead_sums(r, 0)
                own_dot = ahead_sums(r, 1)
            weight = 1.0 / (1.0 + jnp.exp(other_log - own_log))
            other_weight = 1.0 / (1.0 + jnp.exp(own_log - other_log))
            shift = other_weight * (own_dot - other_dot)
            valid = slot < fill_row(fill_ref, r, group + 1, rounds)
            scales.append((jnp.where(valid, weight, 0.0), jnp.where(valid, shift, 0.0)))
        return scales

    def score_grads(prob, inner, scale):
        weighted = prob.astype(f32) * scale[0]
        score_grad = (weighted * (inner.astype(f32) + scale[1])).astype(bf16)
        return weighted.astype(bf16), score_grad

    aheads = []
    for r in range(rounds):
        queries = ahead_ref[r, :, :size]
        cot = ahead_ref[r, :, size:]
        fill = fill_row(fill_ref, r, per_device, rounds)
        score = scored(units_ref[r, per_device - 1], queries, fill, False)
        inner = dot_nt(rows_ref[r, per_device - 1, :, size : 2 * size], cot)
        aheads.append(([jnp.exp(score - ahead_sums(r, 0))], [inner - ahead_sums(r, 1)]))
    scales = [scales_of(r) for r in range(rounds)]
    carried = [None] * rounds
    for group in range(per_device + 1):
        for r in range(rounds):
            if group < per_device:
                queries = rows_ref[r, group, :, :size]
                cot = rows_ref[r, group, :, 2 * size :]
            else:
                queries = ahead_ref[r, :, :size]
                cot = ahead_ref[r, :, size:]
            if group == 0:
                probs = [first_prob_ref[r, :cap, :], first_prob_ref[r, cap:, :]]
                inners = [first_inner_ref[r, :cap, :], first_inner_ref[r, cap:, :]]
            elif group < per_device:
                probs = [prob_ref[r, group - 1, :cap, :], prob_ref[r, group - 1, cap:, :]]
                inners = [inner_ref[r, group - 1, :cap, :], inner_ref[r, group - 1, cap:, :]]
            else:
                probs, inners = aheads[r]
            scale = scales[r][group]
            weighted, score_grad = score_grads(probs[0], inners[0], scale)
            if group > 0:
                query_grad, unit_grad, value_grad = carried[r]
                unit_grad = unit_grad + dot_nn(score_grad, queries)
                value_grad = value_grad + dot_nn(weighted, cot)
                key_part = key_grad(rows_ref[r, group - 1, :, :size], unit_grad)
                span = slice((group - 1) * cap, group * cap)
                grads_ref[r, span, :size] = (query_grad + key_part).astype(bf16)
                grads_ref[r, span, size:] = value_grad.astype(bf16)
            if group < per_device:
                unit_before = behind_unit_ref[r] if group == 0 else units_ref[r, group - 1]
                query_grad = dot_tn(score_grad, unit_before)
                weighted, score_grad = score_grads(probs[1], inners[1], scale)
                query_grad = query_grad + dot_tn(score_grad, units_ref[r, group])
                unit_grad = dot_nn(score_grad, queries)
                carried[r] = (query_grad, unit_grad, dot_nn(weighted, cot))
    for r in range(rounds):
        packed = dot_nn(spread_t_ref[r], grads_ref[r]).astype(bf16)
        send_ref[:, r * bound : (r + 1) * bound, :] = packed.reshape(devices, bound, 2 * size)


def home_kernel(home_ref, got_ref, qk_ref, value_ref):
    size = qk_ref.shape[1]
    total = dot_nn(home_ref[...], got_ref[...])
    qk_ref[...] = total[:, :size].astype(bf16)
    value_ref[...] = total[:, size:].astype(bf16)


def exchange_in_half(array):
    devices = lax.axis_size("seq")
    half = devices // 2
    halves = [list(range(half)), list(range(half, devices))]
    return lax.all_to_all(
        array, "seq", split_axis=0, concat_axis=0, tiled=True, axis_index_groups=halves
    )


def crossed(array, by):
    devices = lax.axis_size("seq")
    return lax.ppermute(array, "seq", [(i, i ^ by) for i in range(devices)])


def mirrored(array):
    devices = lax.axis_size("seq")
    half = devices // 2
    return lax.ppermute(array, "seq", [(i, (i + half) % devices) for i in range(devices)])


def exchange(array):
    return lax.all_to_all(array, "seq", split_axis=0, concat_axis=0, tiled=True)


def shifted(array, by):
    devices = lax.axis_size("seq")
    order = [device_of(block, devices) for block in range(devices)]
    return lax.ppermute(array, "seq", [(order[i], order[(i + by) % devices]) for i in range(devices)])


def head_backward(qk, values, cot, members, counts):
    devices = lax.axis_size("seq")
    token_count, size = qk.shape
    rounds, groups, cap = members.shape
    per_device = groups // devices
    slots = per_device * cap
    bound = 2 * token_count // devices
    span = rounds * bound
    buffer_rows = devices * bound
    sum_rows = 2 * rounds * per_device
    listed = members.reshape(rounds * groups, cap)
    keys = [((per_device, rounds * devices, cap), f32)] * 2
    pick = ((devices * span, token_count), bf16)
    half = devices // 2
    far_rows = [mirrored(rows) for rows in (qk, values, cot)]
    near_send, tokens = call(
        functools.partial(pack_kernel, rounds, devices, bound),
        [((half * span, 3 * size), bf16), (keys[0][0], jnp.int32)],
        [counts, listed, qk, values, cot],
        [((half * span, 3 * size), bf16)]
        + keys
        + [
            (counts.shape, jnp.int32),
            ((cap // lane, rounds * groups, lane), jnp.int32),
            ((token_count, 3 * size), bf16),
        ],
        remote=5,
        semaphores=cap // lane + 8,
        far=(0,),
        direct=(0,),
    )
    near = exchange_in_half(near_send).reshape(half, span, 3 * size)
    (far_pick,) = call(
        functools.partial(far_pick_kernel, rounds, devices, bound, token_count),
        [((half * span, token_count), bf16)],
        [tokens],
        keys,
    )
    place, home_place, fill = call(
        functools.partial(place_kernel, rounds, devices, bound, token_count),
        [
            ((rounds * per_device, cap), f32),
            ((rounds * per_device, cap), f32),
            ((rounds * (per_device + 2), cap), f32),
        ],
        [tokens],
    )
    partner, low = call(
        functools.partial(index_kernel, rounds, devices, bound, token_count),
        [
            ((rounds, devices * table_kept(slots // lane), slots + cap), bf16),
            ((rounds * (per_device + 1), cap), f32),
        ],
        [tokens],
        [((rounds, 2 * devices * token_count // lane, lane), bf16)],
        far=(0,),
    )
    far_send = call(
        far_pack_kernel,
        [((span, 3 * size), bf16)] * half,
        [far_pick] + far_rows,
        cost=50_000_000_000,
    )
    far_send, partner, tokens, home_place = lax.optimization_barrier(
        (far_send, partner, tokens, home_place)
    )
    far = [far_send[0]] + [crossed(far_send[by], by) for by in range(1, half)]
    spread_t, home_pick = call(
        functools.partial(return_index_kernel, rounds, devices, bound, token_count),
        [((rounds, buffer_rows, slots), bf16), ((token_count, devices * span), bf16)],
        [tokens, home_place],
        [pick] + keys,
        far=(0, 1),
    )
    far, spread_t, home_pick = lax.optimization_barrier((far, spread_t, home_pick))
    last, first = call(
        functools.partial(ends_kernel, rounds),
        [((rounds, cap, 2 * size), bf16)] * 2,
        [near, place] + far,
    )
    behind = shifted(last, 1)
    ahead = shifted(first, -1)
    square = (rounds, cap, cap)
    rows, units, prob, inner, first_score, first_inner_now, inner_sums = call(
        functools.partial(forward_inner_kernel, rounds),
        [
            ((rounds, per_device, cap, 3 * size), bf16),
            ((rounds, per_device, cap, size), bf16),
            ((rounds, per_device - 1, 2 * cap, cap), bf16),
            ((rounds, per_device - 1, 2 * cap, cap), bf16),
            (square, f32),
            (square, f32),
            ((sum_rows, cap), f32),
        ],
        [fill, near, place, last, first] + far,
    )
    behind_unit, first_prob, first_inner, sums, sums_send = call(
        functools.partial(forward_first_kernel, rounds, devices),
        [
            ((rounds, cap, size), bf16),
            ((rounds, 2 * cap, cap), bf16),
            ((rounds, 2 * cap, cap), bf16),
            ((sum_rows, cap), f32),
            ((devices, sum_rows * cap // lane, lane), f32),
        ],
        [fill, rows, behind, first_score, first_inner_now, inner_sums],
        [((sum_rows * cap // lane, lane), f32)],
    )
    sums_send, ahead = lax.optimization_barrier((sums_send, ahead))
    everyone = exchange(sums_send)
    (grads_send,) = call(
        functools.partial(backward_kernel, rounds, devices, bound),
        [((devices, span, 2 * size), bf16)],
        [
            fill,
            everyone,
            partner,
            low,
            sums,
            rows,
            ahead,
            units,
            behind_unit,
            first_prob,
            first_inner,
            prob,
            inner,
            spread_t,
        ],
        [((rounds, slots, 2 * size), bf16)],
    )
    home = exchange(grads_send.reshape(devices * span, 2 * size))
    return call(
        home_kernel,
        [((token_count, size), bf16), ((token_count, size), bf16)],
        [home_pick, home],
    )


def on_device(qk, values, grad_out, members, counts):
    grad_qk, grad_v = head_backward(qk[0], values[0], grad_out[0], members[0], counts[0])
    return (grad_qk[None], grad_v[None])


def solution(mesh):
    in_specs = (
        P("head", "seq", None),
        P("head", "seq", None),
        P("head", "seq", None),
        P("head", None, None, None),
        P("head", None, None),
    )
    out_specs = (P("head", "seq", None), P("head", "seq", None))
    return jax.shard_map(
        on_device, mesh=mesh, in_specs=in_specs, out_specs=out_specs, check_vma=False
    )
```

```python
import functools
import math

import jax
import jax.numpy as jnp
from jax import lax
from jax.experimental import pallas as pl
from jax.experimental.pallas import tpu as pltpu
from jax.sharding import PartitionSpec as P

masked_score = -1e30
norm_eps = 1e-06
lane = 128
f32 = jnp.float32
bf16 = jnp.bfloat16


def iota(shape, axis):
    return lax.broadcasted_iota(jnp.int32, shape, axis)


def float_iota(shape, axis):
    return iota(shape, axis).astype(f32)


def dot_nn(a, b):
    return lax.dot_general(a, b, (((1,), (0,)), ((), ())), preferred_element_type=f32)


def dot_nt(a, b):
    return lax.dot_general(a, b, (((1,), (1,)), ((), ())), preferred_element_type=f32)


def dot_tn(a, b):
    return lax.dot_general(a, b, (((0,), (0,)), ((), ())), preferred_element_type=f32)


def one_hot(condition):
    return jnp.where(condition, 1.0, 0.0).astype(bf16)


def short_hot(index, shape, axis):
    place = iota(shape, axis).astype(jnp.int16)
    short = jnp.broadcast_to(index.astype(jnp.int32), shape).astype(jnp.int16)
    return jnp.where(short == place, jnp.ones(shape, bf16), jnp.zeros(shape, bf16))


def block_of(device, devices):
    if devices % 4:
        return device
    depth = devices // 4
    level, column = device // 4, device % 4
    turn = column ^ (column >> 1)
    step = level + (turn % 2) * (depth - 1 - 2 * level)
    return turn * depth + step


def device_of(block, devices):
    if devices % 4:
        return block
    depth = devices // 4
    turn, step = block // depth, block % depth
    level = step + (turn % 2) * (depth - 1 - 2 * step)
    return level * 4 + (turn ^ (turn >> 1))


def earlier(size):
    return one_hot(iota((size, size), 0) < iota((size, size), 1))


def call(
    kernel,
    out_shapes,
    operands,
    scratch=(),
    remote=0,
    semaphores=0,
    far=(),
    direct=(),
    cost=0,
):
    count = len(operands)
    held = sum(array.size * array.dtype.itemsize for array in operands[: count - remote])
    for shape, dtype in list(out_shapes) + list(scratch):
        held += math.prod(shape) * jnp.dtype(dtype).itemsize
    spaces = [pltpu.VMEM] * (count - remote) + [pltpu.HBM] * remote
    operands = [
        pltpu.with_memory_space_constraint(array, space) if space is pltpu.HBM else array
        for array, space in zip(operands, spaces)
    ]
    return pl.pallas_call(
        kernel,
        out_shape=tuple(
            pltpu.HBM(shape, dtype) if at in far else jax.ShapeDtypeStruct(shape, dtype)
            for at, (shape, dtype) in enumerate(out_shapes)
        ),
        in_specs=[pl.BlockSpec(memory_space=space) for space in spaces],
        out_specs=tuple(
            pl.BlockSpec(memory_space=pltpu.HBM if at in direct else pltpu.VMEM)
            for at in range(len(out_shapes))
        ),
        scratch_shapes=[pltpu.VMEM(shape, dtype) for shape, dtype in scratch]
        + [pltpu.SemaphoreType.DMA((semaphores,))] * min(semaphores, 1),
        cost_estimate=pl.CostEstimate(flops=cost, transcendentals=0, bytes_accessed=0),
        compiler_params=pltpu.CompilerParams(vmem_limit_bytes=held + 12 * 1024 * 1024),
    )(*operands)


def slot_tokens(members_ref, counts_ref, devices, group):
    rounds, groups = counts_ref.shape
    per_device = groups // devices
    rows = pl.ds(group, rounds * devices, stride=per_device)
    parts = [members_ref[half, rows, :] for half in range(members_ref.shape[0])]
    listed = jnp.concatenate(parts, axis=1)
    diagonal = iota((devices, groups), 1) == iota((devices, groups), 0) * per_device + group
    limits = [
        jnp.sum(
            jnp.where(diagonal, counts_ref[r : r + 1, :].astype(f32), 0.0), axis=1, keepdims=True
        )
        for r in range(rounds)
    ]
    limit = jnp.concatenate(limits, axis=0)
    return jnp.where(float_iota(listed.shape, 1) < limit, listed, -1)


def rank_slots(rounds, devices, token_count, source, tokens_ref, key_ref, value_ref):
    per_device, _, cap = key_ref.shape
    start = source * token_count
    before = earlier(cap)
    carry = jnp.zeros((rounds * devices, 1), f32)
    for group in range(per_device):
        local = tokens_ref[group] - start
        owned = (local >= 0) & (local < token_count)
        rank = dot_nn(one_hot(owned), before) + carry
        carry = carry + jnp.sum(jnp.where(owned, 1.0, 0.0), axis=1, keepdims=True)
        key_ref[group] = jnp.where(owned, rank, -1.0)
        value_ref[group] = jnp.where(owned, local + 1, 0).astype(f32)


def pick_rows(rounds, devices, bound, block, token_count, key_ref, value_ref):
    per_device, _, cap = key_ref.shape
    column = float_iota((bound, cap), 0)
    picks = []
    for r in range(rounds):
        row = r * devices + block
        total = jnp.zeros((bound, cap), f32)
        for group in range(per_device):
            ranks = key_ref[group, pl.ds(row, 1), :]
            values = value_ref[group, pl.ds(row, 1), :]
            total = total + jnp.where(ranks == column, values, 0.0)
        index = jnp.sum(total, axis=1, keepdims=True) - 1.0
        picks.append(short_hot(index, (bound, token_count), 1))
    return jnp.concatenate(picks, axis=0)


def join_kernel(q_hbm, v_hbm, g_hbm, joined_ref, sems):
    size = q_hbm.shape[1]
    copies = []
    for at, source in enumerate((q_hbm, v_hbm, g_hbm)):
        target = joined_ref.at[:, pl.ds(at * size, size)]
        copies.append(pltpu.make_async_copy(source, target, sems.at[at]))
    for copy in copies:
        copy.start()
    for copy in copies:
        copy.wait()


def pack_kernel(
    rounds,
    devices,
    bound,
    joined_ref,
    counts_hbm,
    members_hbm,
    send_hbm,
    tokens_ref,
    packed_ref,
    key_ref,
    value_ref,
    counts_ref,
    members_ref,
    sems,
):
    token_count = joined_ref.shape[0]
    halves = members_ref.shape[0]
    copies = [pltpu.make_async_copy(counts_hbm, counts_ref, sems.at[halves])]
    for half in range(halves):
        source = members_hbm.at[:, pl.ds(half * lane, lane)]
        copies.append(pltpu.make_async_copy(source, members_ref.at[half], sems.at[half]))
    for copy in copies:
        copy.start()
    for copy in copies:
        copy.wait()
    for group in range(tokens_ref.shape[0]):
        tokens_ref[group] = slot_tokens(members_ref, counts_ref, devices, group)
    me = lax.axis_index("seq")
    rank_slots(rounds, devices, token_count, me, tokens_ref, key_ref, value_ref)
    half = devices // 2
    first = me // half * half
    parts = 4
    step = half // parts
    sends = []
    for part in range(parts):
        picks = [
            pick_rows(
                rounds,
                devices,
                bound,
                block_of(first + at, devices),
                token_count,
                key_ref,
                value_ref,
            )
            for at in range(part * step, (part + 1) * step)
        ]
        span = pl.ds(part * step * rounds * bound, step * rounds * bound)
        packed_ref[span, :] = dot_nn(jnp.concatenate(picks, axis=0), joined_ref[...]).astype(bf16)
        copy = pltpu.make_async_copy(
            packed_ref.at[span, :], send_hbm.at[span, :], sems.at[halves + 1 + part]
        )
        copy.start()
        sends.append(copy)
    for copy in sends:
        copy.wait()


def far_pick_kernel(rounds, devices, bound, token_count, tokens_ref, pick_ref, key_ref, value_ref):
    me = lax.axis_index("seq")
    half = devices // 2
    first = me // half * half
    source = lax.rem(me + half, devices)
    rank_slots(rounds, devices, token_count, source, tokens_ref, key_ref, value_ref)
    size = rounds * bound
    for at in range(half):
        block = block_of(first + jnp.bitwise_xor(me - first, at), devices)
        pick_ref[at * size : (at + 1) * size, :] = pick_rows(
            rounds, devices, bound, block, token_count, key_ref, value_ref
        )


def far_pack_kernel(pick_ref, rows_ref, *send_refs):
    rows = rows_ref[...]
    span = send_refs[0].shape[0]
    parts = 4
    count = len(send_refs) // parts
    for part in range(parts):
        first = part * count
        packed = dot_nn(pick_ref[pl.ds(first * span, count * span), :], rows).astype(bf16)
        for at in range(count):
            send_refs[first + at][...] = packed[at * span : (at + 1) * span]


def place_kernel(rounds, devices, bound, token_count, tokens_ref, place_ref, home_place_ref, fill_ref):
    per_device, _, cap = tokens_ref.shape
    seat = lax.axis_index("seq")
    me = block_of(seat, devices)
    half = devices // 2
    before = earlier(cap)
    source = iota((devices, cap), 0)
    source_start = source * token_count
    home_place = source.astype(f32) * bound + 1.0
    first = seat // half * half
    near = (source >= first) & (source < first + half)
    crossed = half + jnp.bitwise_xor(source % half, seat - first)
    source_place = jnp.where(near, source - first, crossed).astype(f32) * bound + 1.0
    for r in range(rounds):
        carry = jnp.zeros((devices, 1), f32)
        for group in range(per_device):
            tokens = tokens_ref[group, pl.ds(r * devices + me, 1), :]
            owned = (tokens >= source_start) & (tokens < source_start + token_count)
            rank = dot_nn(one_hot(owned), before) + carry
            carry = carry + jnp.sum(jnp.where(owned, 1.0, 0.0), axis=1, keepdims=True)
            for target, base in ((place_ref, source_place), (home_place_ref, home_place)):
                place = jnp.sum(jnp.where(owned, rank + base, 0.0), axis=0, keepdims=True) - 1.0
                row = r * per_device + group
                target[row : row + 1, :] = place
    after = lax.rem(me + 1, devices)
    behind = lax.rem(me + devices - 1, devices)
    for r in range(rounds):
        for at in range(per_device + 2):
            block = behind if at == 0 else after if at > per_device else me
            group = (at - 1) % per_device
            tokens = tokens_ref[group, pl.ds(r * devices + block, 1), :]
            fill = jnp.sum(jnp.where(tokens >= 0, 1.0, 0.0), axis=1, keepdims=True)
            row = r * (per_device + 2) + at
            fill_ref[row : row + 1, :] = jnp.broadcast_to(fill, (1, cap))


def index_kernel(
    rounds,
    devices,
    bound,
    token_count,
    tokens_ref,
    partner_ref,
    low_ref,
    table_ref,
):
    per_device, _, cap = tokens_ref.shape
    me = block_of(lax.axis_index("seq"), devices)
    after = lax.rem(me + 1, devices)
    high_count = devices * token_count // lane
    high_start = iota((high_count, cap), 0) * lane
    low_index = iota((lane, cap), 0)
    slot = float_iota((high_count, cap), 1)

    def split(tokens):
        high = (tokens >= high_start) & (tokens < high_start + lane)
        low = jnp.bitwise_and(tokens, lane - 1) == low_index
        return high, low

    for r in range(rounds):

        def one_block(block, total):
            device = device_of(block, devices)
            for group in range(per_device):
                tokens = tokens_ref[group, pl.ds(r * devices + block, 1), :]
                high, low = split(tokens)
                group_index = (device * per_device + group).astype(f32)
                sides = jnp.concatenate(
                    [
                        jnp.where(high, group_index, 0.0).astype(bf16),
                        jnp.where(high, slot, 0.0).astype(bf16),
                    ],
                    axis=0,
                )
                total = total + dot_nt(sides, one_hot(low))
            return total

        total = lax.fori_loop(
            0, devices, one_block, jnp.zeros((2 * high_count, lane), f32), unroll=2
        )
        table_ref[r] = total.astype(bf16)

    halves = cap // lane
    kept = table_kept(per_device * halves)
    row_column = float_iota((devices * kept, cap), 0)
    for r in range(rounds):
        other = 1 - r
        for group in range(per_device + 1):
            if group < per_device:
                tokens = tokens_ref[group, pl.ds(r * devices + me, 1), :]
            else:
                tokens = tokens_ref[0, pl.ds(r * devices + after, 1), :]
            high, low = split(tokens)
            high_hot = one_hot(high)
            found = []
            for part in range(2):
                table = table_ref[other, part * high_count : (part + 1) * high_count, :]
                picked = dot_tn(table, high_hot)
                found.append(jnp.sum(jnp.where(low, picked, 0.0), axis=0, keepdims=True))
            group_index, position = found
            device = jnp.floor((group_index + 0.5) * (1.0 / per_device))
            half = jnp.floor((position + 0.5) * (1.0 / lane))
            row = device * kept + (group_index - device * per_device) * halves + half
            span = pl.ds(group * cap, cap)
            partner_ref[r, :, span] = one_hot(row == row_column)
            low_ref[pl.ds(r * (per_device + 1) + group, 1), :] = position - half * lane


def return_index_kernel(
    rounds,
    devices,
    bound,
    token_count,
    tokens_ref,
    home_place_ref,
    spread_t_ref,
    home_ref,
    pick_ref,
    key_ref,
    value_ref,
):
    per_device, _, cap = tokens_ref.shape
    place_column = float_iota((devices * bound, cap), 0)
    for r in range(rounds):
        for group in range(per_device):
            row = r * per_device + group
            place = home_place_ref[row : row + 1, :]
            spread_t_ref[r, :, pl.ds(group * cap, cap)] = one_hot(place == place_column)
    seat = lax.axis_index("seq")
    rank_slots(rounds, devices, token_count, seat, tokens_ref, key_ref, value_ref)

    size = rounds * bound
    for device in range(devices):
        pick_ref[device * size : (device + 1) * size, :] = pick_rows(
            rounds, devices, bound, block_of(device, devices), token_count, key_ref, value_ref
        )
    home_ref[...] = jnp.transpose(pick_ref[...])


def table_kept(count):
    return (count + 7) // 8 * 8


def spread_of(place_ref, r, group, rounds, buffer_rows):
    row = r * (place_ref.shape[0] // rounds) + group
    cap = place_ref.shape[1]
    return short_hot(place_ref[row : row + 1, :], (buffer_rows, cap), 0)


def received_rows(near_ref, far_refs, r, rounds):
    half, span, width = near_ref.shape
    bound = span // rounds
    rows = slice(r * bound, (r + 1) * bound)
    parts = [near_ref[:, rows, :].reshape(half * bound, width)]
    parts += [far_ref[rows, :] for far_ref in far_refs]
    return jnp.concatenate(parts, axis=0)


def ends_kernel(rounds, near_ref, place_ref, *refs):
    far_refs, (last_ref, first_ref) = refs[:-2], refs[-2:]
    size = near_ref.shape[2] // 3
    per_device = place_ref.shape[0] // rounds
    for r in range(rounds):
        received = received_rows(near_ref, far_refs, r, rounds)
        spread = spread_of(place_ref, r, per_device - 1, rounds, received.shape[0])
        last_ref[r] = dot_tn(spread, received[:, : 2 * size]).astype(bf16)
        spread = spread_of(place_ref, r, 0, rounds, received.shape[0])
        wanted = jnp.concatenate([received[:, :size], received[:, 2 * size :]], axis=1)
        first_ref[r] = dot_tn(spread, wanted).astype(bf16)


def inverse_norm(rows):
    wide = rows.astype(f32)
    return lax.rsqrt(jnp.sum(wide * wide, axis=1, keepdims=True) + norm_eps)


def unit_rows(rows):
    return (rows.astype(f32) * inverse_norm(rows)).astype(bf16)


def fill_row(fill_ref, r, at, rounds):
    row = r * (fill_ref.shape[0] // rounds) + at
    return fill_ref[row : row + 1, :]


def scored(unit, queries, fill, own):
    cap = queries.shape[0]
    key = float_iota((cap, cap), 0)
    allowed = key < fill
    if own:
        allowed = allowed & (key != float_iota((cap, cap), 1))
    return jnp.where(allowed, dot_nt(unit, queries), masked_score)


def normalised(scores, inners):
    highest = jnp.maximum(
        jnp.max(scores[0], axis=0, keepdims=True), jnp.max(scores[1], axis=0, keepdims=True)
    )
    exps = [jnp.exp(score - highest) for score in scores]
    total = jnp.sum(exps[0], axis=0, keepdims=True) + jnp.sum(exps[1], axis=0, keepdims=True)
    inverse = 1.0 / total
    probs = [part * inverse for part in exps]
    dots = jnp.sum(probs[0] * inners[0], axis=0, keepdims=True) + jnp.sum(
        probs[1] * inners[1], axis=0, keepdims=True
    )
    centred = [(inner - dots).astype(bf16) for inner in inners]
    return highest + jnp.log(total), dots, [prob.astype(bf16) for prob in probs], centred


def forward_inner_kernel(
    rounds,
    fill_ref,
    near_ref,
    place_ref,
    last_ref,
    first_ref,
    *refs,
):
    far_refs, refs = refs[:-7], refs[-7:]
    rows_ref, units_ref, prob_ref, inner_ref, first_score_ref, first_inner_ref, sums_ref = refs
    cap = prob_ref.shape[3]
    per_device = rows_ref.shape[1]
    size = rows_ref.shape[3] // 3
    for r in range(rounds):
        received = received_rows(near_ref, far_refs, r, rounds)
        for group in range(per_device):
            spread = spread_of(place_ref, r, group, rounds, received.shape[0])
            if group == 0:
                values = dot_tn(spread, received[:, size : 2 * size]).astype(bf16)
                rows_ref[r, group, :, :size] = first_ref[r, :, :size]
                rows_ref[r, group, :, size : 2 * size] = values
                rows_ref[r, group, :, 2 * size :] = first_ref[r, :, size:]
            elif group < per_device - 1:
                rows_ref[r, group] = dot_tn(spread, received).astype(bf16)
            else:
                rows_ref[r, group, :, : 2 * size] = last_ref[r]
                cots = dot_tn(spread, received[:, 2 * size :]).astype(bf16)
                rows_ref[r, group, :, 2 * size :] = cots
        units = [unit_rows(rows_ref[r, group, :, :size]) for group in range(per_device)]
        for group in range(per_device):
            units_ref[r, group] = units[group]
        for group in range(per_device):
            queries = rows_ref[r, group, :, :size]
            cot = rows_ref[r, group, :, 2 * size :]
            values = rows_ref[r, group, :, size : 2 * size]
            score_now = scored(
                units[group], queries, fill_row(fill_ref, r, group + 1, rounds), True
            )
            inner_now = dot_nt(values, cot)
            if group == 0:
                first_score_ref[r] = score_now
                first_inner_ref[r] = inner_now
                continue
            values = rows_ref[r, group - 1, :, size : 2 * size]
            inner_before = dot_nt(values, cot)
            score_before = scored(
                units[group - 1], queries, fill_row(fill_ref, r, group, rounds), False
            )
            inners = [inner_before, inner_now]
            log_total, dots, probs, centred = normalised([score_before, score_now], inners)
            for side in range(2):
                span = slice(side * cap, (side + 1) * cap)
                prob_ref[r, group - 1, span, :] = probs[side]
                inner_ref[r, group - 1, span, :] = centred[side]
            row = r * per_device + group
            sums_ref[row : row + 1, :] = log_total
            row = (rounds + r) * per_device + group
            sums_ref[row : row + 1, :] = dots


def forward_first_kernel(
    rounds,
    devices,
    fill_ref,
    rows_ref,
    behind_ref,
    score_ref,
    inner_now_ref,
    inner_sums_ref,
    unit_ref,
    prob_ref,
    inner_ref,
    sums_ref,
    send_ref,
    block_ref,
):
    cap = prob_ref.shape[2]
    per_device = rows_ref.shape[1]
    size = rows_ref.shape[3] // 3
    sums_ref[...] = inner_sums_ref[...]
    for r in range(rounds):
        behind_unit = unit_rows(behind_ref[r, :, :size])
        unit_ref[r] = behind_unit
        queries = rows_ref[r, 0, :, :size]
        cot = rows_ref[r, 0, :, 2 * size :]
        score_before = scored(behind_unit, queries, fill_row(fill_ref, r, 0, rounds), False)
        inners = [dot_nt(behind_ref[r, :, size:], cot), inner_now_ref[r]]
        log_total, dots, probs, centred = normalised([score_before, score_ref[r]], inners)
        for side in range(2):
            span = slice(side * cap, (side + 1) * cap)
            prob_ref[r, span, :] = probs[side]
            inner_ref[r, span, :] = centred[side]
        row = r * per_device
        sums_ref[row : row + 1, :] = log_total
        row = (rounds + r) * per_device
        sums_ref[row : row + 1, :] = dots
    halves = cap // lane
    count = per_device * halves
    for r in range(rounds):
        for kind in range(2):
            for group in range(per_device):
                row = (kind * rounds + r) * per_device + group
                for half in range(halves):
                    at = (2 * r + kind) * count + group * halves + half
                    block_ref[at : at + 1, :] = sums_ref[
                        row : row + 1, half * lane : (half + 1) * lane
                    ]
    block = block_ref[...]
    for device in range(devices):
        send_ref[device] = block


def key_grad(rows, unit_grad):
    wide = rows.astype(f32)
    inverse = inverse_norm(rows)
    along = jnp.sum(wide * unit_grad, axis=1, keepdims=True)
    return inverse * unit_grad - wide * (inverse * inverse * inverse * along)


def three_parts(values):
    high = values.astype(bf16)
    rest = values - high.astype(f32)
    middle = rest.astype(bf16)
    return high, middle, (rest - middle.astype(f32)).astype(bf16)


def backward_kernel(
    rounds,
    devices,
    bound,
    fill_ref,
    everyone_ref,
    partner_ref,
    low_ref,
    sums_ref,
    rows_ref,
    ahead_ref,
    units_ref,
    behind_unit_ref,
    first_prob_ref,
    first_inner_ref,
    prob_ref,
    inner_ref,
    spread_t_ref,
    send_ref,
    grads_ref,
):
    cap = rows_ref.shape[2]
    per_device = rows_ref.shape[1]
    size = rows_ref.shape[3] // 3
    me = block_of(lax.axis_index("seq"), devices)
    ahead_device = device_of(lax.rem(me + 1, devices), devices)
    halves = cap // lane
    count = per_device * halves
    kept = table_kept(count)
    low_column = float_iota((lane, cap), 0)
    slot = float_iota((1, cap), 1)

    def sums_of_all(r, kind):
        start = (2 * r + kind) * count
        held = min(start, everyone_ref.shape[1] - kept)
        rows = everyone_ref[:, held : held + kept, :]
        if start > held:
            rows = jnp.concatenate(
                [rows[:, start - held :], jnp.zeros((devices, start - held, lane), f32)], axis=1
            )
        return jnp.transpose(rows.reshape(devices * kept, lane))

    def ahead_sums(r, kind):
        start = (2 * r + kind) * count
        rows = [everyone_ref[ahead_device, start + h : start + h + 1, :] for h in range(halves)]
        return jnp.concatenate(rows, axis=1)

    def scales_of(r):
        logs = three_parts(sums_of_all(1 - r, 0))
        dots = three_parts(sums_of_all(1 - r, 1))
        upright = jnp.concatenate(logs + dots[:2], axis=0)
        picked = dot_nn(upright, partner_ref[r])
        picked_log = picked[:lane] + (picked[lane : 2 * lane] + picked[2 * lane : 3 * lane])
        picked_dot = picked[3 * lane : 4 * lane] + picked[4 * lane :]
        scales = []
        for group in range(per_device + 1):
            at = r * (per_device + 1) + group
            here = low_ref[at : at + 1, :] == low_column
            span = slice(group * cap, (group + 1) * cap)
            other_log = jnp.sum(jnp.where(here, picked_log[:, span], 0.0), axis=0, keepdims=True)
            other_dot = jnp.sum(jnp.where(here, picked_dot[:, span], 0.0), axis=0, keepdims=True)
            if group < per_device:
                row = r * per_device + group
                own_log = sums_ref[row : row + 1, :]
                own_dot = sums_ref[rounds * per_device + row : rounds * per_device + row + 1, :]
            else:
                own_log = ahead_sums(r, 0)
                own_dot = ahead_sums(r, 1)
            weight = 1.0 / (1.0 + jnp.exp(other_log - own_log))
            other_weight = 1.0 / (1.0 + jnp.exp(own_log - other_log))
            shift = other_weight * (own_dot - other_dot)
            valid = slot < fill_row(fill_ref, r, group + 1, rounds)
            scales.append((jnp.where(valid, weight, 0.0), jnp.where(valid, shift, 0.0)))
        return scales

    def score_grads(prob, inner, scale):
        weighted = prob.astype(f32) * scale[0]
        score_grad = (weighted * (inner.astype(f32) + scale[1])).astype(bf16)
        return weighted.astype(bf16), score_grad

    aheads = []
    for r in range(rounds):
        queries = ahead_ref[r, :, :size]
        cot = ahead_ref[r, :, size:]
        fill = fill_row(fill_ref, r, per_device, rounds)
        score = scored(units_ref[r, per_device - 1], queries, fill, False)
        inner = dot_nt(rows_ref[r, per_device - 1, :, size : 2 * size], cot)
        aheads.append(([jnp.exp(score - ahead_sums(r, 0))], [inner - ahead_sums(r, 1)]))
    scales = [scales_of(r) for r in range(rounds)]
    carried = [None] * rounds
    for group in range(per_device + 1):
        for r in range(rounds):
            if group < per_device:
                queries = rows_ref[r, group, :, :size]
                cot = rows_ref[r, group, :, 2 * size :]
            else:
                queries = ahead_ref[r, :, :size]
                cot = ahead_ref[r, :, size:]
            if group == 0:
                probs = [first_prob_ref[r, :cap, :], first_prob_ref[r, cap:, :]]
                inners = [first_inner_ref[r, :cap, :], first_inner_ref[r, cap:, :]]
            elif group < per_device:
                probs = [prob_ref[r, group - 1, :cap, :], prob_ref[r, group - 1, cap:, :]]
                inners = [inner_ref[r, group - 1, :cap, :], inner_ref[r, group - 1, cap:, :]]
            else:
                probs, inners = aheads[r]
            scale = scales[r][group]
            weighted, score_grad = score_grads(probs[0], inners[0], scale)
            if group > 0:
                query_grad, unit_grad, value_grad = carried[r]
                unit_grad = unit_grad + dot_nn(score_grad, queries)
                value_grad = value_grad + dot_nn(weighted, cot)
                key_part = key_grad(rows_ref[r, group - 1, :, :size], unit_grad)
                span = slice((group - 1) * cap, group * cap)
                grads_ref[r, span, :size] = (query_grad + key_part).astype(bf16)
                grads_ref[r, span, size:] = value_grad.astype(bf16)
            if group < per_device:
                unit_before = behind_unit_ref[r] if group == 0 else units_ref[r, group - 1]
                query_grad = dot_tn(score_grad, unit_before)
                weighted, score_grad = score_grads(probs[1], inners[1], scale)
                query_grad = query_grad + dot_tn(score_grad, units_ref[r, group])
                unit_grad = dot_nn(score_grad, queries)
                carried[r] = (query_grad, unit_grad, dot_nn(weighted, cot))
    for r in range(rounds):
        packed = dot_nn(spread_t_ref[r], grads_ref[r]).astype(bf16)
        send_ref[:, r * bound : (r + 1) * bound, :] = packed.reshape(devices, bound, 2 * size)


def home_kernel(home_ref, got_ref, qk_ref, value_ref):
    size = qk_ref.shape[1]
    total = dot_nn(home_ref[...], got_ref[...])
    qk_ref[...] = total[:, :size].astype(bf16)
    value_ref[...] = total[:, size:].astype(bf16)


def exchange_in_half(array):
    devices = lax.axis_size("seq")
    half = devices // 2
    halves = [list(range(half)), list(range(half, devices))]
    return lax.all_to_all(
        array, "seq", split_axis=0, concat_axis=0, tiled=True, axis_index_groups=halves
    )


def crossed(array, by):
    devices = lax.axis_size("seq")
    return lax.ppermute(array, "seq", [(i, i ^ by) for i in range(devices)])


def mirrored(array):
    devices = lax.axis_size("seq")
    half = devices // 2
    return lax.ppermute(array, "seq", [(i, (i + half) % devices) for i in range(devices)])


def exchange(array):
    return lax.all_to_all(array, "seq", split_axis=0, concat_axis=0, tiled=True)


def shifted(array, by):
    devices = lax.axis_size("seq")
    order = [device_of(block, devices) for block in range(devices)]
    return lax.ppermute(array, "seq", [(order[i], order[(i + by) % devices]) for i in range(devices)])


def head_backward(qk, values, cot, members, counts):
    devices = lax.axis_size("seq")
    token_count, size = qk.shape
    rounds, groups, cap = members.shape
    per_device = groups // devices
    slots = per_device * cap
    bound = 2 * token_count // devices
    span = rounds * bound
    buffer_rows = devices * bound
    sum_rows = 2 * rounds * per_device
    listed = members.reshape(rounds * groups, cap)
    keys = [((per_device, rounds * devices, cap), f32)] * 2
    pick = ((devices * span, token_count), bf16)
    half = devices // 2
    (joined,) = call(
        join_kernel,
        [((token_count, 3 * size), bf16)],
        [qk, values, cot],
        remote=3,
        semaphores=3,
    )
    far_rows = mirrored(joined)
    near_send, tokens = call(
        functools.partial(pack_kernel, rounds, devices, bound),
        [((half * span, 3 * size), bf16), (keys[0][0], jnp.int32)],
        [joined, counts, listed],
        [((half * span, 3 * size), bf16)]
        + keys
        + [
            (counts.shape, jnp.int32),
            ((cap // lane, rounds * groups, lane), jnp.int32),
        ],
        remote=2,
        semaphores=cap // lane + 5,
        far=(0,),
        direct=(0,),
    )
    near = exchange_in_half(near_send).reshape(half, span, 3 * size)
    (far_pick,) = call(
        functools.partial(far_pick_kernel, rounds, devices, bound, token_count),
        [((half * span, token_count), bf16)],
        [tokens],
        keys,
    )
    place, home_place, fill = call(
        functools.partial(place_kernel, rounds, devices, bound, token_count),
        [
            ((rounds * per_device, cap), f32),
            ((rounds * per_device, cap), f32),
            ((rounds * (per_device + 2), cap), f32),
        ],
        [tokens],
    )
    partner, low = call(
        functools.partial(index_kernel, rounds, devices, bound, token_count),
        [
            ((rounds, devices * table_kept(slots // lane), slots + cap), bf16),
            ((rounds * (per_device + 1), cap), f32),
        ],
        [tokens],
        [((rounds, 2 * devices * token_count // lane, lane), bf16)],
        far=(0,),
    )
    far_send = call(
        far_pack_kernel,
        [((span, 3 * size), bf16)] * half,
        [far_pick, far_rows],
        cost=50_000_000_000,
    )
    far_send, partner, tokens, home_place = lax.optimization_barrier(
        (far_send, partner, tokens, home_place)
    )
    far = [far_send[0]] + [crossed(far_send[by], by) for by in range(1, half)]
    spread_t, home_pick = call(
        functools.partial(return_index_kernel, rounds, devices, bound, token_count),
        [((rounds, buffer_rows, slots), bf16), ((token_count, devices * span), bf16)],
        [tokens, home_place],
        [pick] + keys,
        far=(0, 1),
    )
    far, spread_t, home_pick = lax.optimization_barrier((far, spread_t, home_pick))
    last, first = call(
        functools.partial(ends_kernel, rounds),
        [((rounds, cap, 2 * size), bf16)] * 2,
        [near, place] + far,
    )
    behind = shifted(last, 1)
    ahead = shifted(first, -1)
    square = (rounds, cap, cap)
    rows, units, prob, inner, first_score, first_inner_now, inner_sums = call(
        functools.partial(forward_inner_kernel, rounds),
        [
            ((rounds, per_device, cap, 3 * size), bf16),
            ((rounds, per_device, cap, size), bf16),
            ((rounds, per_device - 1, 2 * cap, cap), bf16),
            ((rounds, per_device - 1, 2 * cap, cap), bf16),
            (square, f32),
            (square, f32),
            ((sum_rows, cap), f32),
        ],
        [fill, near, place, last, first] + far,
    )
    behind_unit, first_prob, first_inner, sums, sums_send = call(
        functools.partial(forward_first_kernel, rounds, devices),
        [
            ((rounds, cap, size), bf16),
            ((rounds, 2 * cap, cap), bf16),
            ((rounds, 2 * cap, cap), bf16),
            ((sum_rows, cap), f32),
            ((devices, sum_rows * cap // lane, lane), f32),
        ],
        [fill, rows, behind, first_score, first_inner_now, inner_sums],
        [((sum_rows * cap // lane, lane), f32)],
    )
    sums_send, ahead = lax.optimization_barrier((sums_send, ahead))
    everyone = exchange(sums_send)
    (grads_send,) = call(
        functools.partial(backward_kernel, rounds, devices, bound),
        [((devices, span, 2 * size), bf16)],
        [
            fill,
            everyone,
            partner,
            low,
            sums,
            rows,
            ahead,
            units,
            behind_unit,
            first_prob,
            first_inner,
            prob,
            inner,
            spread_t,
        ],
        [((rounds, slots, 2 * size), bf16)],
    )
    home = exchange(grads_send.reshape(devices * span, 2 * size))
    return call(
        home_kernel,
        [((token_count, size), bf16), ((token_count, size), bf16)],
        [home_pick, home],
    )


def on_device(qk, values, grad_out, members, counts):
    grad_qk, grad_v = head_backward(qk[0], values[0], grad_out[0], members[0], counts[0])
    return (grad_qk[None], grad_v[None])


def solution(mesh):
    in_specs = (
        P("head", "seq", None),
        P("head", "seq", None),
        P("head", "seq", None),
        P("head", None, None, None),
        P("head", None, None),
    )
    out_specs = (P("head", "seq", None), P("head", "seq", None))
    return jax.shard_map(
        on_device, mesh=mesh, in_specs=in_specs, out_specs=out_specs, check_vma=False
    )
```

```python
import functools
import math

import jax
import jax.numpy as jnp
from jax import lax
from jax.experimental import pallas as pl
from jax.experimental.pallas import tpu as pltpu
from jax.sharding import PartitionSpec as P

masked_score = -1e30
norm_eps = 1e-06
lane = 128
f32 = jnp.float32
bf16 = jnp.bfloat16


def iota(shape, axis):
    return lax.broadcasted_iota(jnp.int32, shape, axis)


def float_iota(shape, axis):
    return iota(shape, axis).astype(f32)


def dot_nn(a, b):
    return lax.dot_general(a, b, (((1,), (0,)), ((), ())), preferred_element_type=f32)


def dot_nt(a, b):
    return lax.dot_general(a, b, (((1,), (1,)), ((), ())), preferred_element_type=f32)


def dot_tn(a, b):
    return lax.dot_general(a, b, (((0,), (0,)), ((), ())), preferred_element_type=f32)


def one_hot(condition):
    return jnp.where(condition, 1.0, 0.0).astype(bf16)


def short_hot(index, shape, axis):
    place = iota(shape, axis).astype(jnp.int16)
    short = jnp.broadcast_to(index.astype(jnp.int32), shape).astype(jnp.int16)
    return jnp.where(short == place, jnp.ones(shape, bf16), jnp.zeros(shape, bf16))


def block_of(device, devices):
    if devices % 4:
        return device
    depth = devices // 4
    level, column = device // 4, device % 4
    turn = column ^ (column >> 1)
    step = level + (turn % 2) * (depth - 1 - 2 * level)
    return turn * depth + step


def device_of(block, devices):
    if devices % 4:
        return block
    depth = devices // 4
    turn, step = block // depth, block % depth
    level = step + (turn % 2) * (depth - 1 - 2 * step)
    return level * 4 + (turn ^ (turn >> 1))


def earlier(size):
    return one_hot(iota((size, size), 0) < iota((size, size), 1))


def call(
    kernel,
    out_shapes,
    operands,
    scratch=(),
    remote=0,
    semaphores=0,
    far=(),
    direct=(),
    cost=0,
):
    count = len(operands)
    held = sum(array.size * array.dtype.itemsize for array in operands[: count - remote])
    for shape, dtype in list(out_shapes) + list(scratch):
        held += math.prod(shape) * jnp.dtype(dtype).itemsize
    spaces = [pltpu.VMEM] * (count - remote) + [pltpu.HBM] * remote
    operands = [
        pltpu.with_memory_space_constraint(array, space) if space is pltpu.HBM else array
        for array, space in zip(operands, spaces)
    ]
    return pl.pallas_call(
        kernel,
        out_shape=tuple(
            pltpu.HBM(shape, dtype) if at in far else jax.ShapeDtypeStruct(shape, dtype)
            for at, (shape, dtype) in enumerate(out_shapes)
        ),
        in_specs=[pl.BlockSpec(memory_space=space) for space in spaces],
        out_specs=tuple(
            pl.BlockSpec(memory_space=pltpu.HBM if at in direct else pltpu.VMEM)
            for at in range(len(out_shapes))
        ),
        scratch_shapes=[pltpu.VMEM(shape, dtype) for shape, dtype in scratch]
        + [pltpu.SemaphoreType.DMA((semaphores,))] * min(semaphores, 1),
        cost_estimate=pl.CostEstimate(flops=cost, transcendentals=0, bytes_accessed=0),
        compiler_params=pltpu.CompilerParams(vmem_limit_bytes=held + 12 * 1024 * 1024),
    )(*operands)


def slot_tokens(members_ref, counts_ref, devices, group):
    rounds, groups = counts_ref.shape
    per_device = groups // devices
    rows = pl.ds(group, rounds * devices, stride=per_device)
    parts = [members_ref[half, rows, :] for half in range(members_ref.shape[0])]
    listed = jnp.concatenate(parts, axis=1)
    diagonal = iota((devices, groups), 1) == iota((devices, groups), 0) * per_device + group
    limits = [
        jnp.sum(
            jnp.where(diagonal, counts_ref[r : r + 1, :].astype(f32), 0.0), axis=1, keepdims=True
        )
        for r in range(rounds)
    ]
    limit = jnp.concatenate(limits, axis=0)
    return jnp.where(float_iota(listed.shape, 1) < limit, listed, -1)


def rank_slots(rounds, devices, token_count, source, tokens_ref, key_ref, value_ref):
    per_device, _, cap = key_ref.shape
    start = source * token_count
    before = earlier(cap)
    carry = jnp.zeros((rounds * devices, 1), f32)
    for group in range(per_device):
        local = tokens_ref[group] - start
        owned = (local >= 0) & (local < token_count)
        rank = dot_nn(one_hot(owned), before) + carry
        carry = carry + jnp.sum(jnp.where(owned, 1.0, 0.0), axis=1, keepdims=True)
        key_ref[group] = jnp.where(owned, rank, -1.0)
        value_ref[group] = jnp.where(owned, local + 1, 0).astype(f32)


def pick_rows(rounds, devices, bound, block, token_count, key_ref, value_ref):
    per_device, _, cap = key_ref.shape
    column = float_iota((bound, cap), 0)
    picks = []
    for r in range(rounds):
        row = r * devices + block
        total = jnp.zeros((bound, cap), f32)
        for group in range(per_device):
            ranks = key_ref[group, pl.ds(row, 1), :]
            values = value_ref[group, pl.ds(row, 1), :]
            total = total + jnp.where(ranks == column, values, 0.0)
        index = jnp.sum(total, axis=1, keepdims=True) - 1.0
        picks.append(short_hot(index, (bound, token_count), 1))
    return jnp.concatenate(picks, axis=0)


def join_kernel(q_hbm, v_hbm, g_hbm, joined_ref, sems):
    size = q_hbm.shape[1]
    copies = []
    for at, source in enumerate((q_hbm, v_hbm, g_hbm)):
        target = joined_ref.at[:, pl.ds(at * size, size)]
        copies.append(pltpu.make_async_copy(source, target, sems.at[at]))
    for copy in copies:
        copy.start()
    for copy in copies:
        copy.wait()


def pack_kernel(
    rounds,
    devices,
    bound,
    joined_ref,
    counts_hbm,
    members_hbm,
    send_hbm,
    tokens_ref,
    packed_ref,
    key_ref,
    value_ref,
    counts_ref,
    members_ref,
    sems,
):
    token_count = joined_ref.shape[0]
    halves = members_ref.shape[0]
    copies = [pltpu.make_async_copy(counts_hbm, counts_ref, sems.at[halves])]
    for half in range(halves):
        source = members_hbm.at[:, pl.ds(half * lane, lane)]
        copies.append(pltpu.make_async_copy(source, members_ref.at[half], sems.at[half]))
    for copy in copies:
        copy.start()
    for copy in copies:
        copy.wait()
    for group in range(tokens_ref.shape[0]):
        tokens_ref[group] = slot_tokens(members_ref, counts_ref, devices, group)
    me = lax.axis_index("seq")
    rank_slots(rounds, devices, token_count, me, tokens_ref, key_ref, value_ref)
    half = devices // 2
    first = me // half * half
    parts = 4
    step = half // parts
    sends = []
    for part in range(parts):
        picks = [
            pick_rows(
                rounds,
                devices,
                bound,
                block_of(first + at, devices),
                token_count,
                key_ref,
                value_ref,
            )
            for at in range(part * step, (part + 1) * step)
        ]
        span = pl.ds(part * step * rounds * bound, step * rounds * bound)
        packed_ref[span, :] = dot_nn(jnp.concatenate(picks, axis=0), joined_ref[...]).astype(bf16)
        copy = pltpu.make_async_copy(
            packed_ref.at[span, :], send_hbm.at[span, :], sems.at[halves + 1 + part]
        )
        copy.start()
        sends.append(copy)
    for copy in sends:
        copy.wait()


def far_pick_kernel(rounds, devices, bound, token_count, tokens_ref, pick_ref, key_ref, value_ref):
    me = lax.axis_index("seq")
    half = devices // 2
    first = me // half * half
    source = lax.rem(me + half, devices)
    rank_slots(rounds, devices, token_count, source, tokens_ref, key_ref, value_ref)
    size = rounds * bound
    for at in range(half):
        block = block_of(first + jnp.bitwise_xor(me - first, -at % half), devices)
        pick_ref[at * size : (at + 1) * size, :] = pick_rows(
            rounds, devices, bound, block, token_count, key_ref, value_ref
        )


def far_pack_kernel(pick_ref, rows_ref, *send_refs):
    rows = rows_ref[...]
    span = send_refs[0].shape[0]
    parts = 4
    count = len(send_refs) // parts
    for part in range(parts):
        first = part * count
        packed = dot_nn(pick_ref[pl.ds(first * span, count * span), :], rows).astype(bf16)
        for at in range(count):
            send_refs[first + at][...] = packed[at * span : (at + 1) * span]


def place_kernel(rounds, devices, bound, token_count, tokens_ref, place_ref, home_place_ref, fill_ref):
    per_device, _, cap = tokens_ref.shape
    seat = lax.axis_index("seq")
    me = block_of(seat, devices)
    half = devices // 2
    before = earlier(cap)
    source = iota((devices, cap), 0)
    source_start = source * token_count
    home_place = source.astype(f32) * bound + 1.0
    first = seat // half * half
    near = (source >= first) & (source < first + half)
    bits = jnp.bitwise_xor(source % half, seat - first)
    crossed = half + jnp.where(bits > 0, half - bits, 0)
    source_place = jnp.where(near, source - first, crossed).astype(f32) * bound + 1.0
    for r in range(rounds):
        carry = jnp.zeros((devices, 1), f32)
        for group in range(per_device):
            tokens = tokens_ref[group, pl.ds(r * devices + me, 1), :]
            owned = (tokens >= source_start) & (tokens < source_start + token_count)
            rank = dot_nn(one_hot(owned), before) + carry
            carry = carry + jnp.sum(jnp.where(owned, 1.0, 0.0), axis=1, keepdims=True)
            for target, base in ((place_ref, source_place), (home_place_ref, home_place)):
                place = jnp.sum(jnp.where(owned, rank + base, 0.0), axis=0, keepdims=True) - 1.0
                row = r * per_device + group
                target[row : row + 1, :] = place
    after = lax.rem(me + 1, devices)
    behind = lax.rem(me + devices - 1, devices)
    for r in range(rounds):
        for at in range(per_device + 2):
            block = behind if at == 0 else after if at > per_device else me
            group = (at - 1) % per_device
            tokens = tokens_ref[group, pl.ds(r * devices + block, 1), :]
            fill = jnp.sum(jnp.where(tokens >= 0, 1.0, 0.0), axis=1, keepdims=True)
            row = r * (per_device + 2) + at
            fill_ref[row : row + 1, :] = jnp.broadcast_to(fill, (1, cap))


def index_kernel(
    rounds,
    devices,
    bound,
    token_count,
    tokens_ref,
    partner_ref,
    low_ref,
    table_ref,
):
    per_device, _, cap = tokens_ref.shape
    me = block_of(lax.axis_index("seq"), devices)
    after = lax.rem(me + 1, devices)
    high_count = devices * token_count // lane
    high_start = iota((high_count, cap), 0) * lane
    low_index = iota((lane, cap), 0)
    slot = float_iota((high_count, cap), 1)

    def split(tokens):
        high = (tokens >= high_start) & (tokens < high_start + lane)
        low = jnp.bitwise_and(tokens, lane - 1) == low_index
        return high, low

    for r in range(rounds):

        def one_block(block, total):
            device = device_of(block, devices)
            for group in range(per_device):
                tokens = tokens_ref[group, pl.ds(r * devices + block, 1), :]
                high, low = split(tokens)
                group_index = (device * per_device + group).astype(f32)
                sides = jnp.concatenate(
                    [
                        jnp.where(high, group_index, 0.0).astype(bf16),
                        jnp.where(high, slot, 0.0).astype(bf16),
                    ],
                    axis=0,
                )
                total = total + dot_nt(sides, one_hot(low))
            return total

        total = lax.fori_loop(
            0, devices, one_block, jnp.zeros((2 * high_count, lane), f32), unroll=2
        )
        table_ref[r] = total.astype(bf16)

    halves = cap // lane
    kept = table_kept(per_device * halves)
    row_column = float_iota((devices * kept, cap), 0)
    for r in range(rounds):
        other = 1 - r
        for group in range(per_device + 1):
            if group < per_device:
                tokens = tokens_ref[group, pl.ds(r * devices + me, 1), :]
            else:
                tokens = tokens_ref[0, pl.ds(r * devices + after, 1), :]
            high, low = split(tokens)
            high_hot = one_hot(high)
            found = []
            for part in range(2):
                table = table_ref[other, part * high_count : (part + 1) * high_count, :]
                picked = dot_tn(table, high_hot)
                found.append(jnp.sum(jnp.where(low, picked, 0.0), axis=0, keepdims=True))
            group_index, position = found
            device = jnp.floor((group_index + 0.5) * (1.0 / per_device))
            half = jnp.floor((position + 0.5) * (1.0 / lane))
            row = device * kept + (group_index - device * per_device) * halves + half
            span = pl.ds(group * cap, cap)
            partner_ref[r, :, span] = one_hot(row == row_column)
            low_ref[pl.ds(r * (per_device + 1) + group, 1), :] = position - half * lane


def return_index_kernel(
    rounds,
    devices,
    bound,
    token_count,
    tokens_ref,
    home_place_ref,
    spread_t_ref,
    home_ref,
    pick_ref,
    key_ref,
    value_ref,
):
    per_device, _, cap = tokens_ref.shape
    place_column = float_iota((devices * bound, cap), 0)
    for r in range(rounds):
        for group in range(per_device):
            row = r * per_device + group
            place = home_place_ref[row : row + 1, :]
            spread_t_ref[r, :, pl.ds(group * cap, cap)] = one_hot(place == place_column)
    seat = lax.axis_index("seq")
    rank_slots(rounds, devices, token_count, seat, tokens_ref, key_ref, value_ref)

    size = rounds * bound
    for device in range(devices):
        pick_ref[device * size : (device + 1) * size, :] = pick_rows(
            rounds, devices, bound, block_of(device, devices), token_count, key_ref, value_ref
        )
    home_ref[...] = jnp.transpose(pick_ref[...])


def table_kept(count):
    return (count + 7) // 8 * 8


def spread_of(place_ref, r, group, rounds, buffer_rows):
    row = r * (place_ref.shape[0] // rounds) + group
    cap = place_ref.shape[1]
    return short_hot(place_ref[row : row + 1, :], (buffer_rows, cap), 0)


def received_rows(near_ref, far_refs, r, rounds):
    half, span, width = near_ref.shape
    bound = span // rounds
    rows = slice(r * bound, (r + 1) * bound)
    parts = [near_ref[:, rows, :].reshape(half * bound, width)]
    parts += [far_ref[rows, :] for far_ref in far_refs]
    return jnp.concatenate(parts, axis=0)


def ends_kernel(rounds, near_ref, place_ref, *refs):
    far_refs, (last_ref, first_ref) = refs[:-2], refs[-2:]
    size = near_ref.shape[2] // 3
    per_device = place_ref.shape[0] // rounds
    for r in range(rounds):
        received = received_rows(near_ref, far_refs, r, rounds)
        spread = spread_of(place_ref, r, per_device - 1, rounds, received.shape[0])
        last_ref[r] = dot_tn(spread, received[:, : 2 * size]).astype(bf16)
        spread = spread_of(place_ref, r, 0, rounds, received.shape[0])
        wanted = jnp.concatenate([received[:, :size], received[:, 2 * size :]], axis=1)
        first_ref[r] = dot_tn(spread, wanted).astype(bf16)


def inverse_norm(rows):
    wide = rows.astype(f32)
    return lax.rsqrt(jnp.sum(wide * wide, axis=1, keepdims=True) + norm_eps)


def unit_rows(rows):
    return (rows.astype(f32) * inverse_norm(rows)).astype(bf16)


def fill_row(fill_ref, r, at, rounds):
    row = r * (fill_ref.shape[0] // rounds) + at
    return fill_ref[row : row + 1, :]


def scored(unit, queries, fill, own):
    cap = queries.shape[0]
    key = float_iota((cap, cap), 0)
    allowed = key < fill
    if own:
        allowed = allowed & (key != float_iota((cap, cap), 1))
    return jnp.where(allowed, dot_nt(unit, queries), masked_score)


def normalised(scores, inners):
    highest = jnp.maximum(
        jnp.max(scores[0], axis=0, keepdims=True), jnp.max(scores[1], axis=0, keepdims=True)
    )
    exps = [jnp.exp(score - highest) for score in scores]
    total = jnp.sum(exps[0], axis=0, keepdims=True) + jnp.sum(exps[1], axis=0, keepdims=True)
    inverse = 1.0 / total
    probs = [part * inverse for part in exps]
    dots = jnp.sum(probs[0] * inners[0], axis=0, keepdims=True) + jnp.sum(
        probs[1] * inners[1], axis=0, keepdims=True
    )
    centred = [(inner - dots).astype(bf16) for inner in inners]
    return highest + jnp.log(total), dots, [prob.astype(bf16) for prob in probs], centred


def forward_inner_kernel(
    rounds,
    fill_ref,
    near_ref,
    place_ref,
    last_ref,
    first_ref,
    *refs,
):
    far_refs, refs = refs[:-7], refs[-7:]
    rows_ref, units_ref, prob_ref, inner_ref, first_score_ref, first_inner_ref, sums_ref = refs
    cap = prob_ref.shape[3]
    per_device = rows_ref.shape[1]
    size = rows_ref.shape[3] // 3
    for r in range(rounds):
        received = received_rows(near_ref, far_refs, r, rounds)
        for group in range(per_device):
            spread = spread_of(place_ref, r, group, rounds, received.shape[0])
            if group == 0:
                values = dot_tn(spread, received[:, size : 2 * size]).astype(bf16)
                rows_ref[r, group, :, :size] = first_ref[r, :, :size]
                rows_ref[r, group, :, size : 2 * size] = values
                rows_ref[r, group, :, 2 * size :] = first_ref[r, :, size:]
            elif group < per_device - 1:
                rows_ref[r, group] = dot_tn(spread, received).astype(bf16)
            else:
                rows_ref[r, group, :, : 2 * size] = last_ref[r]
                cots = dot_tn(spread, received[:, 2 * size :]).astype(bf16)
                rows_ref[r, group, :, 2 * size :] = cots
        units = [unit_rows(rows_ref[r, group, :, :size]) for group in range(per_device)]
        for group in range(per_device):
            units_ref[r, group] = units[group]
        for group in range(per_device):
            queries = rows_ref[r, group, :, :size]
            cot = rows_ref[r, group, :, 2 * size :]
            values = rows_ref[r, group, :, size : 2 * size]
            score_now = scored(
                units[group], queries, fill_row(fill_ref, r, group + 1, rounds), True
            )
            inner_now = dot_nt(values, cot)
            if group == 0:
                first_score_ref[r] = score_now
                first_inner_ref[r] = inner_now
                continue
            values = rows_ref[r, group - 1, :, size : 2 * size]
            inner_before = dot_nt(values, cot)
            score_before = scored(
                units[group - 1], queries, fill_row(fill_ref, r, group, rounds), False
            )
            inners = [inner_before, inner_now]
            log_total, dots, probs, centred = normalised([score_before, score_now], inners)
            for side in range(2):
                span = slice(side * cap, (side + 1) * cap)
                prob_ref[r, group - 1, span, :] = probs[side]
                inner_ref[r, group - 1, span, :] = centred[side]
            row = r * per_device + group
            sums_ref[row : row + 1, :] = log_total
            row = (rounds + r) * per_device + group
            sums_ref[row : row + 1, :] = dots


def forward_first_kernel(
    rounds,
    devices,
    fill_ref,
    rows_ref,
    behind_ref,
    score_ref,
    inner_now_ref,
    inner_sums_ref,
    unit_ref,
    prob_ref,
    inner_ref,
    sums_ref,
    send_ref,
    block_ref,
):
    cap = prob_ref.shape[2]
    per_device = rows_ref.shape[1]
    size = rows_ref.shape[3] // 3
    sums_ref[...] = inner_sums_ref[...]
    for r in range(rounds):
        behind_unit = unit_rows(behind_ref[r, :, :size])
        unit_ref[r] = behind_unit
        queries = rows_ref[r, 0, :, :size]
        cot = rows_ref[r, 0, :, 2 * size :]
        score_before = scored(behind_unit, queries, fill_row(fill_ref, r, 0, rounds), False)
        inners = [dot_nt(behind_ref[r, :, size:], cot), inner_now_ref[r]]
        log_total, dots, probs, centred = normalised([score_before, score_ref[r]], inners)
        for side in range(2):
            span = slice(side * cap, (side + 1) * cap)
            prob_ref[r, span, :] = probs[side]
            inner_ref[r, span, :] = centred[side]
        row = r * per_device
        sums_ref[row : row + 1, :] = log_total
        row = (rounds + r) * per_device
        sums_ref[row : row + 1, :] = dots
    halves = cap // lane
    count = per_device * halves
    for r in range(rounds):
        for kind in range(2):
            for group in range(per_device):
                row = (kind * rounds + r) * per_device + group
                for half in range(halves):
                    at = (2 * r + kind) * count + group * halves + half
                    block_ref[at : at + 1, :] = sums_ref[
                        row : row + 1, half * lane : (half + 1) * lane
                    ]
    block = block_ref[...]
    for device in range(devices):
        send_ref[device] = block


def key_grad(rows, unit_grad):
    wide = rows.astype(f32)
    inverse = inverse_norm(rows)
    along = jnp.sum(wide * unit_grad, axis=1, keepdims=True)
    return inverse * unit_grad - wide * (inverse * inverse * inverse * along)


def three_parts(values):
    high = values.astype(bf16)
    rest = values - high.astype(f32)
    middle = rest.astype(bf16)
    return high, middle, (rest - middle.astype(f32)).astype(bf16)


def backward_kernel(
    rounds,
    devices,
    bound,
    fill_ref,
    everyone_ref,
    partner_ref,
    low_ref,
    sums_ref,
    rows_ref,
    ahead_ref,
    units_ref,
    behind_unit_ref,
    first_prob_ref,
    first_inner_ref,
    prob_ref,
    inner_ref,
    spread_t_ref,
    send_ref,
    grads_ref,
):
    cap = rows_ref.shape[2]
    per_device = rows_ref.shape[1]
    size = rows_ref.shape[3] // 3
    me = block_of(lax.axis_index("seq"), devices)
    ahead_device = device_of(lax.rem(me + 1, devices), devices)
    halves = cap // lane
    count = per_device * halves
    kept = table_kept(count)
    low_column = float_iota((lane, cap), 0)
    slot = float_iota((1, cap), 1)

    def sums_of_all(r, kind):
        start = (2 * r + kind) * count
        held = min(start, everyone_ref.shape[1] - kept)
        rows = everyone_ref[:, held : held + kept, :]
        if start > held:
            rows = jnp.concatenate(
                [rows[:, start - held :], jnp.zeros((devices, start - held, lane), f32)], axis=1
            )
        return jnp.transpose(rows.reshape(devices * kept, lane))

    def ahead_sums(r, kind):
        start = (2 * r + kind) * count
        rows = [everyone_ref[ahead_device, start + h : start + h + 1, :] for h in range(halves)]
        return jnp.concatenate(rows, axis=1)

    def scales_of(r):
        logs = three_parts(sums_of_all(1 - r, 0))
        dots = three_parts(sums_of_all(1 - r, 1))
        upright = jnp.concatenate(logs + dots[:2], axis=0)
        picked = dot_nn(upright, partner_ref[r])
        picked_log = picked[:lane] + (picked[lane : 2 * lane] + picked[2 * lane : 3 * lane])
        picked_dot = picked[3 * lane : 4 * lane] + picked[4 * lane :]
        scales = []
        for group in range(per_device + 1):
            at = r * (per_device + 1) + group
            here = low_ref[at : at + 1, :] == low_column
            span = slice(group * cap, (group + 1) * cap)
            other_log = jnp.sum(jnp.where(here, picked_log[:, span], 0.0), axis=0, keepdims=True)
            other_dot = jnp.sum(jnp.where(here, picked_dot[:, span], 0.0), axis=0, keepdims=True)
            if group < per_device:
                row = r * per_device + group
                own_log = sums_ref[row : row + 1, :]
                own_dot = sums_ref[rounds * per_device + row : rounds * per_device + row + 1, :]
            else:
                own_log = ahead_sums(r, 0)
                own_dot = ahead_sums(r, 1)
            weight = 1.0 / (1.0 + jnp.exp(other_log - own_log))
            other_weight = 1.0 / (1.0 + jnp.exp(own_log - other_log))
            shift = other_weight * (own_dot - other_dot)
            valid = slot < fill_row(fill_ref, r, group + 1, rounds)
            scales.append((jnp.where(valid, weight, 0.0), jnp.where(valid, shift, 0.0)))
        return scales

    def score_grads(prob, inner, scale):
        weighted = prob.astype(f32) * scale[0]
        score_grad = (weighted * (inner.astype(f32) + scale[1])).astype(bf16)
        return weighted.astype(bf16), score_grad

    aheads = []
    for r in range(rounds):
        queries = ahead_ref[r, :, :size]
        cot = ahead_ref[r, :, size:]
        fill = fill_row(fill_ref, r, per_device, rounds)
        score = scored(units_ref[r, per_device - 1], queries, fill, False)
        inner = dot_nt(rows_ref[r, per_device - 1, :, size : 2 * size], cot)
        aheads.append(([jnp.exp(score - ahead_sums(r, 0))], [inner - ahead_sums(r, 1)]))
    scales = [scales_of(r) for r in range(rounds)]
    carried = [None] * rounds
    for group in range(per_device + 1):
        for r in range(rounds):
            if group < per_device:
                queries = rows_ref[r, group, :, :size]
                cot = rows_ref[r, group, :, 2 * size :]
            else:
                queries = ahead_ref[r, :, :size]
                cot = ahead_ref[r, :, size:]
            if group == 0:
                probs = [first_prob_ref[r, :cap, :], first_prob_ref[r, cap:, :]]
                inners = [first_inner_ref[r, :cap, :], first_inner_ref[r, cap:, :]]
            elif group < per_device:
                probs = [prob_ref[r, group - 1, :cap, :], prob_ref[r, group - 1, cap:, :]]
                inners = [inner_ref[r, group - 1, :cap, :], inner_ref[r, group - 1, cap:, :]]
            else:
                probs, inners = aheads[r]
            scale = scales[r][group]
            weighted, score_grad = score_grads(probs[0], inners[0], scale)
            if group > 0:
                query_grad, unit_grad, value_grad = carried[r]
                unit_grad = unit_grad + dot_nn(score_grad, queries)
                value_grad = value_grad + dot_nn(weighted, cot)
                key_part = key_grad(rows_ref[r, group - 1, :, :size], unit_grad)
                span = slice((group - 1) * cap, group * cap)
                grads_ref[r, span, :size] = (query_grad + key_part).astype(bf16)
                grads_ref[r, span, size:] = value_grad.astype(bf16)
            if group < per_device:
                unit_before = behind_unit_ref[r] if group == 0 else units_ref[r, group - 1]
                query_grad = dot_tn(score_grad, unit_before)
                weighted, score_grad = score_grads(probs[1], inners[1], scale)
                query_grad = query_grad + dot_tn(score_grad, units_ref[r, group])
                unit_grad = dot_nn(score_grad, queries)
                carried[r] = (query_grad, unit_grad, dot_nn(weighted, cot))
    for r in range(rounds):
        packed = dot_nn(spread_t_ref[r], grads_ref[r]).astype(bf16)
        send_ref[:, r * bound : (r + 1) * bound, :] = packed.reshape(devices, bound, 2 * size)


def home_kernel(home_ref, got_ref, qk_ref, value_ref):
    size = qk_ref.shape[1]
    total = dot_nn(home_ref[...], got_ref[...])
    qk_ref[...] = total[:, :size].astype(bf16)
    value_ref[...] = total[:, size:].astype(bf16)


def exchange_in_half(array):
    devices = lax.axis_size("seq")
    half = devices // 2
    halves = [list(range(half)), list(range(half, devices))]
    return lax.all_to_all(
        array, "seq", split_axis=0, concat_axis=0, tiled=True, axis_index_groups=halves
    )


def crossed(array, by):
    devices = lax.axis_size("seq")
    return lax.ppermute(array, "seq", [(i, i ^ by) for i in range(devices)])


def mirrored(array):
    devices = lax.axis_size("seq")
    half = devices // 2
    return lax.ppermute(array, "seq", [(i, (i + half) % devices) for i in range(devices)])


def exchange(array):
    return lax.all_to_all(array, "seq", split_axis=0, concat_axis=0, tiled=True)


def shifted(array, by):
    devices = lax.axis_size("seq")
    order = [device_of(block, devices) for block in range(devices)]
    return lax.ppermute(array, "seq", [(order[i], order[(i + by) % devices]) for i in range(devices)])


def head_backward(qk, values, cot, members, counts):
    devices = lax.axis_size("seq")
    token_count, size = qk.shape
    rounds, groups, cap = members.shape
    per_device = groups // devices
    slots = per_device * cap
    bound = 2 * token_count // devices
    span = rounds * bound
    buffer_rows = devices * bound
    sum_rows = 2 * rounds * per_device
    listed = members.reshape(rounds * groups, cap)
    keys = [((per_device, rounds * devices, cap), f32)] * 2
    pick = ((devices * span, token_count), bf16)
    half = devices // 2
    (joined,) = call(
        join_kernel,
        [((token_count, 3 * size), bf16)],
        [qk, values, cot],
        remote=3,
        semaphores=3,
    )
    far_rows = mirrored(joined)
    near_send, tokens = call(
        functools.partial(pack_kernel, rounds, devices, bound),
        [((half * span, 3 * size), bf16), (keys[0][0], jnp.int32)],
        [joined, counts, listed],
        [((half * span, 3 * size), bf16)]
        + keys
        + [
            (counts.shape, jnp.int32),
            ((cap // lane, rounds * groups, lane), jnp.int32),
        ],
        remote=2,
        semaphores=cap // lane + 5,
        far=(0,),
        direct=(0,),
    )
    near = exchange_in_half(near_send).reshape(half, span, 3 * size)
    (far_pick,) = call(
        functools.partial(far_pick_kernel, rounds, devices, bound, token_count),
        [((half * span, token_count), bf16)],
        [tokens],
        keys,
    )
    place, home_place, fill = call(
        functools.partial(place_kernel, rounds, devices, bound, token_count),
        [
            ((rounds * per_device, cap), f32),
            ((rounds * per_device, cap), f32),
            ((rounds * (per_device + 2), cap), f32),
        ],
        [tokens],
    )
    partner, low = call(
        functools.partial(index_kernel, rounds, devices, bound, token_count),
        [
            ((rounds, devices * table_kept(slots // lane), slots + cap), bf16),
            ((rounds * (per_device + 1), cap), f32),
        ],
        [tokens],
        [((rounds, 2 * devices * token_count // lane, lane), bf16)],
        far=(0,),
    )
    far_send = call(
        far_pack_kernel,
        [((span, 3 * size), bf16)] * half,
        [far_pick, far_rows],
        cost=50_000_000_000,
    )
    far_send, partner, tokens, home_place = lax.optimization_barrier(
        (far_send, partner, tokens, home_place)
    )
    far = [far_send[0]] + [crossed(far_send[at], half - at) for at in range(1, half)]
    spread_t, home_pick = call(
        functools.partial(return_index_kernel, rounds, devices, bound, token_count),
        [((rounds, buffer_rows, slots), bf16), ((token_count, devices * span), bf16)],
        [tokens, home_place],
        [pick] + keys,
        far=(0, 1),
    )
    far, spread_t, home_pick = lax.optimization_barrier((far, spread_t, home_pick))
    last, first = call(
        functools.partial(ends_kernel, rounds),
        [((rounds, cap, 2 * size), bf16)] * 2,
        [near, place] + far,
    )
    behind = shifted(last, 1)
    ahead = shifted(first, -1)
    square = (rounds, cap, cap)
    rows, units, prob, inner, first_score, first_inner_now, inner_sums = call(
        functools.partial(forward_inner_kernel, rounds),
        [
            ((rounds, per_device, cap, 3 * size), bf16),
            ((rounds, per_device, cap, size), bf16),
            ((rounds, per_device - 1, 2 * cap, cap), bf16),
            ((rounds, per_device - 1, 2 * cap, cap), bf16),
            (square, f32),
            (square, f32),
            ((sum_rows, cap), f32),
        ],
        [fill, near, place, last, first] + far,
    )
    behind_unit, first_prob, first_inner, sums, sums_send = call(
        functools.partial(forward_first_kernel, rounds, devices),
        [
            ((rounds, cap, size), bf16),
            ((rounds, 2 * cap, cap), bf16),
            ((rounds, 2 * cap, cap), bf16),
            ((sum_rows, cap), f32),
            ((devices, sum_rows * cap // lane, lane), f32),
        ],
        [fill, rows, behind, first_score, first_inner_now, inner_sums],
        [((sum_rows * cap // lane, lane), f32)],
    )
    sums_send, ahead = lax.optimization_barrier((sums_send, ahead))
    everyone = exchange(sums_send)
    (grads_send,) = call(
        functools.partial(backward_kernel, rounds, devices, bound),
        [((devices, span, 2 * size), bf16)],
        [
            fill,
            everyone,
            partner,
            low,
            sums,
            rows,
            ahead,
            units,
            behind_unit,
            first_prob,
            first_inner,
            prob,
            inner,
            spread_t,
        ],
        [((rounds, slots, 2 * size), bf16)],
    )
    home = exchange(grads_send.reshape(devices * span, 2 * size))
    return call(
        home_kernel,
        [((token_count, size), bf16), ((token_count, size), bf16)],
        [home_pick, home],
    )


def on_device(qk, values, grad_out, members, counts):
    grad_qk, grad_v = head_backward(qk[0], values[0], grad_out[0], members[0], counts[0])
    return (grad_qk[None], grad_v[None])


def solution(mesh):
    in_specs = (
        P("head", "seq", None),
        P("head", "seq", None),
        P("head", "seq", None),
        P("head", None, None, None),
        P("head", None, None),
    )
    out_specs = (P("head", "seq", None), P("head", "seq", None))
    return jax.shard_map(
        on_device, mesh=mesh, in_specs=in_specs, out_specs=out_specs, check_vma=False
    )
```

```python
import functools
import math

import jax
import jax.numpy as jnp
from jax import lax
from jax.experimental import pallas as pl
from jax.experimental.pallas import tpu as pltpu
from jax.sharding import PartitionSpec as P

masked_score = -1e30
norm_eps = 1e-06
lane = 128
f32 = jnp.float32
bf16 = jnp.bfloat16


def iota(shape, axis):
    return lax.broadcasted_iota(jnp.int32, shape, axis)


def float_iota(shape, axis):
    return iota(shape, axis).astype(f32)


def dot_nn(a, b):
    return lax.dot_general(a, b, (((1,), (0,)), ((), ())), preferred_element_type=f32)


def dot_nt(a, b):
    return lax.dot_general(a, b, (((1,), (1,)), ((), ())), preferred_element_type=f32)


def dot_tn(a, b):
    return lax.dot_general(a, b, (((0,), (0,)), ((), ())), preferred_element_type=f32)


def one_hot(condition):
    return jnp.where(condition, 1.0, 0.0).astype(bf16)


def short_hot(index, shape, axis):
    place = iota(shape, axis).astype(jnp.int16)
    short = jnp.broadcast_to(index.astype(jnp.int32), shape).astype(jnp.int16)
    return jnp.where(short == place, jnp.ones(shape, bf16), jnp.zeros(shape, bf16))


def block_of(device, devices):
    if devices % 4:
        return device
    depth = devices // 4
    level, column = device // 4, device % 4
    turn = column ^ (column >> 1)
    step = level + (turn % 2) * (depth - 1 - 2 * level)
    return turn * depth + step


def device_of(block, devices):
    if devices % 4:
        return block
    depth = devices // 4
    turn, step = block // depth, block % depth
    level = step + (turn % 2) * (depth - 1 - 2 * step)
    return level * 4 + (turn ^ (turn >> 1))


def earlier(size):
    return one_hot(iota((size, size), 0) < iota((size, size), 1))


def call(
    kernel,
    out_shapes,
    operands,
    scratch=(),
    remote=0,
    semaphores=0,
    far=(),
    direct=(),
    cost=0,
):
    count = len(operands)
    held = sum(array.size * array.dtype.itemsize for array in operands[: count - remote])
    for shape, dtype in list(out_shapes) + list(scratch):
        held += math.prod(shape) * jnp.dtype(dtype).itemsize
    spaces = [pltpu.VMEM] * (count - remote) + [pltpu.HBM] * remote
    operands = [
        pltpu.with_memory_space_constraint(array, space) if space is pltpu.HBM else array
        for array, space in zip(operands, spaces)
    ]
    return pl.pallas_call(
        kernel,
        out_shape=tuple(
            pltpu.HBM(shape, dtype) if at in far else jax.ShapeDtypeStruct(shape, dtype)
            for at, (shape, dtype) in enumerate(out_shapes)
        ),
        in_specs=[pl.BlockSpec(memory_space=space) for space in spaces],
        out_specs=tuple(
            pl.BlockSpec(memory_space=pltpu.HBM if at in direct else pltpu.VMEM)
            for at in range(len(out_shapes))
        ),
        scratch_shapes=[pltpu.VMEM(shape, dtype) for shape, dtype in scratch]
        + [pltpu.SemaphoreType.DMA((semaphores,))] * min(semaphores, 1),
        cost_estimate=pl.CostEstimate(flops=cost, transcendentals=0, bytes_accessed=0),
        compiler_params=pltpu.CompilerParams(vmem_limit_bytes=held + 12 * 1024 * 1024),
    )(*operands)


def slot_tokens(members_ref, counts_ref, devices, group):
    rounds, groups = counts_ref.shape
    per_device = groups // devices
    rows = pl.ds(group, rounds * devices, stride=per_device)
    parts = [members_ref[half, rows, :] for half in range(members_ref.shape[0])]
    listed = jnp.concatenate(parts, axis=1)
    diagonal = iota((devices, groups), 1) == iota((devices, groups), 0) * per_device + group
    limits = [
        jnp.sum(
            jnp.where(diagonal, counts_ref[r : r + 1, :].astype(f32), 0.0), axis=1, keepdims=True
        )
        for r in range(rounds)
    ]
    limit = jnp.concatenate(limits, axis=0)
    return jnp.where(float_iota(listed.shape, 1) < limit, listed, -1)


def rank_slots(rounds, devices, token_count, source, tokens_ref, key_ref, value_ref):
    per_device, _, cap = key_ref.shape
    start = source * token_count
    before = earlier(cap)
    carry = jnp.zeros((rounds * devices, 1), f32)
    for group in range(per_device):
        local = tokens_ref[group] - start
        owned = (local >= 0) & (local < token_count)
        rank = dot_nn(one_hot(owned), before) + carry
        carry = carry + jnp.sum(jnp.where(owned, 1.0, 0.0), axis=1, keepdims=True)
        key_ref[group] = jnp.where(owned, rank, -1.0)
        value_ref[group] = jnp.where(owned, local + 1, 0).astype(f32)


def pick_rows(rounds, devices, bound, block, token_count, key_ref, value_ref):
    per_device, _, cap = key_ref.shape
    column = float_iota((bound, cap), 0)
    picks = []
    for r in range(rounds):
        row = r * devices + block
        total = jnp.zeros((bound, cap), f32)
        for group in range(per_device):
            ranks = key_ref[group, pl.ds(row, 1), :]
            values = value_ref[group, pl.ds(row, 1), :]
            total = total + jnp.where(ranks == column, values, 0.0)
        index = jnp.sum(total, axis=1, keepdims=True) - 1.0
        picks.append(short_hot(index, (bound, token_count), 1))
    return jnp.concatenate(picks, axis=0)


def join_kernel(q_hbm, v_hbm, g_hbm, joined_ref, sems):
    size = q_hbm.shape[1]
    copies = []
    for at, source in enumerate((q_hbm, v_hbm, g_hbm)):
        target = joined_ref.at[:, pl.ds(at * size, size)]
        copies.append(pltpu.make_async_copy(source, target, sems.at[at]))
    for copy in copies:
        copy.start()
    for copy in copies:
        copy.wait()


def pack_kernel(
    rounds,
    devices,
    bound,
    joined_ref,
    counts_hbm,
    members_hbm,
    send_hbm,
    tokens_ref,
    packed_ref,
    key_ref,
    value_ref,
    counts_ref,
    members_ref,
    sems,
):
    token_count = joined_ref.shape[0]
    halves = members_ref.shape[0]
    copies = [pltpu.make_async_copy(counts_hbm, counts_ref, sems.at[halves])]
    for half in range(halves):
        source = members_hbm.at[:, pl.ds(half * lane, lane)]
        target = members_ref.at[half, pl.ds(0, members_hbm.shape[0])]
        copies.append(pltpu.make_async_copy(source, target, sems.at[half]))
    for copy in copies:
        copy.start()
    for copy in copies:
        copy.wait()
    for group in range(tokens_ref.shape[0]):
        tokens_ref[group] = slot_tokens(members_ref, counts_ref, devices, group)
    me = lax.axis_index("seq")
    rank_slots(rounds, devices, token_count, me, tokens_ref, key_ref, value_ref)
    half = devices // 2
    first = me // half * half
    parts = 4
    step = half // parts
    sends = []
    for part in range(parts):
        picks = [
            pick_rows(
                rounds,
                devices,
                bound,
                block_of(first + at, devices),
                token_count,
                key_ref,
                value_ref,
            )
            for at in range(part * step, (part + 1) * step)
        ]
        span = pl.ds(part * step * rounds * bound, step * rounds * bound)
        packed_ref[span, :] = dot_nn(jnp.concatenate(picks, axis=0), joined_ref[...]).astype(bf16)
        copy = pltpu.make_async_copy(
            packed_ref.at[span, :], send_hbm.at[span, :], sems.at[halves + 1 + part]
        )
        copy.start()
        sends.append(copy)
    for copy in sends:
        copy.wait()


def far_pick_kernel(rounds, devices, bound, token_count, tokens_ref, pick_ref, key_ref, value_ref):
    me = lax.axis_index("seq")
    half = devices // 2
    first = me // half * half
    source = lax.rem(me + half, devices)
    rank_slots(rounds, devices, token_count, source, tokens_ref, key_ref, value_ref)
    size = rounds * bound
    for at in range(half):
        block = block_of(first + jnp.bitwise_xor(me - first, -at % half), devices)
        pick_ref[at * size : (at + 1) * size, :] = pick_rows(
            rounds, devices, bound, block, token_count, key_ref, value_ref
        )


def far_pack_kernel(pick_ref, rows_ref, *send_refs):
    rows = rows_ref[...]
    span = send_refs[0].shape[0]
    parts = 4
    count = len(send_refs) // parts
    for part in range(parts):
        first = part * count
        packed = dot_nn(pick_ref[pl.ds(first * span, count * span), :], rows).astype(bf16)
        for at in range(count):
            send_refs[first + at][...] = packed[at * span : (at + 1) * span]


def place_kernel(rounds, devices, bound, token_count, tokens_ref, place_ref, home_place_ref, fill_ref):
    per_device, _, cap = tokens_ref.shape
    seat = lax.axis_index("seq")
    me = block_of(seat, devices)
    half = devices // 2
    before = earlier(cap)
    source = iota((devices, cap), 0)
    source_start = source * token_count
    home_place = source.astype(f32) * bound + 1.0
    first = seat // half * half
    near = (source >= first) & (source < first + half)
    bits = jnp.bitwise_xor(source % half, seat - first)
    crossed = half + jnp.where(bits > 0, half - bits, 0)
    source_place = jnp.where(near, source - first, crossed).astype(f32) * bound + 1.0
    for r in range(rounds):
        carry = jnp.zeros((devices, 1), f32)
        for group in range(per_device):
            tokens = tokens_ref[group, pl.ds(r * devices + me, 1), :]
            owned = (tokens >= source_start) & (tokens < source_start + token_count)
            rank = dot_nn(one_hot(owned), before) + carry
            carry = carry + jnp.sum(jnp.where(owned, 1.0, 0.0), axis=1, keepdims=True)
            for target, base in ((place_ref, source_place), (home_place_ref, home_place)):
                place = jnp.sum(jnp.where(owned, rank + base, 0.0), axis=0, keepdims=True) - 1.0
                row = r * per_device + group
                target[row : row + 1, :] = place
    after = lax.rem(me + 1, devices)
    behind = lax.rem(me + devices - 1, devices)
    for r in range(rounds):
        for at in range(per_device + 2):
            block = behind if at == 0 else after if at > per_device else me
            group = (at - 1) % per_device
            tokens = tokens_ref[group, pl.ds(r * devices + block, 1), :]
            fill = jnp.sum(jnp.where(tokens >= 0, 1.0, 0.0), axis=1, keepdims=True)
            row = r * (per_device + 2) + at
            fill_ref[row : row + 1, :] = jnp.broadcast_to(fill, (1, cap))


def index_kernel(
    rounds,
    devices,
    bound,
    token_count,
    tokens_ref,
    partner_ref,
    low_ref,
    table_ref,
):
    per_device, _, cap = tokens_ref.shape
    me = block_of(lax.axis_index("seq"), devices)
    after = lax.rem(me + 1, devices)
    high_count = devices * token_count // lane
    high_start = iota((high_count, cap), 0) * lane
    low_index = iota((lane, cap), 0)
    slot = float_iota((high_count, cap), 1)

    def split(tokens):
        high = (tokens >= high_start) & (tokens < high_start + lane)
        low = jnp.bitwise_and(tokens, lane - 1) == low_index
        return high, low

    for r in range(rounds):

        def one_block(block, total):
            device = device_of(block, devices)
            for group in range(per_device):
                tokens = tokens_ref[group, pl.ds(r * devices + block, 1), :]
                high, low = split(tokens)
                group_index = (device * per_device + group).astype(f32)
                sides = jnp.concatenate(
                    [
                        jnp.where(high, group_index, 0.0).astype(bf16),
                        jnp.where(high, slot, 0.0).astype(bf16),
                    ],
                    axis=0,
                )
                total = total + dot_nt(sides, one_hot(low))
            return total

        total = lax.fori_loop(
            0, devices, one_block, jnp.zeros((2 * high_count, lane), f32), unroll=2
        )
        table_ref[r] = total.astype(bf16)

    halves = cap // lane
    kept = table_kept(per_device * halves)
    row_column = float_iota((devices * kept, cap), 0)
    for r in range(rounds):
        other = 1 - r
        for group in range(per_device + 1):
            if group < per_device:
                tokens = tokens_ref[group, pl.ds(r * devices + me, 1), :]
            else:
                tokens = tokens_ref[0, pl.ds(r * devices + after, 1), :]
            high, low = split(tokens)
            high_hot = one_hot(high)
            found = []
            for part in range(2):
                table = table_ref[other, part * high_count : (part + 1) * high_count, :]
                picked = dot_tn(table, high_hot)
                found.append(jnp.sum(jnp.where(low, picked, 0.0), axis=0, keepdims=True))
            group_index, position = found
            device = jnp.floor((group_index + 0.5) * (1.0 / per_device))
            half = jnp.floor((position + 0.5) * (1.0 / lane))
            row = device * kept + (group_index - device * per_device) * halves + half
            span = pl.ds(group * cap, cap)
            partner_ref[r, :, span] = one_hot(row == row_column)
            low_ref[pl.ds(r * (per_device + 1) + group, 1), :] = position - half * lane


def return_index_kernel(
    rounds,
    devices,
    bound,
    token_count,
    tokens_ref,
    home_place_ref,
    spread_t_ref,
    home_ref,
    pick_ref,
    key_ref,
    value_ref,
):
    per_device, _, cap = tokens_ref.shape
    place_column = float_iota((devices * bound, cap), 0)
    for r in range(rounds):
        for group in range(per_device):
            row = r * per_device + group
            place = home_place_ref[row : row + 1, :]
            spread_t_ref[r, :, pl.ds(group * cap, cap)] = one_hot(place == place_column)
    seat = lax.axis_index("seq")
    rank_slots(rounds, devices, token_count, seat, tokens_ref, key_ref, value_ref)

    size = rounds * bound
    for device in range(devices):
        pick_ref[device * size : (device + 1) * size, :] = pick_rows(
            rounds, devices, bound, block_of(device, devices), token_count, key_ref, value_ref
        )
    home_ref[...] = jnp.transpose(pick_ref[...])


def table_kept(count):
    return (count + 7) // 8 * 8


def spread_of(place_ref, r, group, rounds, buffer_rows):
    row = r * (place_ref.shape[0] // rounds) + group
    cap = place_ref.shape[1]
    return short_hot(place_ref[row : row + 1, :], (buffer_rows, cap), 0)


def received_rows(near_ref, far_refs, r, rounds):
    half, span, width = near_ref.shape
    bound = span // rounds
    rows = slice(r * bound, (r + 1) * bound)
    parts = [near_ref[:, rows, :].reshape(half * bound, width)]
    parts += [far_ref[rows, :] for far_ref in far_refs]
    return jnp.concatenate(parts, axis=0)


def ends_kernel(rounds, near_ref, place_ref, *refs):
    far_refs, (last_ref, first_ref) = refs[:-2], refs[-2:]
    size = near_ref.shape[2] // 3
    per_device = place_ref.shape[0] // rounds
    for r in range(rounds):
        received = received_rows(near_ref, far_refs, r, rounds)
        spread = spread_of(place_ref, r, per_device - 1, rounds, received.shape[0])
        last_ref[r] = dot_tn(spread, received[:, : 2 * size]).astype(bf16)
        spread = spread_of(place_ref, r, 0, rounds, received.shape[0])
        wanted = jnp.concatenate([received[:, :size], received[:, 2 * size :]], axis=1)
        first_ref[r] = dot_tn(spread, wanted).astype(bf16)


def inverse_norm(rows):
    wide = rows.astype(f32)
    return lax.rsqrt(jnp.sum(wide * wide, axis=1, keepdims=True) + norm_eps)


def unit_rows(rows):
    return (rows.astype(f32) * inverse_norm(rows)).astype(bf16)


def fill_row(fill_ref, r, at, rounds):
    row = r * (fill_ref.shape[0] // rounds) + at
    return fill_ref[row : row + 1, :]


def scored(unit, queries, fill, own):
    cap = queries.shape[0]
    key = float_iota((cap, cap), 0)
    allowed = key < fill
    if own:
        allowed = allowed & (key != float_iota((cap, cap), 1))
    return jnp.where(allowed, dot_nt(unit, queries), masked_score)


def normalised(scores, inners):
    highest = jnp.maximum(
        jnp.max(scores[0], axis=0, keepdims=True), jnp.max(scores[1], axis=0, keepdims=True)
    )
    exps = [jnp.exp(score - highest) for score in scores]
    total = jnp.sum(exps[0], axis=0, keepdims=True) + jnp.sum(exps[1], axis=0, keepdims=True)
    inverse = 1.0 / total
    probs = [part * inverse for part in exps]
    dots = jnp.sum(probs[0] * inners[0], axis=0, keepdims=True) + jnp.sum(
        probs[1] * inners[1], axis=0, keepdims=True
    )
    centred = [(inner - dots).astype(bf16) for inner in inners]
    return highest + jnp.log(total), dots, [prob.astype(bf16) for prob in probs], centred


def forward_inner_kernel(
    rounds,
    fill_ref,
    near_ref,
    place_ref,
    last_ref,
    first_ref,
    *refs,
):
    far_refs, refs = refs[:-7], refs[-7:]
    rows_ref, units_ref, prob_ref, inner_ref, first_score_ref, first_inner_ref, sums_ref = refs
    cap = prob_ref.shape[3]
    per_device = rows_ref.shape[1]
    size = rows_ref.shape[3] // 3
    for r in range(rounds):
        received = received_rows(near_ref, far_refs, r, rounds)
        for group in range(per_device):
            spread = spread_of(place_ref, r, group, rounds, received.shape[0])
            if group == 0:
                values = dot_tn(spread, received[:, size : 2 * size]).astype(bf16)
                rows_ref[r, group, :, :size] = first_ref[r, :, :size]
                rows_ref[r, group, :, size : 2 * size] = values
                rows_ref[r, group, :, 2 * size :] = first_ref[r, :, size:]
            elif group < per_device - 1:
                rows_ref[r, group] = dot_tn(spread, received).astype(bf16)
            else:
                rows_ref[r, group, :, : 2 * size] = last_ref[r]
                cots = dot_tn(spread, received[:, 2 * size :]).astype(bf16)
                rows_ref[r, group, :, 2 * size :] = cots
        units = [unit_rows(rows_ref[r, group, :, :size]) for group in range(per_device)]
        for group in range(per_device):
            units_ref[r, group] = units[group]
        for group in range(per_device):
            queries = rows_ref[r, group, :, :size]
            cot = rows_ref[r, group, :, 2 * size :]
            values = rows_ref[r, group, :, size : 2 * size]
            score_now = scored(
                units[group], queries, fill_row(fill_ref, r, group + 1, rounds), True
            )
            inner_now = dot_nt(values, cot)
            if group == 0:
                first_score_ref[r] = score_now
                first_inner_ref[r] = inner_now
                continue
            values = rows_ref[r, group - 1, :, size : 2 * size]
            inner_before = dot_nt(values, cot)
            score_before = scored(
                units[group - 1], queries, fill_row(fill_ref, r, group, rounds), False
            )
            inners = [inner_before, inner_now]
            log_total, dots, probs, centred = normalised([score_before, score_now], inners)
            for side in range(2):
                span = slice(side * cap, (side + 1) * cap)
                prob_ref[r, group - 1, span, :] = probs[side]
                inner_ref[r, group - 1, span, :] = centred[side]
            row = r * per_device + group
            sums_ref[row : row + 1, :] = log_total
            row = (rounds + r) * per_device + group
            sums_ref[row : row + 1, :] = dots


def forward_first_kernel(
    rounds,
    devices,
    fill_ref,
    rows_ref,
    behind_ref,
    score_ref,
    inner_now_ref,
    inner_sums_ref,
    unit_ref,
    prob_ref,
    inner_ref,
    sums_ref,
    send_ref,
    block_ref,
):
    cap = prob_ref.shape[2]
    per_device = rows_ref.shape[1]
    size = rows_ref.shape[3] // 3
    sums_ref[...] = inner_sums_ref[...]
    for r in range(rounds):
        behind_unit = unit_rows(behind_ref[r, :, :size])
        unit_ref[r] = behind_unit
        queries = rows_ref[r, 0, :, :size]
        cot = rows_ref[r, 0, :, 2 * size :]
        score_before = scored(behind_unit, queries, fill_row(fill_ref, r, 0, rounds), False)
        inners = [dot_nt(behind_ref[r, :, size:], cot), inner_now_ref[r]]
        log_total, dots, probs, centred = normalised([score_before, score_ref[r]], inners)
        for side in range(2):
            span = slice(side * cap, (side + 1) * cap)
            prob_ref[r, span, :] = probs[side]
            inner_ref[r, span, :] = centred[side]
        row = r * per_device
        sums_ref[row : row + 1, :] = log_total
        row = (rounds + r) * per_device
        sums_ref[row : row + 1, :] = dots
    halves = cap // lane
    count = per_device * halves
    for r in range(rounds):
        for kind in range(2):
            for group in range(per_device):
                row = (kind * rounds + r) * per_device + group
                for half in range(halves):
                    at = (2 * r + kind) * count + group * halves + half
                    block_ref[at : at + 1, :] = sums_ref[
                        row : row + 1, half * lane : (half + 1) * lane
                    ]
    block = block_ref[...]
    for device in range(devices):
        send_ref[device] = block


def key_grad(rows, unit_grad):
    wide = rows.astype(f32)
    inverse = inverse_norm(rows)
    along = jnp.sum(wide * unit_grad, axis=1, keepdims=True)
    return inverse * unit_grad - wide * (inverse * inverse * inverse * along)


def three_parts(values):
    high = values.astype(bf16)
    rest = values - high.astype(f32)
    middle = rest.astype(bf16)
    return high, middle, (rest - middle.astype(f32)).astype(bf16)


def backward_kernel(
    rounds,
    devices,
    bound,
    fill_ref,
    everyone_ref,
    partner_ref,
    low_ref,
    sums_ref,
    rows_ref,
    ahead_ref,
    units_ref,
    behind_unit_ref,
    first_prob_ref,
    first_inner_ref,
    prob_ref,
    inner_ref,
    spread_t_ref,
    send_ref,
    grads_ref,
):
    cap = rows_ref.shape[2]
    per_device = rows_ref.shape[1]
    size = rows_ref.shape[3] // 3
    me = block_of(lax.axis_index("seq"), devices)
    ahead_device = device_of(lax.rem(me + 1, devices), devices)
    halves = cap // lane
    count = per_device * halves
    kept = table_kept(count)
    low_column = float_iota((lane, cap), 0)
    slot = float_iota((1, cap), 1)

    def sums_of_all(r, kind):
        start = (2 * r + kind) * count
        held = min(start, everyone_ref.shape[1] - kept)
        rows = everyone_ref[:, held : held + kept, :]
        if start > held:
            rows = jnp.concatenate(
                [rows[:, start - held :], jnp.zeros((devices, start - held, lane), f32)], axis=1
            )
        return jnp.transpose(rows.reshape(devices * kept, lane))

    def ahead_sums(r, kind):
        start = (2 * r + kind) * count
        rows = [everyone_ref[ahead_device, start + h : start + h + 1, :] for h in range(halves)]
        return jnp.concatenate(rows, axis=1)

    def scales_of(r):
        logs = three_parts(sums_of_all(1 - r, 0))
        dots = three_parts(sums_of_all(1 - r, 1))
        upright = jnp.concatenate(logs + dots[:2], axis=0)
        picked = dot_nn(upright, partner_ref[r])
        picked_log = picked[:lane] + (picked[lane : 2 * lane] + picked[2 * lane : 3 * lane])
        picked_dot = picked[3 * lane : 4 * lane] + picked[4 * lane :]
        scales = []
        for group in range(per_device + 1):
            at = r * (per_device + 1) + group
            here = low_ref[at : at + 1, :] == low_column
            span = slice(group * cap, (group + 1) * cap)
            other_log = jnp.sum(jnp.where(here, picked_log[:, span], 0.0), axis=0, keepdims=True)
            other_dot = jnp.sum(jnp.where(here, picked_dot[:, span], 0.0), axis=0, keepdims=True)
            if group < per_device:
                row = r * per_device + group
                own_log = sums_ref[row : row + 1, :]
                own_dot = sums_ref[rounds * per_device + row : rounds * per_device + row + 1, :]
            else:
                own_log = ahead_sums(r, 0)
                own_dot = ahead_sums(r, 1)
            weight = 1.0 / (1.0 + jnp.exp(other_log - own_log))
            other_weight = 1.0 / (1.0 + jnp.exp(own_log - other_log))
            shift = other_weight * (own_dot - other_dot)
            valid = slot < fill_row(fill_ref, r, group + 1, rounds)
            scales.append((jnp.where(valid, weight, 0.0), jnp.where(valid, shift, 0.0)))
        return scales

    def score_grads(prob, inner, scale):
        weighted = prob.astype(f32) * scale[0]
        score_grad = (weighted * (inner.astype(f32) + scale[1])).astype(bf16)
        return weighted.astype(bf16), score_grad

    aheads = []
    for r in range(rounds):
        queries = ahead_ref[r, :, :size]
        cot = ahead_ref[r, :, size:]
        fill = fill_row(fill_ref, r, per_device, rounds)
        score = scored(units_ref[r, per_device - 1], queries, fill, False)
        inner = dot_nt(rows_ref[r, per_device - 1, :, size : 2 * size], cot)
        aheads.append(([jnp.exp(score - ahead_sums(r, 0))], [inner - ahead_sums(r, 1)]))
    scales = [scales_of(r) for r in range(rounds)]
    carried = [None] * rounds
    for group in range(per_device + 1):
        for r in range(rounds):
            if group < per_device:
                queries = rows_ref[r, group, :, :size]
                cot = rows_ref[r, group, :, 2 * size :]
            else:
                queries = ahead_ref[r, :, :size]
                cot = ahead_ref[r, :, size:]
            if group == 0:
                probs = [first_prob_ref[r, :cap, :], first_prob_ref[r, cap:, :]]
                inners = [first_inner_ref[r, :cap, :], first_inner_ref[r, cap:, :]]
            elif group < per_device:
                probs = [prob_ref[r, group - 1, :cap, :], prob_ref[r, group - 1, cap:, :]]
                inners = [inner_ref[r, group - 1, :cap, :], inner_ref[r, group - 1, cap:, :]]
            else:
                probs, inners = aheads[r]
            scale = scales[r][group]
            weighted, score_grad = score_grads(probs[0], inners[0], scale)
            if group > 0:
                query_grad, unit_grad, value_grad = carried[r]
                unit_grad = unit_grad + dot_nn(score_grad, queries)
                value_grad = value_grad + dot_nn(weighted, cot)
                key_part = key_grad(rows_ref[r, group - 1, :, :size], unit_grad)
                span = slice((group - 1) * cap, group * cap)
                grads_ref[r, span, :size] = (query_grad + key_part).astype(bf16)
                grads_ref[r, span, size:] = value_grad.astype(bf16)
            if group < per_device:
                unit_before = behind_unit_ref[r] if group == 0 else units_ref[r, group - 1]
                query_grad = dot_tn(score_grad, unit_before)
                weighted, score_grad = score_grads(probs[1], inners[1], scale)
                query_grad = query_grad + dot_tn(score_grad, units_ref[r, group])
                unit_grad = dot_nn(score_grad, queries)
                carried[r] = (query_grad, unit_grad, dot_nn(weighted, cot))
    for r in range(rounds):
        packed = dot_nn(spread_t_ref[r], grads_ref[r]).astype(bf16)
        send_ref[:, r * bound : (r + 1) * bound, :] = packed.reshape(devices, bound, 2 * size)


def home_kernel(home_ref, got_ref, qk_ref, value_ref):
    size = qk_ref.shape[1]
    total = dot_nn(home_ref[...], got_ref[...])
    qk_ref[...] = total[:, :size].astype(bf16)
    value_ref[...] = total[:, size:].astype(bf16)


def exchange_in_half(array):
    devices = lax.axis_size("seq")
    half = devices // 2
    halves = [list(range(half)), list(range(half, devices))]
    return lax.all_to_all(
        array, "seq", split_axis=0, concat_axis=0, tiled=True, axis_index_groups=halves
    )


def crossed(array, by):
    devices = lax.axis_size("seq")
    return lax.ppermute(array, "seq", [(i, i ^ by) for i in range(devices)])


def mirrored(array):
    devices = lax.axis_size("seq")
    half = devices // 2
    return lax.ppermute(array, "seq", [(i, (i + half) % devices) for i in range(devices)])


def exchange(array):
    return lax.all_to_all(array, "seq", split_axis=0, concat_axis=0, tiled=True)


def shifted(array, by):
    devices = lax.axis_size("seq")
    order = [device_of(block, devices) for block in range(devices)]
    return lax.ppermute(array, "seq", [(order[i], order[(i + by) % devices]) for i in range(devices)])


def head_backward(qk, values, cot, members, counts):
    devices = lax.axis_size("seq")
    token_count, size = qk.shape
    rounds, groups, cap = members.shape
    per_device = groups // devices
    slots = per_device * cap
    bound = 2 * token_count // devices
    span = rounds * bound
    buffer_rows = devices * bound
    sum_rows = 2 * rounds * per_device
    listed = members.reshape(rounds * groups, cap)
    keys = [((per_device, rounds * devices, cap), f32)] * 2
    pick = ((devices * span, token_count), bf16)
    half = devices // 2
    (joined,) = call(
        join_kernel,
        [((token_count, 3 * size), bf16)],
        [qk, values, cot],
        remote=3,
        semaphores=3,
    )
    far_rows = mirrored(joined)
    near_send, tokens = call(
        functools.partial(pack_kernel, rounds, devices, bound),
        [((half * span, 3 * size), bf16), (keys[0][0], jnp.int32)],
        [joined, counts, listed],
        [((half * span, 3 * size), bf16)]
        + keys
        + [
            (counts.shape, jnp.int32),
            ((cap // lane, rounds * groups + 8 * per_device, lane), jnp.int32),
        ],
        remote=2,
        semaphores=cap // lane + 5,
        far=(0,),
        direct=(0,),
    )
    near = exchange_in_half(near_send).reshape(half, span, 3 * size)
    (far_pick,) = call(
        functools.partial(far_pick_kernel, rounds, devices, bound, token_count),
        [((half * span, token_count), bf16)],
        [tokens],
        keys,
    )
    place, home_place, fill = call(
        functools.partial(place_kernel, rounds, devices, bound, token_count),
        [
            ((rounds * per_device, cap), f32),
            ((rounds * per_device, cap), f32),
            ((rounds * (per_device + 2), cap), f32),
        ],
        [tokens],
    )
    partner, low = call(
        functools.partial(index_kernel, rounds, devices, bound, token_count),
        [
            ((rounds, devices * table_kept(slots // lane), slots + cap), bf16),
            ((rounds * (per_device + 1), cap), f32),
        ],
        [tokens],
        [((rounds, 2 * devices * token_count // lane, lane), bf16)],
        far=(0,),
    )
    far_send = call(
        far_pack_kernel,
        [((span, 3 * size), bf16)] * half,
        [far_pick, far_rows],
        cost=50_000_000_000,
    )
    far_send, partner, tokens, home_place = lax.optimization_barrier(
        (far_send, partner, tokens, home_place)
    )
    far = [far_send[0]] + [crossed(far_send[at], half - at) for at in range(1, half)]
    spread_t, home_pick = call(
        functools.partial(return_index_kernel, rounds, devices, bound, token_count),
        [((rounds, buffer_rows, slots), bf16), ((token_count, devices * span), bf16)],
        [tokens, home_place],
        [pick] + keys,
        far=(0, 1),
    )
    far, spread_t, home_pick = lax.optimization_barrier((far, spread_t, home_pick))
    last, first = call(
        functools.partial(ends_kernel, rounds),
        [((rounds, cap, 2 * size), bf16)] * 2,
        [near, place] + far,
    )
    behind = shifted(last, 1)
    ahead = shifted(first, -1)
    square = (rounds, cap, cap)
    rows, units, prob, inner, first_score, first_inner_now, inner_sums = call(
        functools.partial(forward_inner_kernel, rounds),
        [
            ((rounds, per_device, cap, 3 * size), bf16),
            ((rounds, per_device, cap, size), bf16),
            ((rounds, per_device - 1, 2 * cap, cap), bf16),
            ((rounds, per_device - 1, 2 * cap, cap), bf16),
            (square, f32),
            (square, f32),
            ((sum_rows, cap), f32),
        ],
        [fill, near, place, last, first] + far,
    )
    behind_unit, first_prob, first_inner, sums, sums_send = call(
        functools.partial(forward_first_kernel, rounds, devices),
        [
            ((rounds, cap, size), bf16),
            ((rounds, 2 * cap, cap), bf16),
            ((rounds, 2 * cap, cap), bf16),
            ((sum_rows, cap), f32),
            ((devices, sum_rows * cap // lane, lane), f32),
        ],
        [fill, rows, behind, first_score, first_inner_now, inner_sums],
        [((sum_rows * cap // lane, lane), f32)],
    )
    sums_send, ahead = lax.optimization_barrier((sums_send, ahead))
    everyone = exchange(sums_send)
    (grads_send,) = call(
        functools.partial(backward_kernel, rounds, devices, bound),
        [((devices, span, 2 * size), bf16)],
        [
            fill,
            everyone,
            partner,
            low,
            sums,
            rows,
            ahead,
            units,
            behind_unit,
            first_prob,
            first_inner,
            prob,
            inner,
            spread_t,
        ],
        [((rounds, slots, 2 * size), bf16)],
    )
    home = exchange(grads_send.reshape(devices * span, 2 * size))
    return call(
        home_kernel,
        [((token_count, size), bf16), ((token_count, size), bf16)],
        [home_pick, home],
    )


def on_device(qk, values, grad_out, members, counts):
    grad_qk, grad_v = head_backward(qk[0], values[0], grad_out[0], members[0], counts[0])
    return (grad_qk[None], grad_v[None])


def solution(mesh):
    in_specs = (
        P("head", "seq", None),
        P("head", "seq", None),
        P("head", "seq", None),
        P("head", None, None, None),
        P("head", None, None),
    )
    out_specs = (P("head", "seq", None), P("head", "seq", None))
    return jax.shard_map(
        on_device, mesh=mesh, in_specs=in_specs, out_specs=out_specs, check_vma=False
    )
```

```python
import functools
import math

import jax
import jax.numpy as jnp
from jax import lax
from jax.experimental import pallas as pl
from jax.experimental.pallas import tpu as pltpu
from jax.sharding import PartitionSpec as P

masked_score = -1e30
norm_eps = 1e-06
lane = 128
f32 = jnp.float32
bf16 = jnp.bfloat16


def iota(shape, axis):
    return lax.broadcasted_iota(jnp.int32, shape, axis)


def float_iota(shape, axis):
    return iota(shape, axis).astype(f32)


def dot_nn(a, b):
    return lax.dot_general(a, b, (((1,), (0,)), ((), ())), preferred_element_type=f32)


def dot_nt(a, b):
    return lax.dot_general(a, b, (((1,), (1,)), ((), ())), preferred_element_type=f32)


def dot_tn(a, b):
    return lax.dot_general(a, b, (((0,), (0,)), ((), ())), preferred_element_type=f32)


def one_hot(condition):
    return jnp.where(condition, 1.0, 0.0).astype(bf16)


def short_hot(index, shape, axis):
    place = iota(shape, axis).astype(jnp.int16)
    short = jnp.broadcast_to(index.astype(jnp.int32), shape).astype(jnp.int16)
    return jnp.where(short == place, jnp.ones(shape, bf16), jnp.zeros(shape, bf16))


def block_of(device, devices):
    if devices % 4:
        return device
    depth = devices // 4
    level, column = device // 4, device % 4
    turn = column ^ (column >> 1)
    step = level + (turn % 2) * (depth - 1 - 2 * level)
    return turn * depth + step


def device_of(block, devices):
    if devices % 4:
        return block
    depth = devices // 4
    turn, step = block // depth, block % depth
    level = step + (turn % 2) * (depth - 1 - 2 * step)
    return level * 4 + (turn ^ (turn >> 1))


def earlier(size):
    return one_hot(iota((size, size), 0) < iota((size, size), 1))


def call(
    kernel,
    out_shapes,
    operands,
    scratch=(),
    remote=0,
    semaphores=0,
    far=(),
    direct=(),
    cost=0,
):
    count = len(operands)
    held = sum(array.size * array.dtype.itemsize for array in operands[: count - remote])
    for shape, dtype in list(out_shapes) + list(scratch):
        held += math.prod(shape) * jnp.dtype(dtype).itemsize
    spaces = [pltpu.VMEM] * (count - remote) + [pltpu.HBM] * remote
    operands = [
        pltpu.with_memory_space_constraint(array, space) if space is pltpu.HBM else array
        for array, space in zip(operands, spaces)
    ]
    return pl.pallas_call(
        kernel,
        out_shape=tuple(
            pltpu.HBM(shape, dtype) if at in far else jax.ShapeDtypeStruct(shape, dtype)
            for at, (shape, dtype) in enumerate(out_shapes)
        ),
        in_specs=[pl.BlockSpec(memory_space=space) for space in spaces],
        out_specs=tuple(
            pl.BlockSpec(memory_space=pltpu.HBM if at in direct else pltpu.VMEM)
            for at in range(len(out_shapes))
        ),
        scratch_shapes=[pltpu.VMEM(shape, dtype) for shape, dtype in scratch]
        + [pltpu.SemaphoreType.DMA((semaphores,))] * min(semaphores, 1),
        cost_estimate=pl.CostEstimate(flops=cost, transcendentals=0, bytes_accessed=0),
        compiler_params=pltpu.CompilerParams(vmem_limit_bytes=held + 12 * 1024 * 1024),
    )(*operands)


def slot_tokens(members_ref, counts_ref, devices, group):
    rounds, groups = counts_ref.shape
    per_device = groups // devices
    rows = pl.ds(group, rounds * devices, stride=per_device)
    parts = [members_ref[half, rows, :] for half in range(members_ref.shape[0])]
    listed = jnp.concatenate(parts, axis=1)
    diagonal = iota((devices, groups), 1) == iota((devices, groups), 0) * per_device + group
    limits = [
        jnp.sum(
            jnp.where(diagonal, counts_ref[r : r + 1, :].astype(f32), 0.0), axis=1, keepdims=True
        )
        for r in range(rounds)
    ]
    limit = jnp.concatenate(limits, axis=0)
    return jnp.where(float_iota(listed.shape, 1) < limit, listed, -1)


def rank_slots(rounds, devices, token_count, source, tokens_ref, key_ref, value_ref):
    per_device, _, cap = key_ref.shape
    start = source * token_count
    before = earlier(cap)
    carry = jnp.zeros((rounds * devices, 1), f32)
    for group in range(per_device):
        local = tokens_ref[group] - start
        owned = (local >= 0) & (local < token_count)
        rank = dot_nn(one_hot(owned), before) + carry
        carry = carry + jnp.sum(jnp.where(owned, 1.0, 0.0), axis=1, keepdims=True)
        key_ref[group] = jnp.where(owned, rank, -1.0)
        value_ref[group] = jnp.where(owned, local + 1, 0).astype(f32)


def pick_rows(rounds, devices, bound, block, token_count, key_ref, value_ref):
    per_device, _, cap = key_ref.shape
    column = float_iota((bound, cap), 0)
    picks = []
    for r in range(rounds):
        row = r * devices + block
        total = jnp.zeros((bound, cap), f32)
        for group in range(per_device):
            ranks = key_ref[group, pl.ds(row, 1), :]
            values = value_ref[group, pl.ds(row, 1), :]
            total = total + jnp.where(ranks == column, values, 0.0)
        index = jnp.sum(total, axis=1, keepdims=True) - 1.0
        picks.append(short_hot(index, (bound, token_count), 1))
    return jnp.concatenate(picks, axis=0)


def join_kernel(q_hbm, v_hbm, g_hbm, joined_ref, sems):
    size = q_hbm.shape[1]
    copies = []
    for at, source in enumerate((q_hbm, v_hbm, g_hbm)):
        target = joined_ref.at[:, pl.ds(at * size, size)]
        copies.append(pltpu.make_async_copy(source, target, sems.at[at]))
    for copy in copies:
        copy.start()
    for copy in copies:
        copy.wait()


def pack_kernel(
    rounds,
    devices,
    bound,
    joined_ref,
    counts_hbm,
    members_hbm,
    send_hbm,
    tokens_ref,
    packed_ref,
    key_ref,
    value_ref,
    counts_ref,
    members_ref,
    sems,
):
    token_count = joined_ref.shape[0]
    halves = members_ref.shape[0]
    copies = [pltpu.make_async_copy(counts_hbm, counts_ref, sems.at[halves])]
    for half in range(halves):
        source = members_hbm.at[:, pl.ds(half * lane, lane)]
        target = members_ref.at[half, pl.ds(0, members_hbm.shape[0])]
        copies.append(pltpu.make_async_copy(source, target, sems.at[half]))
    for copy in copies:
        copy.start()
    for copy in copies:
        copy.wait()
    for group in range(tokens_ref.shape[0]):
        tokens_ref[group] = slot_tokens(members_ref, counts_ref, devices, group)
    me = lax.axis_index("seq")
    rank_slots(rounds, devices, token_count, me, tokens_ref, key_ref, value_ref)
    half = devices // 2
    first = me // half * half
    parts = 4
    step = half // parts
    sends = []
    for part in range(parts):
        picks = [
            pick_rows(
                rounds,
                devices,
                bound,
                block_of(first + at, devices),
                token_count,
                key_ref,
                value_ref,
            )
            for at in range(part * step, (part + 1) * step)
        ]
        span = pl.ds(part * step * rounds * bound, step * rounds * bound)
        packed_ref[span, :] = dot_nn(jnp.concatenate(picks, axis=0), joined_ref[...]).astype(bf16)
        copy = pltpu.make_async_copy(
            packed_ref.at[span, :], send_hbm.at[span, :], sems.at[halves + 1 + part]
        )
        copy.start()
        sends.append(copy)
    for copy in sends:
        copy.wait()


def bits_at(at, half):
    plane = half // 2
    if at == 0:
        return 0
    return half - at if at <= plane else at - plane


def far_pick_kernel(rounds, devices, bound, token_count, tokens_ref, pick_ref, key_ref, value_ref):
    me = lax.axis_index("seq")
    half = devices // 2
    first = me // half * half
    source = lax.rem(me + half, devices)
    rank_slots(rounds, devices, token_count, source, tokens_ref, key_ref, value_ref)
    size = rounds * bound
    for at in range(half):
        block = block_of(first + jnp.bitwise_xor(me - first, bits_at(at, half)), devices)
        pick_ref[at * size : (at + 1) * size, :] = pick_rows(
            rounds, devices, bound, block, token_count, key_ref, value_ref
        )


def far_pack_kernel(pick_ref, rows_ref, *send_refs):
    rows = rows_ref[...]
    span = send_refs[0].shape[0]
    parts = 4
    count = len(send_refs) // parts
    for part in range(parts):
        first = part * count
        packed = dot_nn(pick_ref[pl.ds(first * span, count * span), :], rows).astype(bf16)
        for at in range(count):
            send_refs[first + at][...] = packed[at * span : (at + 1) * span]


def place_kernel(rounds, devices, bound, token_count, tokens_ref, place_ref, home_place_ref, fill_ref):
    per_device, _, cap = tokens_ref.shape
    seat = lax.axis_index("seq")
    me = block_of(seat, devices)
    half = devices // 2
    before = earlier(cap)
    source = iota((devices, cap), 0)
    source_start = source * token_count
    home_place = source.astype(f32) * bound + 1.0
    first = seat // half * half
    near = (source >= first) & (source < first + half)
    bits = jnp.bitwise_xor(source % half, seat - first)
    plane = half // 2
    order = jnp.where(bits < plane, bits + plane, half - bits)
    crossed = half + jnp.where(bits > 0, order, 0)
    source_place = jnp.where(near, source - first, crossed).astype(f32) * bound + 1.0
    for r in range(rounds):
        carry = jnp.zeros((devices, 1), f32)
        for group in range(per_device):
            tokens = tokens_ref[group, pl.ds(r * devices + me, 1), :]
            owned = (tokens >= source_start) & (tokens < source_start + token_count)
            rank = dot_nn(one_hot(owned), before) + carry
            carry = carry + jnp.sum(jnp.where(owned, 1.0, 0.0), axis=1, keepdims=True)
            for target, base in ((place_ref, source_place), (home_place_ref, home_place)):
                place = jnp.sum(jnp.where(owned, rank + base, 0.0), axis=0, keepdims=True) - 1.0
                row = r * per_device + group
                target[row : row + 1, :] = place
    after = lax.rem(me + 1, devices)
    behind = lax.rem(me + devices - 1, devices)
    for r in range(rounds):
        for at in range(per_device + 2):
            block = behind if at == 0 else after if at > per_device else me
            group = (at - 1) % per_device
            tokens = tokens_ref[group, pl.ds(r * devices + block, 1), :]
            fill = jnp.sum(jnp.where(tokens >= 0, 1.0, 0.0), axis=1, keepdims=True)
            row = r * (per_device + 2) + at
            fill_ref[row : row + 1, :] = jnp.broadcast_to(fill, (1, cap))


def index_kernel(
    rounds,
    devices,
    bound,
    token_count,
    tokens_ref,
    partner_ref,
    low_ref,
    table_ref,
):
    per_device, _, cap = tokens_ref.shape
    me = block_of(lax.axis_index("seq"), devices)
    after = lax.rem(me + 1, devices)
    high_count = devices * token_count // lane
    high_start = iota((high_count, cap), 0) * lane
    low_index = iota((lane, cap), 0)
    slot = float_iota((high_count, cap), 1)

    def split(tokens):
        high = (tokens >= high_start) & (tokens < high_start + lane)
        low = jnp.bitwise_and(tokens, lane - 1) == low_index
        return high, low

    for r in range(rounds):

        def one_block(block, total):
            device = device_of(block, devices)
            for group in range(per_device):
                tokens = tokens_ref[group, pl.ds(r * devices + block, 1), :]
                high, low = split(tokens)
                group_index = (device * per_device + group).astype(f32)
                sides = jnp.concatenate(
                    [
                        jnp.where(high, group_index, 0.0).astype(bf16),
                        jnp.where(high, slot, 0.0).astype(bf16),
                    ],
                    axis=0,
                )
                total = total + dot_nt(sides, one_hot(low))
            return total

        total = lax.fori_loop(
            0, devices, one_block, jnp.zeros((2 * high_count, lane), f32), unroll=2
        )
        table_ref[r] = total.astype(bf16)

    halves = cap // lane
    kept = table_kept(per_device * halves)
    row_column = float_iota((devices * kept, cap), 0)
    for r in range(rounds):
        other = 1 - r
        for group in range(per_device + 1):
            if group < per_device:
                tokens = tokens_ref[group, pl.ds(r * devices + me, 1), :]
            else:
                tokens = tokens_ref[0, pl.ds(r * devices + after, 1), :]
            high, low = split(tokens)
            high_hot = one_hot(high)
            found = []
            for part in range(2):
                table = table_ref[other, part * high_count : (part + 1) * high_count, :]
                picked = dot_tn(table, high_hot)
                found.append(jnp.sum(jnp.where(low, picked, 0.0), axis=0, keepdims=True))
            group_index, position = found
            device = jnp.floor((group_index + 0.5) * (1.0 / per_device))
            half = jnp.floor((position + 0.5) * (1.0 / lane))
            row = device * kept + (group_index - device * per_device) * halves + half
            span = pl.ds(group * cap, cap)
            partner_ref[r, :, span] = one_hot(row == row_column)
            low_ref[pl.ds(r * (per_device + 1) + group, 1), :] = position - half * lane


def return_index_kernel(
    rounds,
    devices,
    bound,
    token_count,
    tokens_ref,
    home_place_ref,
    spread_t_ref,
    home_ref,
    pick_ref,
    key_ref,
    value_ref,
):
    per_device, _, cap = tokens_ref.shape
    place_column = float_iota((devices * bound, cap), 0)
    for r in range(rounds):
        for group in range(per_device):
            row = r * per_device + group
            place = home_place_ref[row : row + 1, :]
            spread_t_ref[r, :, pl.ds(group * cap, cap)] = one_hot(place == place_column)
    seat = lax.axis_index("seq")
    rank_slots(rounds, devices, token_count, seat, tokens_ref, key_ref, value_ref)

    size = rounds * bound
    for device in range(devices):
        pick_ref[device * size : (device + 1) * size, :] = pick_rows(
            rounds, devices, bound, block_of(device, devices), token_count, key_ref, value_ref
        )
    home_ref[...] = jnp.transpose(pick_ref[...])


def table_kept(count):
    return (count + 7) // 8 * 8


def spread_of(place_ref, r, group, rounds, buffer_rows):
    row = r * (place_ref.shape[0] // rounds) + group
    cap = place_ref.shape[1]
    return short_hot(place_ref[row : row + 1, :], (buffer_rows, cap), 0)


def received_rows(near_ref, far_refs, r, rounds):
    half, span, width = near_ref.shape
    bound = span // rounds
    rows = slice(r * bound, (r + 1) * bound)
    parts = [near_ref[:, rows, :].reshape(half * bound, width)]
    parts += [far_ref[rows, :] for far_ref in far_refs]
    return jnp.concatenate(parts, axis=0)


def ends_kernel(rounds, near_ref, place_ref, *refs):
    far_refs, (last_ref, first_ref) = refs[:-2], refs[-2:]
    size = near_ref.shape[2] // 3
    per_device = place_ref.shape[0] // rounds
    for r in range(rounds):
        received = received_rows(near_ref, far_refs, r, rounds)
        spread = spread_of(place_ref, r, per_device - 1, rounds, received.shape[0])
        last_ref[r] = dot_tn(spread, received[:, : 2 * size]).astype(bf16)
        spread = spread_of(place_ref, r, 0, rounds, received.shape[0])
        wanted = jnp.concatenate([received[:, :size], received[:, 2 * size :]], axis=1)
        first_ref[r] = dot_tn(spread, wanted).astype(bf16)


def inverse_norm(rows):
    wide = rows.astype(f32)
    return lax.rsqrt(jnp.sum(wide * wide, axis=1, keepdims=True) + norm_eps)


def unit_rows(rows):
    return (rows.astype(f32) * inverse_norm(rows)).astype(bf16)


def fill_row(fill_ref, r, at, rounds):
    row = r * (fill_ref.shape[0] // rounds) + at
    return fill_ref[row : row + 1, :]


def scored(unit, queries, fill, own):
    cap = queries.shape[0]
    key = float_iota((cap, cap), 0)
    allowed = key < fill
    if own:
        allowed = allowed & (key != float_iota((cap, cap), 1))
    return jnp.where(allowed, dot_nt(unit, queries), masked_score)


def normalised(scores, inners):
    highest = jnp.maximum(
        jnp.max(scores[0], axis=0, keepdims=True), jnp.max(scores[1], axis=0, keepdims=True)
    )
    exps = [jnp.exp(score - highest) for score in scores]
    total = jnp.sum(exps[0], axis=0, keepdims=True) + jnp.sum(exps[1], axis=0, keepdims=True)
    inverse = 1.0 / total
    probs = [part * inverse for part in exps]
    dots = jnp.sum(probs[0] * inners[0], axis=0, keepdims=True) + jnp.sum(
        probs[1] * inners[1], axis=0, keepdims=True
    )
    centred = [(inner - dots).astype(bf16) for inner in inners]
    return highest + jnp.log(total), dots, [prob.astype(bf16) for prob in probs], centred


def forward_inner_kernel(
    rounds,
    fill_ref,
    near_ref,
    place_ref,
    last_ref,
    first_ref,
    *refs,
):
    far_refs, refs = refs[:-7], refs[-7:]
    rows_ref, units_ref, prob_ref, inner_ref, first_score_ref, first_inner_ref, sums_ref = refs
    cap = prob_ref.shape[3]
    per_device = rows_ref.shape[1]
    size = rows_ref.shape[3] // 3
    for r in range(rounds):
        received = received_rows(near_ref, far_refs, r, rounds)
        for group in range(per_device):
            spread = spread_of(place_ref, r, group, rounds, received.shape[0])
            if group == 0:
                values = dot_tn(spread, received[:, size : 2 * size]).astype(bf16)
                rows_ref[r, group, :, :size] = first_ref[r, :, :size]
                rows_ref[r, group, :, size : 2 * size] = values
                rows_ref[r, group, :, 2 * size :] = first_ref[r, :, size:]
            elif group < per_device - 1:
                rows_ref[r, group] = dot_tn(spread, received).astype(bf16)
            else:
                rows_ref[r, group, :, : 2 * size] = last_ref[r]
                cots = dot_tn(spread, received[:, 2 * size :]).astype(bf16)
                rows_ref[r, group, :, 2 * size :] = cots
        units = [unit_rows(rows_ref[r, group, :, :size]) for group in range(per_device)]
        for group in range(per_device):
            units_ref[r, group] = units[group]
        for group in range(per_device):
            queries = rows_ref[r, group, :, :size]
            cot = rows_ref[r, group, :, 2 * size :]
            values = rows_ref[r, group, :, size : 2 * size]
            score_now = scored(
                units[group], queries, fill_row(fill_ref, r, group + 1, rounds), True
            )
            inner_now = dot_nt(values, cot)
            if group == 0:
                first_score_ref[r] = score_now
                first_inner_ref[r] = inner_now
                continue
            values = rows_ref[r, group - 1, :, size : 2 * size]
            inner_before = dot_nt(values, cot)
            score_before = scored(
                units[group - 1], queries, fill_row(fill_ref, r, group, rounds), False
            )
            inners = [inner_before, inner_now]
            log_total, dots, probs, centred = normalised([score_before, score_now], inners)
            for side in range(2):
                span = slice(side * cap, (side + 1) * cap)
                prob_ref[r, group - 1, span, :] = probs[side]
                inner_ref[r, group - 1, span, :] = centred[side]
            row = r * per_device + group
            sums_ref[row : row + 1, :] = log_total
            row = (rounds + r) * per_device + group
            sums_ref[row : row + 1, :] = dots


def forward_first_kernel(
    rounds,
    devices,
    fill_ref,
    rows_ref,
    behind_ref,
    score_ref,
    inner_now_ref,
    inner_sums_ref,
    unit_ref,
    prob_ref,
    inner_ref,
    sums_ref,
    send_ref,
    block_ref,
):
    cap = prob_ref.shape[2]
    per_device = rows_ref.shape[1]
    size = rows_ref.shape[3] // 3
    sums_ref[...] = inner_sums_ref[...]
    for r in range(rounds):
        behind_unit = unit_rows(behind_ref[r, :, :size])
        unit_ref[r] = behind_unit
        queries = rows_ref[r, 0, :, :size]
        cot = rows_ref[r, 0, :, 2 * size :]
        score_before = scored(behind_unit, queries, fill_row(fill_ref, r, 0, rounds), False)
        inners = [dot_nt(behind_ref[r, :, size:], cot), inner_now_ref[r]]
        log_total, dots, probs, centred = normalised([score_before, score_ref[r]], inners)
        for side in range(2):
            span = slice(side * cap, (side + 1) * cap)
            prob_ref[r, span, :] = probs[side]
            inner_ref[r, span, :] = centred[side]
        row = r * per_device
        sums_ref[row : row + 1, :] = log_total
        row = (rounds + r) * per_device
        sums_ref[row : row + 1, :] = dots
    halves = cap // lane
    count = per_device * halves
    for r in range(rounds):
        for kind in range(2):
            for group in range(per_device):
                row = (kind * rounds + r) * per_device + group
                for half in range(halves):
                    at = (2 * r + kind) * count + group * halves + half
                    block_ref[at : at + 1, :] = sums_ref[
                        row : row + 1, half * lane : (half + 1) * lane
                    ]
    block = block_ref[...]
    for device in range(devices):
        send_ref[device] = block


def key_grad(rows, unit_grad):
    wide = rows.astype(f32)
    inverse = inverse_norm(rows)
    along = jnp.sum(wide * unit_grad, axis=1, keepdims=True)
    return inverse * unit_grad - wide * (inverse * inverse * inverse * along)


def three_parts(values):
    high = values.astype(bf16)
    rest = values - high.astype(f32)
    middle = rest.astype(bf16)
    return high, middle, (rest - middle.astype(f32)).astype(bf16)


def backward_kernel(
    rounds,
    devices,
    bound,
    fill_ref,
    everyone_ref,
    partner_ref,
    low_ref,
    sums_ref,
    rows_ref,
    ahead_ref,
    units_ref,
    behind_unit_ref,
    first_prob_ref,
    first_inner_ref,
    prob_ref,
    inner_ref,
    spread_t_ref,
    send_ref,
    grads_ref,
):
    cap = rows_ref.shape[2]
    per_device = rows_ref.shape[1]
    size = rows_ref.shape[3] // 3
    me = block_of(lax.axis_index("seq"), devices)
    ahead_device = device_of(lax.rem(me + 1, devices), devices)
    halves = cap // lane
    count = per_device * halves
    kept = table_kept(count)
    low_column = float_iota((lane, cap), 0)
    slot = float_iota((1, cap), 1)

    def sums_of_all(r, kind):
        start = (2 * r + kind) * count
        held = min(start, everyone_ref.shape[1] - kept)
        rows = everyone_ref[:, held : held + kept, :]
        if start > held:
            rows = jnp.concatenate(
                [rows[:, start - held :], jnp.zeros((devices, start - held, lane), f32)], axis=1
            )
        return jnp.transpose(rows.reshape(devices * kept, lane))

    def ahead_sums(r, kind):
        start = (2 * r + kind) * count
        rows = [everyone_ref[ahead_device, start + h : start + h + 1, :] for h in range(halves)]
        return jnp.concatenate(rows, axis=1)

    def scales_of(r):
        logs = three_parts(sums_of_all(1 - r, 0))
        dots = three_parts(sums_of_all(1 - r, 1))
        upright = jnp.concatenate(logs + dots[:2], axis=0)
        picked = dot_nn(upright, partner_ref[r])
        picked_log = picked[:lane] + (picked[lane : 2 * lane] + picked[2 * lane : 3 * lane])
        picked_dot = picked[3 * lane : 4 * lane] + picked[4 * lane :]
        scales = []
        for group in range(per_device + 1):
            at = r * (per_device + 1) + group
            here = low_ref[at : at + 1, :] == low_column
            span = slice(group * cap, (group + 1) * cap)
            other_log = jnp.sum(jnp.where(here, picked_log[:, span], 0.0), axis=0, keepdims=True)
            other_dot = jnp.sum(jnp.where(here, picked_dot[:, span], 0.0), axis=0, keepdims=True)
            if group < per_device:
                row = r * per_device + group
                own_log = sums_ref[row : row + 1, :]
                own_dot = sums_ref[rounds * per_device + row : rounds * per_device + row + 1, :]
            else:
                own_log = ahead_sums(r, 0)
                own_dot = ahead_sums(r, 1)
            weight = 1.0 / (1.0 + jnp.exp(other_log - own_log))
            other_weight = 1.0 / (1.0 + jnp.exp(own_log - other_log))
            shift = other_weight * (own_dot - other_dot)
            valid = slot < fill_row(fill_ref, r, group + 1, rounds)
            scales.append((jnp.where(valid, weight, 0.0), jnp.where(valid, shift, 0.0)))
        return scales

    def score_grads(prob, inner, scale):
        weighted = prob.astype(f32) * scale[0]
        score_grad = (weighted * (inner.astype(f32) + scale[1])).astype(bf16)
        return weighted.astype(bf16), score_grad

    aheads = []
    for r in range(rounds):
        queries = ahead_ref[r, :, :size]
        cot = ahead_ref[r, :, size:]
        fill = fill_row(fill_ref, r, per_device, rounds)
        score = scored(units_ref[r, per_device - 1], queries, fill, False)
        inner = dot_nt(rows_ref[r, per_device - 1, :, size : 2 * size], cot)
        aheads.append(([jnp.exp(score - ahead_sums(r, 0))], [inner - ahead_sums(r, 1)]))
    scales = [scales_of(r) for r in range(rounds)]
    carried = [None] * rounds
    for group in range(per_device + 1):
        for r in range(rounds):
            if group < per_device:
                queries = rows_ref[r, group, :, :size]
                cot = rows_ref[r, group, :, 2 * size :]
            else:
                queries = ahead_ref[r, :, :size]
                cot = ahead_ref[r, :, size:]
            if group == 0:
                probs = [first_prob_ref[r, :cap, :], first_prob_ref[r, cap:, :]]
                inners = [first_inner_ref[r, :cap, :], first_inner_ref[r, cap:, :]]
            elif group < per_device:
                probs = [prob_ref[r, group - 1, :cap, :], prob_ref[r, group - 1, cap:, :]]
                inners = [inner_ref[r, group - 1, :cap, :], inner_ref[r, group - 1, cap:, :]]
            else:
                probs, inners = aheads[r]
            scale = scales[r][group]
            weighted, score_grad = score_grads(probs[0], inners[0], scale)
            if group > 0:
                query_grad, unit_grad, value_grad = carried[r]
                unit_grad = unit_grad + dot_nn(score_grad, queries)
                value_grad = value_grad + dot_nn(weighted, cot)
                key_part = key_grad(rows_ref[r, group - 1, :, :size], unit_grad)
                span = slice((group - 1) * cap, group * cap)
                grads_ref[r, span, :size] = (query_grad + key_part).astype(bf16)
                grads_ref[r, span, size:] = value_grad.astype(bf16)
            if group < per_device:
                unit_before = behind_unit_ref[r] if group == 0 else units_ref[r, group - 1]
                query_grad = dot_tn(score_grad, unit_before)
                weighted, score_grad = score_grads(probs[1], inners[1], scale)
                query_grad = query_grad + dot_tn(score_grad, units_ref[r, group])
                unit_grad = dot_nn(score_grad, queries)
                carried[r] = (query_grad, unit_grad, dot_nn(weighted, cot))
    for r in range(rounds):
        packed = dot_nn(spread_t_ref[r], grads_ref[r]).astype(bf16)
        send_ref[:, r * bound : (r + 1) * bound, :] = packed.reshape(devices, bound, 2 * size)


def home_kernel(home_ref, got_ref, qk_ref, value_ref):
    size = qk_ref.shape[1]
    total = dot_nn(home_ref[...], got_ref[...])
    qk_ref[...] = total[:, :size].astype(bf16)
    value_ref[...] = total[:, size:].astype(bf16)


def exchange_in_half(array):
    devices = lax.axis_size("seq")
    half = devices // 2
    halves = [list(range(half)), list(range(half, devices))]
    return lax.all_to_all(
        array, "seq", split_axis=0, concat_axis=0, tiled=True, axis_index_groups=halves
    )


def crossed(array, by):
    devices = lax.axis_size("seq")
    return lax.ppermute(array, "seq", [(i, i ^ by) for i in range(devices)])


def mirrored(array):
    devices = lax.axis_size("seq")
    half = devices // 2
    return lax.ppermute(array, "seq", [(i, (i + half) % devices) for i in range(devices)])


def exchange(array):
    return lax.all_to_all(array, "seq", split_axis=0, concat_axis=0, tiled=True)


def shifted(array, by):
    devices = lax.axis_size("seq")
    order = [device_of(block, devices) for block in range(devices)]
    return lax.ppermute(array, "seq", [(order[i], order[(i + by) % devices]) for i in range(devices)])


def head_backward(qk, values, cot, members, counts):
    devices = lax.axis_size("seq")
    token_count, size = qk.shape
    rounds, groups, cap = members.shape
    per_device = groups // devices
    slots = per_device * cap
    bound = 2 * token_count // devices
    span = rounds * bound
    buffer_rows = devices * bound
    sum_rows = 2 * rounds * per_device
    listed = members.reshape(rounds * groups, cap)
    keys = [((per_device, rounds * devices, cap), f32)] * 2
    pick = ((devices * span, token_count), bf16)
    half = devices // 2
    (joined,) = call(
        join_kernel,
        [((token_count, 3 * size), bf16)],
        [qk, values, cot],
        remote=3,
        semaphores=3,
    )
    far_rows = mirrored(joined)
    near_send, tokens = call(
        functools.partial(pack_kernel, rounds, devices, bound),
        [((half * span, 3 * size), bf16), (keys[0][0], jnp.int32)],
        [joined, counts, listed],
        [((half * span, 3 * size), bf16)]
        + keys
        + [
            (counts.shape, jnp.int32),
            ((cap // lane, rounds * groups + 8 * per_device, lane), jnp.int32),
        ],
        remote=2,
        semaphores=cap // lane + 5,
        far=(0,),
        direct=(0,),
    )
    near = exchange_in_half(near_send).reshape(half, span, 3 * size)
    (far_pick,) = call(
        functools.partial(far_pick_kernel, rounds, devices, bound, token_count),
        [((half * span, token_count), bf16)],
        [tokens],
        keys,
    )
    place, home_place, fill = call(
        functools.partial(place_kernel, rounds, devices, bound, token_count),
        [
            ((rounds * per_device, cap), f32),
            ((rounds * per_device, cap), f32),
            ((rounds * (per_device + 2), cap), f32),
        ],
        [tokens],
    )
    partner, low = call(
        functools.partial(index_kernel, rounds, devices, bound, token_count),
        [
            ((rounds, devices * table_kept(slots // lane), slots + cap), bf16),
            ((rounds * (per_device + 1), cap), f32),
        ],
        [tokens],
        [((rounds, 2 * devices * token_count // lane, lane), bf16)],
        far=(0,),
    )
    far_send = call(
        far_pack_kernel,
        [((span, 3 * size), bf16)] * half,
        [far_pick, far_rows],
        cost=50_000_000_000,
    )
    spread_t, home_pick = call(
        functools.partial(return_index_kernel, rounds, devices, bound, token_count),
        [((rounds, buffer_rows, slots), bf16), ((token_count, devices * span), bf16)],
        [tokens, home_place],
        [pick] + keys,
        far=(0, 1),
    )
    far_send, partner, spread_t, home_pick = lax.optimization_barrier(
        (far_send, partner, spread_t, home_pick)
    )
    far = [far_send[0]] + [crossed(far_send[at], bits_at(at, half)) for at in range(1, half)]
    last, first = call(
        functools.partial(ends_kernel, rounds),
        [((rounds, cap, 2 * size), bf16)] * 2,
        [near, place] + far,
    )
    behind = shifted(last, 1)
    ahead = shifted(first, -1)
    square = (rounds, cap, cap)
    rows, units, prob, inner, first_score, first_inner_now, inner_sums = call(
        functools.partial(forward_inner_kernel, rounds),
        [
            ((rounds, per_device, cap, 3 * size), bf16),
            ((rounds, per_device, cap, size), bf16),
            ((rounds, per_device - 1, 2 * cap, cap), bf16),
            ((rounds, per_device - 1, 2 * cap, cap), bf16),
            (square, f32),
            (square, f32),
            ((sum_rows, cap), f32),
        ],
        [fill, near, place, last, first] + far,
    )
    behind_unit, first_prob, first_inner, sums, sums_send = call(
        functools.partial(forward_first_kernel, rounds, devices),
        [
            ((rounds, cap, size), bf16),
            ((rounds, 2 * cap, cap), bf16),
            ((rounds, 2 * cap, cap), bf16),
            ((sum_rows, cap), f32),
            ((devices, sum_rows * cap // lane, lane), f32),
        ],
        [fill, rows, behind, first_score, first_inner_now, inner_sums],
        [((sum_rows * cap // lane, lane), f32)],
    )
    sums_send, ahead = lax.optimization_barrier((sums_send, ahead))
    everyone = exchange(sums_send)
    (grads_send,) = call(
        functools.partial(backward_kernel, rounds, devices, bound),
        [((devices, span, 2 * size), bf16)],
        [
            fill,
            everyone,
            partner,
            low,
            sums,
            rows,
            ahead,
            units,
            behind_unit,
            first_prob,
            first_inner,
            prob,
            inner,
            spread_t,
        ],
        [((rounds, slots, 2 * size), bf16)],
    )
    home = exchange(grads_send.reshape(devices * span, 2 * size))
    return call(
        home_kernel,
        [((token_count, size), bf16), ((token_count, size), bf16)],
        [home_pick, home],
    )


def on_device(qk, values, grad_out, members, counts):
    grad_qk, grad_v = head_backward(qk[0], values[0], grad_out[0], members[0], counts[0])
    return (grad_qk[None], grad_v[None])


def solution(mesh):
    in_specs = (
        P("head", "seq", None),
        P("head", "seq", None),
        P("head", "seq", None),
        P("head", None, None, None),
        P("head", None, None),
    )
    out_specs = (P("head", "seq", None), P("head", "seq", None))
    return jax.shard_map(
        on_device, mesh=mesh, in_specs=in_specs, out_specs=out_specs, check_vma=False
    )
```

```python
import functools
import math

import jax
import jax.numpy as jnp
from jax import lax
from jax.experimental import pallas as pl
from jax.experimental.pallas import tpu as pltpu
from jax.sharding import PartitionSpec as P

masked_score = -1e30
norm_eps = 1e-06
lane = 128
f32 = jnp.float32
bf16 = jnp.bfloat16


def iota(shape, axis):
    return lax.broadcasted_iota(jnp.int32, shape, axis)


def float_iota(shape, axis):
    return iota(shape, axis).astype(f32)


def dot_nn(a, b):
    return lax.dot_general(a, b, (((1,), (0,)), ((), ())), preferred_element_type=f32)


def dot_nt(a, b):
    return lax.dot_general(a, b, (((1,), (1,)), ((), ())), preferred_element_type=f32)


def dot_tn(a, b):
    return lax.dot_general(a, b, (((0,), (0,)), ((), ())), preferred_element_type=f32)


def one_hot(condition):
    return jnp.where(condition, 1.0, 0.0).astype(bf16)


def short_hot(index, shape, axis):
    place = iota(shape, axis).astype(jnp.int16)
    short = jnp.broadcast_to(index.astype(jnp.int32), shape).astype(jnp.int16)
    return jnp.where(short == place, jnp.ones(shape, bf16), jnp.zeros(shape, bf16))


def block_of(device, devices):
    if devices % 4:
        return device
    depth = devices // 4
    level, column = device // 4, device % 4
    turn = column ^ (column >> 1)
    step = level + (turn % 2) * (depth - 1 - 2 * level)
    return turn * depth + step


def device_of(block, devices):
    if devices % 4:
        return block
    depth = devices // 4
    turn, step = block // depth, block % depth
    level = step + (turn % 2) * (depth - 1 - 2 * step)
    return level * 4 + (turn ^ (turn >> 1))


def earlier(size):
    return one_hot(iota((size, size), 0) < iota((size, size), 1))


def call(
    kernel,
    out_shapes,
    operands,
    scratch=(),
    remote=0,
    semaphores=0,
    far=(),
    direct=(),
    cost=0,
):
    count = len(operands)
    held = sum(array.size * array.dtype.itemsize for array in operands[: count - remote])
    for shape, dtype in list(out_shapes) + list(scratch):
        held += math.prod(shape) * jnp.dtype(dtype).itemsize
    spaces = [pltpu.VMEM] * (count - remote) + [pltpu.HBM] * remote
    operands = [
        pltpu.with_memory_space_constraint(array, space) if space is pltpu.HBM else array
        for array, space in zip(operands, spaces)
    ]
    return pl.pallas_call(
        kernel,
        out_shape=tuple(
            pltpu.HBM(shape, dtype) if at in far else jax.ShapeDtypeStruct(shape, dtype)
            for at, (shape, dtype) in enumerate(out_shapes)
        ),
        in_specs=[pl.BlockSpec(memory_space=space) for space in spaces],
        out_specs=tuple(
            pl.BlockSpec(memory_space=pltpu.HBM if at in direct else pltpu.VMEM)
            for at in range(len(out_shapes))
        ),
        scratch_shapes=[pltpu.VMEM(shape, dtype) for shape, dtype in scratch]
        + [pltpu.SemaphoreType.DMA((semaphores,))] * min(semaphores, 1),
        cost_estimate=pl.CostEstimate(flops=cost, transcendentals=0, bytes_accessed=0),
        compiler_params=pltpu.CompilerParams(vmem_limit_bytes=held + 12 * 1024 * 1024),
    )(*operands)


def slot_tokens(members_ref, counts_ref, devices, group):
    rounds, groups = counts_ref.shape
    per_device = groups // devices
    rows = pl.ds(group, rounds * devices, stride=per_device)
    parts = [members_ref[half, rows, :] for half in range(members_ref.shape[0])]
    listed = jnp.concatenate(parts, axis=1)
    diagonal = iota((devices, groups), 1) == iota((devices, groups), 0) * per_device + group
    limits = [
        jnp.sum(
            jnp.where(diagonal, counts_ref[r : r + 1, :].astype(f32), 0.0), axis=1, keepdims=True
        )
        for r in range(rounds)
    ]
    limit = jnp.concatenate(limits, axis=0)
    return jnp.where(float_iota(listed.shape, 1) < limit, listed, -1)


def rank_slots(rounds, devices, token_count, source, tokens_ref, key_ref, value_ref):
    per_device, _, cap = key_ref.shape
    start = source * token_count
    before = earlier(cap)
    carry = jnp.zeros((rounds * devices, 1), f32)
    for group in range(per_device):
        local = tokens_ref[group] - start
        owned = (local >= 0) & (local < token_count)
        rank = dot_nn(one_hot(owned), before) + carry
        carry = carry + jnp.sum(jnp.where(owned, 1.0, 0.0), axis=1, keepdims=True)
        key_ref[group] = jnp.where(owned, rank, -1.0)
        value_ref[group] = jnp.where(owned, local + 1, 0).astype(f32)


def pick_rows(rounds, devices, bound, block, token_count, key_ref, value_ref):
    per_device, _, cap = key_ref.shape
    column = float_iota((bound, cap), 0)
    picks = []
    for r in range(rounds):
        row = r * devices + block
        total = jnp.zeros((bound, cap), f32)
        for group in range(per_device):
            ranks = key_ref[group, pl.ds(row, 1), :]
            values = value_ref[group, pl.ds(row, 1), :]
            total = total + jnp.where(ranks == column, values, 0.0)
        index = jnp.sum(total, axis=1, keepdims=True) - 1.0
        picks.append(short_hot(index, (bound, token_count), 1))
    return jnp.concatenate(picks, axis=0)


def join_kernel(q_hbm, v_hbm, g_hbm, joined_ref, sems):
    size = q_hbm.shape[1]
    copies = []
    for at, source in enumerate((q_hbm, v_hbm, g_hbm)):
        target = joined_ref.at[:, pl.ds(at * size, size)]
        copies.append(pltpu.make_async_copy(source, target, sems.at[at]))
    for copy in copies:
        copy.start()
    for copy in copies:
        copy.wait()


def pack_kernel(
    rounds,
    devices,
    bound,
    joined_ref,
    counts_hbm,
    members_hbm,
    send_hbm,
    tokens_ref,
    packed_ref,
    key_ref,
    value_ref,
    counts_ref,
    members_ref,
    sems,
):
    token_count = joined_ref.shape[0]
    halves = members_ref.shape[0]
    copies = [pltpu.make_async_copy(counts_hbm, counts_ref, sems.at[halves])]
    for half in range(halves):
        source = members_hbm.at[:, pl.ds(half * lane, lane)]
        target = members_ref.at[half, pl.ds(0, members_hbm.shape[0])]
        copies.append(pltpu.make_async_copy(source, target, sems.at[half]))
    for copy in copies:
        copy.start()
    for copy in copies:
        copy.wait()
    for group in range(tokens_ref.shape[0]):
        tokens_ref[group] = slot_tokens(members_ref, counts_ref, devices, group)
    me = lax.axis_index("seq")
    rank_slots(rounds, devices, token_count, me, tokens_ref, key_ref, value_ref)
    half = devices // 2
    first = me // half * half
    parts = 4
    step = half // parts
    sends = []
    for part in range(parts):
        picks = [
            pick_rows(
                rounds,
                devices,
                bound,
                block_of(first + at, devices),
                token_count,
                key_ref,
                value_ref,
            )
            for at in range(part * step, (part + 1) * step)
        ]
        span = pl.ds(part * step * rounds * bound, step * rounds * bound)
        packed_ref[span, :] = dot_nn(jnp.concatenate(picks, axis=0), joined_ref[...]).astype(bf16)
        copy = pltpu.make_async_copy(
            packed_ref.at[span, :], send_hbm.at[span, :], sems.at[halves + 1 + part]
        )
        copy.start()
        sends.append(copy)
    for copy in sends:
        copy.wait()


def bits_at(at, half):
    plane = half // 2
    if at == 0:
        return 0
    return half - at if at <= plane else at - plane


def far_pick_kernel(rounds, devices, bound, token_count, tokens_ref, pick_ref, key_ref, value_ref):
    me = lax.axis_index("seq")
    half = devices // 2
    first = me // half * half
    source = lax.rem(me + half, devices)
    rank_slots(rounds, devices, token_count, source, tokens_ref, key_ref, value_ref)
    size = rounds * bound
    for at in range(half):
        block = block_of(first + jnp.bitwise_xor(me - first, bits_at(at, half)), devices)
        pick_ref[at * size : (at + 1) * size, :] = pick_rows(
            rounds, devices, bound, block, token_count, key_ref, value_ref
        )


def far_pack_kernel(pick_ref, rows_ref, *send_refs):
    rows = rows_ref[...]
    span = send_refs[0].shape[0]
    parts = 4
    count = len(send_refs) // parts
    for part in range(parts):
        first = part * count
        packed = dot_nn(pick_ref[pl.ds(first * span, count * span), :], rows).astype(bf16)
        for at in range(count):
            send_refs[first + at][...] = packed[at * span : (at + 1) * span]


def place_kernel(rounds, devices, bound, token_count, tokens_ref, place_ref, home_place_ref, fill_ref):
    per_device, _, cap = tokens_ref.shape
    seat = lax.axis_index("seq")
    me = block_of(seat, devices)
    half = devices // 2
    before = earlier(cap)
    source = iota((devices, cap), 0)
    source_start = source * token_count
    home_place = source.astype(f32) * bound + 1.0
    first = seat // half * half
    near = (source >= first) & (source < first + half)
    bits = jnp.bitwise_xor(source % half, seat - first)
    plane = half // 2
    order = jnp.where(bits < plane, bits + plane, half - bits)
    crossed = half + jnp.where(bits > 0, order, 0)
    source_place = jnp.where(near, source - first, crossed).astype(f32) * bound + 1.0
    for r in range(rounds):
        carry = jnp.zeros((devices, 1), f32)
        for group in range(per_device):
            tokens = tokens_ref[group, pl.ds(r * devices + me, 1), :]
            owned = (tokens >= source_start) & (tokens < source_start + token_count)
            rank = dot_nn(one_hot(owned), before) + carry
            carry = carry + jnp.sum(jnp.where(owned, 1.0, 0.0), axis=1, keepdims=True)
            for target, base in ((place_ref, source_place), (home_place_ref, home_place)):
                place = jnp.sum(jnp.where(owned, rank + base, 0.0), axis=0, keepdims=True) - 1.0
                row = r * per_device + group
                target[row : row + 1, :] = place
    after = lax.rem(me + 1, devices)
    behind = lax.rem(me + devices - 1, devices)
    for r in range(rounds):
        for at in range(per_device + 2):
            block = behind if at == 0 else after if at > per_device else me
            group = (at - 1) % per_device
            tokens = tokens_ref[group, pl.ds(r * devices + block, 1), :]
            fill = jnp.sum(jnp.where(tokens >= 0, 1.0, 0.0), axis=1, keepdims=True)
            row = r * (per_device + 2) + at
            fill_ref[row : row + 1, :] = jnp.broadcast_to(fill, (1, cap))


def index_kernel(
    rounds,
    devices,
    bound,
    token_count,
    tokens_ref,
    partner_ref,
    low_ref,
    table_ref,
):
    per_device, _, cap = tokens_ref.shape
    me = block_of(lax.axis_index("seq"), devices)
    after = lax.rem(me + 1, devices)
    high_count = devices * token_count // lane
    high_start = iota((high_count, cap), 0) * lane
    low_index = iota((lane, cap), 0)
    slot = float_iota((high_count, cap), 1)

    def split(tokens):
        high = (tokens >= high_start) & (tokens < high_start + lane)
        low = jnp.bitwise_and(tokens, lane - 1) == low_index
        return high, low

    for r in range(rounds):

        def one_block(block, total):
            device = device_of(block, devices)
            for group in range(per_device):
                tokens = tokens_ref[group, pl.ds(r * devices + block, 1), :]
                high, low = split(tokens)
                group_index = (device * per_device + group).astype(f32)
                sides = jnp.concatenate(
                    [
                        jnp.where(high, group_index, 0.0).astype(bf16),
                        jnp.where(high, slot, 0.0).astype(bf16),
                    ],
                    axis=0,
                )
                total = total + dot_nt(sides, one_hot(low))
            return total

        total = lax.fori_loop(
            0, devices, one_block, jnp.zeros((2 * high_count, lane), f32), unroll=4
        )
        table_ref[r] = total.astype(bf16)

    halves = cap // lane
    kept = table_kept(per_device * halves)
    row_column = float_iota((devices * kept, cap), 0)
    for r in range(rounds):
        other = 1 - r
        for group in range(per_device + 1):
            if group < per_device:
                tokens = tokens_ref[group, pl.ds(r * devices + me, 1), :]
            else:
                tokens = tokens_ref[0, pl.ds(r * devices + after, 1), :]
            high, low = split(tokens)
            high_hot = one_hot(high)
            found = []
            for part in range(2):
                table = table_ref[other, part * high_count : (part + 1) * high_count, :]
                picked = dot_tn(table, high_hot)
                found.append(jnp.sum(jnp.where(low, picked, 0.0), axis=0, keepdims=True))
            group_index, position = found
            device = jnp.floor((group_index + 0.5) * (1.0 / per_device))
            half = jnp.floor((position + 0.5) * (1.0 / lane))
            row = device * kept + (group_index - device * per_device) * halves + half
            span = pl.ds(group * cap, cap)
            partner_ref[r, :, span] = one_hot(row == row_column)
            low_ref[pl.ds(r * (per_device + 1) + group, 1), :] = position - half * lane


def return_index_kernel(
    rounds,
    devices,
    bound,
    token_count,
    tokens_ref,
    home_place_ref,
    spread_t_ref,
    home_ref,
    pick_ref,
    key_ref,
    value_ref,
):
    per_device, _, cap = tokens_ref.shape
    place_column = float_iota((devices * bound, cap), 0)
    for r in range(rounds):
        for group in range(per_device):
            row = r * per_device + group
            place = home_place_ref[row : row + 1, :]
            spread_t_ref[r, :, pl.ds(group * cap, cap)] = one_hot(place == place_column)
    seat = lax.axis_index("seq")
    rank_slots(rounds, devices, token_count, seat, tokens_ref, key_ref, value_ref)

    size = rounds * bound
    for device in range(devices):
        pick_ref[device * size : (device + 1) * size, :] = pick_rows(
            rounds, devices, bound, block_of(device, devices), token_count, key_ref, value_ref
        )
    home_ref[...] = jnp.transpose(pick_ref[...])


def table_kept(count):
    return (count + 7) // 8 * 8


def spread_of(place_ref, r, group, rounds, buffer_rows):
    row = r * (place_ref.shape[0] // rounds) + group
    cap = place_ref.shape[1]
    return short_hot(place_ref[row : row + 1, :], (buffer_rows, cap), 0)


def received_rows(near_ref, far_refs, r, rounds):
    half, span, width = near_ref.shape
    bound = span // rounds
    rows = slice(r * bound, (r + 1) * bound)
    parts = [near_ref[:, rows, :].reshape(half * bound, width)]
    parts += [far_ref[rows, :] for far_ref in far_refs]
    return jnp.concatenate(parts, axis=0)


def ends_kernel(rounds, near_ref, place_ref, *refs):
    far_refs, (last_ref, first_ref) = refs[:-2], refs[-2:]
    size = near_ref.shape[2] // 3
    per_device = place_ref.shape[0] // rounds
    for r in range(rounds):
        received = received_rows(near_ref, far_refs, r, rounds)
        spread = spread_of(place_ref, r, per_device - 1, rounds, received.shape[0])
        last_ref[r] = dot_tn(spread, received[:, : 2 * size]).astype(bf16)
        spread = spread_of(place_ref, r, 0, rounds, received.shape[0])
        wanted = jnp.concatenate([received[:, :size], received[:, 2 * size :]], axis=1)
        first_ref[r] = dot_tn(spread, wanted).astype(bf16)


def inverse_norm(rows):
    wide = rows.astype(f32)
    return lax.rsqrt(jnp.sum(wide * wide, axis=1, keepdims=True) + norm_eps)


def unit_rows(rows):
    return (rows.astype(f32) * inverse_norm(rows)).astype(bf16)


def fill_row(fill_ref, r, at, rounds):
    row = r * (fill_ref.shape[0] // rounds) + at
    return fill_ref[row : row + 1, :]


def scored(unit, queries, fill, own):
    cap = queries.shape[0]
    key = float_iota((cap, cap), 0)
    allowed = key < fill
    if own:
        allowed = allowed & (key != float_iota((cap, cap), 1))
    return jnp.where(allowed, dot_nt(unit, queries), masked_score)


def normalised(scores, inners):
    highest = jnp.maximum(
        jnp.max(scores[0], axis=0, keepdims=True), jnp.max(scores[1], axis=0, keepdims=True)
    )
    exps = [jnp.exp(score - highest) for score in scores]
    total = jnp.sum(exps[0], axis=0, keepdims=True) + jnp.sum(exps[1], axis=0, keepdims=True)
    inverse = 1.0 / total
    probs = [part * inverse for part in exps]
    dots = jnp.sum(probs[0] * inners[0], axis=0, keepdims=True) + jnp.sum(
        probs[1] * inners[1], axis=0, keepdims=True
    )
    centred = [(inner - dots).astype(bf16) for inner in inners]
    return highest + jnp.log(total), dots, [prob.astype(bf16) for prob in probs], centred


def forward_inner_kernel(
    rounds,
    fill_ref,
    near_ref,
    place_ref,
    last_ref,
    first_ref,
    *refs,
):
    far_refs, refs = refs[:-7], refs[-7:]
    rows_ref, units_ref, prob_ref, inner_ref, first_score_ref, first_inner_ref, sums_ref = refs
    cap = prob_ref.shape[3]
    per_device = rows_ref.shape[1]
    size = rows_ref.shape[3] // 3
    for r in range(rounds):
        received = received_rows(near_ref, far_refs, r, rounds)
        for group in range(per_device):
            spread = spread_of(place_ref, r, group, rounds, received.shape[0])
            if group == 0:
                values = dot_tn(spread, received[:, size : 2 * size]).astype(bf16)
                rows_ref[r, group, :, :size] = first_ref[r, :, :size]
                rows_ref[r, group, :, size : 2 * size] = values
                rows_ref[r, group, :, 2 * size :] = first_ref[r, :, size:]
            elif group < per_device - 1:
                rows_ref[r, group] = dot_tn(spread, received).astype(bf16)
            else:
                rows_ref[r, group, :, : 2 * size] = last_ref[r]
                cots = dot_tn(spread, received[:, 2 * size :]).astype(bf16)
                rows_ref[r, group, :, 2 * size :] = cots
        units = [unit_rows(rows_ref[r, group, :, :size]) for group in range(per_device)]
        for group in range(per_device):
            units_ref[r, group] = units[group]
        for group in range(per_device):
            queries = rows_ref[r, group, :, :size]
            cot = rows_ref[r, group, :, 2 * size :]
            values = rows_ref[r, group, :, size : 2 * size]
            score_now = scored(
                units[group], queries, fill_row(fill_ref, r, group + 1, rounds), True
            )
            inner_now = dot_nt(values, cot)
            if group == 0:
                first_score_ref[r] = score_now
                first_inner_ref[r] = inner_now
                continue
            values = rows_ref[r, group - 1, :, size : 2 * size]
            inner_before = dot_nt(values, cot)
            score_before = scored(
                units[group - 1], queries, fill_row(fill_ref, r, group, rounds), False
            )
            inners = [inner_before, inner_now]
            log_total, dots, probs, centred = normalised([score_before, score_now], inners)
            for side in range(2):
                span = slice(side * cap, (side + 1) * cap)
                prob_ref[r, group - 1, span, :] = probs[side]
                inner_ref[r, group - 1, span, :] = centred[side]
            row = r * per_device + group
            sums_ref[row : row + 1, :] = log_total
            row = (rounds + r) * per_device + group
            sums_ref[row : row + 1, :] = dots


def forward_first_kernel(
    rounds,
    devices,
    fill_ref,
    rows_ref,
    behind_ref,
    score_ref,
    inner_now_ref,
    inner_sums_ref,
    unit_ref,
    prob_ref,
    inner_ref,
    sums_ref,
    send_ref,
    block_ref,
):
    cap = prob_ref.shape[2]
    per_device = rows_ref.shape[1]
    size = rows_ref.shape[3] // 3
    sums_ref[...] = inner_sums_ref[...]
    for r in range(rounds):
        behind_unit = unit_rows(behind_ref[r, :, :size])
        unit_ref[r] = behind_unit
        queries = rows_ref[r, 0, :, :size]
        cot = rows_ref[r, 0, :, 2 * size :]
        score_before = scored(behind_unit, queries, fill_row(fill_ref, r, 0, rounds), False)
        inners = [dot_nt(behind_ref[r, :, size:], cot), inner_now_ref[r]]
        log_total, dots, probs, centred = normalised([score_before, score_ref[r]], inners)
        for side in range(2):
            span = slice(side * cap, (side + 1) * cap)
            prob_ref[r, span, :] = probs[side]
            inner_ref[r, span, :] = centred[side]
        row = r * per_device
        sums_ref[row : row + 1, :] = log_total
        row = (rounds + r) * per_device
        sums_ref[row : row + 1, :] = dots
    halves = cap // lane
    count = per_device * halves
    for r in range(rounds):
        for kind in range(2):
            for group in range(per_device):
                row = (kind * rounds + r) * per_device + group
                for half in range(halves):
                    at = (2 * r + kind) * count + group * halves + half
                    block_ref[at : at + 1, :] = sums_ref[
                        row : row + 1, half * lane : (half + 1) * lane
                    ]
    block = block_ref[...]
    for device in range(devices):
        send_ref[device] = block


def key_grad(rows, unit_grad):
    wide = rows.astype(f32)
    inverse = inverse_norm(rows)
    along = jnp.sum(wide * unit_grad, axis=1, keepdims=True)
    return inverse * unit_grad - wide * (inverse * inverse * inverse * along)


def three_parts(values):
    high = values.astype(bf16)
    rest = values - high.astype(f32)
    middle = rest.astype(bf16)
    return high, middle, (rest - middle.astype(f32)).astype(bf16)


def backward_kernel(
    rounds,
    devices,
    bound,
    fill_ref,
    everyone_ref,
    partner_ref,
    low_ref,
    sums_ref,
    rows_ref,
    ahead_ref,
    units_ref,
    behind_unit_ref,
    first_prob_ref,
    first_inner_ref,
    prob_ref,
    inner_ref,
    spread_t_ref,
    send_ref,
    grads_ref,
):
    cap = rows_ref.shape[2]
    per_device = rows_ref.shape[1]
    size = rows_ref.shape[3] // 3
    me = block_of(lax.axis_index("seq"), devices)
    ahead_device = device_of(lax.rem(me + 1, devices), devices)
    halves = cap // lane
    count = per_device * halves
    kept = table_kept(count)
    low_column = float_iota((lane, cap), 0)
    slot = float_iota((1, cap), 1)

    def sums_of_all(r, kind):
        start = (2 * r + kind) * count
        held = min(start, everyone_ref.shape[1] - kept)
        rows = everyone_ref[:, held : held + kept, :]
        if start > held:
            rows = jnp.concatenate(
                [rows[:, start - held :], jnp.zeros((devices, start - held, lane), f32)], axis=1
            )
        return jnp.transpose(rows.reshape(devices * kept, lane))

    def ahead_sums(r, kind):
        start = (2 * r + kind) * count
        rows = [everyone_ref[ahead_device, start + h : start + h + 1, :] for h in range(halves)]
        return jnp.concatenate(rows, axis=1)

    def scales_of(r):
        logs = three_parts(sums_of_all(1 - r, 0))
        dots = three_parts(sums_of_all(1 - r, 1))
        upright = jnp.concatenate(logs + dots[:2], axis=0)
        picked = dot_nn(upright, partner_ref[r])
        picked_log = picked[:lane] + (picked[lane : 2 * lane] + picked[2 * lane : 3 * lane])
        picked_dot = picked[3 * lane : 4 * lane] + picked[4 * lane :]
        scales = []
        for group in range(per_device + 1):
            at = r * (per_device + 1) + group
            here = low_ref[at : at + 1, :] == low_column
            span = slice(group * cap, (group + 1) * cap)
            other_log = jnp.sum(jnp.where(here, picked_log[:, span], 0.0), axis=0, keepdims=True)
            other_dot = jnp.sum(jnp.where(here, picked_dot[:, span], 0.0), axis=0, keepdims=True)
            if group < per_device:
                row = r * per_device + group
                own_log = sums_ref[row : row + 1, :]
                own_dot = sums_ref[rounds * per_device + row : rounds * per_device + row + 1, :]
            else:
                own_log = ahead_sums(r, 0)
                own_dot = ahead_sums(r, 1)
            weight = 1.0 / (1.0 + jnp.exp(other_log - own_log))
            other_weight = 1.0 / (1.0 + jnp.exp(own_log - other_log))
            shift = other_weight * (own_dot - other_dot)
            valid = slot < fill_row(fill_ref, r, group + 1, rounds)
            scales.append((jnp.where(valid, weight, 0.0), jnp.where(valid, shift, 0.0)))
        return scales

    def score_grads(prob, inner, scale):
        weighted = prob.astype(f32) * scale[0]
        score_grad = (weighted * (inner.astype(f32) + scale[1])).astype(bf16)
        return weighted.astype(bf16), score_grad

    aheads = []
    for r in range(rounds):
        queries = ahead_ref[r, :, :size]
        cot = ahead_ref[r, :, size:]
        fill = fill_row(fill_ref, r, per_device, rounds)
        score = scored(units_ref[r, per_device - 1], queries, fill, False)
        inner = dot_nt(rows_ref[r, per_device - 1, :, size : 2 * size], cot)
        aheads.append(([jnp.exp(score - ahead_sums(r, 0))], [inner - ahead_sums(r, 1)]))
    scales = [scales_of(r) for r in range(rounds)]
    carried = [None] * rounds
    for group in range(per_device + 1):
        for r in range(rounds):
            if group < per_device:
                queries = rows_ref[r, group, :, :size]
                cot = rows_ref[r, group, :, 2 * size :]
            else:
                queries = ahead_ref[r, :, :size]
                cot = ahead_ref[r, :, size:]
            if group == 0:
                probs = [first_prob_ref[r, :cap, :], first_prob_ref[r, cap:, :]]
                inners = [first_inner_ref[r, :cap, :], first_inner_ref[r, cap:, :]]
            elif group < per_device:
                probs = [prob_ref[r, group - 1, :cap, :], prob_ref[r, group - 1, cap:, :]]
                inners = [inner_ref[r, group - 1, :cap, :], inner_ref[r, group - 1, cap:, :]]
            else:
                probs, inners = aheads[r]
            scale = scales[r][group]
            weighted, score_grad = score_grads(probs[0], inners[0], scale)
            if group > 0:
                query_grad, unit_grad, value_grad = carried[r]
                unit_grad = unit_grad + dot_nn(score_grad, queries)
                value_grad = value_grad + dot_nn(weighted, cot)
                key_part = key_grad(rows_ref[r, group - 1, :, :size], unit_grad)
                span = slice((group - 1) * cap, group * cap)
                grads_ref[r, span, :size] = (query_grad + key_part).astype(bf16)
                grads_ref[r, span, size:] = value_grad.astype(bf16)
            if group < per_device:
                unit_before = behind_unit_ref[r] if group == 0 else units_ref[r, group - 1]
                query_grad = dot_tn(score_grad, unit_before)
                weighted, score_grad = score_grads(probs[1], inners[1], scale)
                query_grad = query_grad + dot_tn(score_grad, units_ref[r, group])
                unit_grad = dot_nn(score_grad, queries)
                carried[r] = (query_grad, unit_grad, dot_nn(weighted, cot))
    for r in range(rounds):
        packed = dot_nn(spread_t_ref[r], grads_ref[r]).astype(bf16)
        send_ref[:, r * bound : (r + 1) * bound, :] = packed.reshape(devices, bound, 2 * size)


def home_kernel(home_ref, got_ref, qk_ref, value_ref):
    size = qk_ref.shape[1]
    total = dot_nn(home_ref[...], got_ref[...])
    qk_ref[...] = total[:, :size].astype(bf16)
    value_ref[...] = total[:, size:].astype(bf16)


def exchange_in_half(array):
    devices = lax.axis_size("seq")
    half = devices // 2
    halves = [list(range(half)), list(range(half, devices))]
    return lax.all_to_all(
        array, "seq", split_axis=0, concat_axis=0, tiled=True, axis_index_groups=halves
    )


def crossed(array, by):
    devices = lax.axis_size("seq")
    return lax.ppermute(array, "seq", [(i, i ^ by) for i in range(devices)])


def mirrored(array):
    devices = lax.axis_size("seq")
    half = devices // 2
    return lax.ppermute(array, "seq", [(i, (i + half) % devices) for i in range(devices)])


def exchange(array):
    return lax.all_to_all(array, "seq", split_axis=0, concat_axis=0, tiled=True)


def shifted(array, by):
    devices = lax.axis_size("seq")
    order = [device_of(block, devices) for block in range(devices)]
    return lax.ppermute(array, "seq", [(order[i], order[(i + by) % devices]) for i in range(devices)])


def head_backward(qk, values, cot, members, counts):
    devices = lax.axis_size("seq")
    token_count, size = qk.shape
    rounds, groups, cap = members.shape
    per_device = groups // devices
    slots = per_device * cap
    bound = 2 * token_count // devices
    span = rounds * bound
    buffer_rows = devices * bound
    sum_rows = 2 * rounds * per_device
    listed = members.reshape(rounds * groups, cap)
    keys = [((per_device, rounds * devices, cap), f32)] * 2
    pick = ((devices * span, token_count), bf16)
    half = devices // 2
    (joined,) = call(
        join_kernel,
        [((token_count, 3 * size), bf16)],
        [qk, values, cot],
        remote=3,
        semaphores=3,
    )
    far_rows = mirrored(joined)
    near_send, tokens = call(
        functools.partial(pack_kernel, rounds, devices, bound),
        [((half * span, 3 * size), bf16), (keys[0][0], jnp.int32)],
        [joined, counts, listed],
        [((half * span, 3 * size), bf16)]
        + keys
        + [
            (counts.shape, jnp.int32),
            ((cap // lane, rounds * groups + 8 * per_device, lane), jnp.int32),
        ],
        remote=2,
        semaphores=cap // lane + 5,
        far=(0,),
        direct=(0,),
    )
    near = exchange_in_half(near_send).reshape(half, span, 3 * size)
    (far_pick,) = call(
        functools.partial(far_pick_kernel, rounds, devices, bound, token_count),
        [((half * span, token_count), bf16)],
        [tokens],
        keys,
    )
    place, home_place, fill = call(
        functools.partial(place_kernel, rounds, devices, bound, token_count),
        [
            ((rounds * per_device, cap), f32),
            ((rounds * per_device, cap), f32),
            ((rounds * (per_device + 2), cap), f32),
        ],
        [tokens],
    )
    partner, low = call(
        functools.partial(index_kernel, rounds, devices, bound, token_count),
        [
            ((rounds, devices * table_kept(slots // lane), slots + cap), bf16),
            ((rounds * (per_device + 1), cap), f32),
        ],
        [tokens],
        [((rounds, 2 * devices * token_count // lane, lane), bf16)],
        far=(0,),
    )
    far_send = call(
        far_pack_kernel,
        [((span, 3 * size), bf16)] * half,
        [far_pick, far_rows],
        cost=50_000_000_000,
    )
    spread_t, home_pick = call(
        functools.partial(return_index_kernel, rounds, devices, bound, token_count),
        [((rounds, buffer_rows, slots), bf16), ((token_count, devices * span), bf16)],
        [tokens, home_place],
        [pick] + keys,
        far=(0, 1),
    )
    far_send, partner, spread_t, home_pick = lax.optimization_barrier(
        (far_send, partner, spread_t, home_pick)
    )
    far = [far_send[0]] + [crossed(far_send[at], bits_at(at, half)) for at in range(1, half)]
    last, first = call(
        functools.partial(ends_kernel, rounds),
        [((rounds, cap, 2 * size), bf16)] * 2,
        [near, place] + far,
    )
    behind = shifted(last, 1)
    ahead = shifted(first, -1)
    square = (rounds, cap, cap)
    rows, units, prob, inner, first_score, first_inner_now, inner_sums = call(
        functools.partial(forward_inner_kernel, rounds),
        [
            ((rounds, per_device, cap, 3 * size), bf16),
            ((rounds, per_device, cap, size), bf16),
            ((rounds, per_device - 1, 2 * cap, cap), bf16),
            ((rounds, per_device - 1, 2 * cap, cap), bf16),
            (square, f32),
            (square, f32),
            ((sum_rows, cap), f32),
        ],
        [fill, near, place, last, first] + far,
    )
    behind_unit, first_prob, first_inner, sums, sums_send = call(
        functools.partial(forward_first_kernel, rounds, devices),
        [
            ((rounds, cap, size), bf16),
            ((rounds, 2 * cap, cap), bf16),
            ((rounds, 2 * cap, cap), bf16),
            ((sum_rows, cap), f32),
            ((devices, sum_rows * cap // lane, lane), f32),
        ],
        [fill, rows, behind, first_score, first_inner_now, inner_sums],
        [((sum_rows * cap // lane, lane), f32)],
    )
    sums_send, ahead = lax.optimization_barrier((sums_send, ahead))
    everyone = exchange(sums_send)
    (grads_send,) = call(
        functools.partial(backward_kernel, rounds, devices, bound),
        [((devices, span, 2 * size), bf16)],
        [
            fill,
            everyone,
            partner,
            low,
            sums,
            rows,
            ahead,
            units,
            behind_unit,
            first_prob,
            first_inner,
            prob,
            inner,
            spread_t,
        ],
        [((rounds, slots, 2 * size), bf16)],
    )
    home = exchange(grads_send.reshape(devices * span, 2 * size))
    return call(
        home_kernel,
        [((token_count, size), bf16), ((token_count, size), bf16)],
        [home_pick, home],
    )


def on_device(qk, values, grad_out, members, counts):
    grad_qk, grad_v = head_backward(qk[0], values[0], grad_out[0], members[0], counts[0])
    return (grad_qk[None], grad_v[None])


def solution(mesh):
    in_specs = (
        P("head", "seq", None),
        P("head", "seq", None),
        P("head", "seq", None),
        P("head", None, None, None),
        P("head", None, None),
    )
    out_specs = (P("head", "seq", None), P("head", "seq", None))
    return jax.shard_map(
        on_device, mesh=mesh, in_specs=in_specs, out_specs=out_specs, check_vma=False
    )
```
